128 devices in a mesh: blk: 8 (over y, x_hi), grp: 16 (over x_lo, z, core).
Axes of the slice: x: 4 (x_hi: 2, x_lo: 2; x = x_hi * 2 + x_lo), y: 4, z: 4, core: 2. Of those that a mesh axis runs over, the one named last changes fastest.
Arguments:
- grad_out: bfloat16 [16, 32768, 256], P('grp', 'blk'), may hold values from -6 to 6
- pre_act: bfloat16 [16, 32768, 256], P('grp', 'blk'), may hold values from -6 to 6
- node_feats: bfloat16 [16, 32768, 256], P('grp', 'blk'), may hold values from -6 to 6
- w_message: bfloat16 [256, 256], replicated, may hold values from -0.375 to 0.375
- w_update: bfloat16 [256, 256], replicated, may hold values from -0.375 to 0.375
- tile_vals: bfloat16 [16, 8, 8, 16, 128, 128], P('grp', 'blk'), may hold values from -0.25 to 0.25
- tile_rows: int32 [16, 8, 8, 16], P('grp'), may hold values from 0 to 31
- tile_cols: int32 [16, 8, 8, 16], P('grp', 'blk'), may hold values from 0 to 31
- rec_slab: int32 [16, 32768, 1], P('grp', 'blk'), may hold values from 0 to 15; in each aligned block of 4096 rows (0 to 4095, 4096 to 8191, ..., all dimensions but the last counted through in order) at most 512 rows name the same one
- rec_local: int32 [16, 32768], P('grp', 'blk'), may hold values from 0 to 4095
- rec_remote: int32 [16, 32768], P('grp', 'blk'), may hold values from 0 to 4095
- rec_weight: float32 [16, 32768], P('grp', 'blk'), may hold values from 0.25 to 2
Outputs:
- grad_feats: bfloat16 [16, 32768, 256], P('grp', 'blk')
- grad_message: float32 [256, 256], replicated
- grad_update: float32 [256, 256], replicated
The draws below stay inside these ranges and needn't reach their ends.
Inputs may be any that keep to these rules, and one draw needn't show every extreme that they name: `rec_slab`: among the 4096 records of one device at most 512 name the same slab, and in every draw some device has a slab named by exactly 512 of its records.
All inputs are finite; a program needn't handle non-finite values.
Results may differ from the reference program's by a relative error of at most 0.009.
Values may be sent and summed in bfloat16 or wider, within the bound.
A program may use at most 128 MiB of HBM per device.

```python
import math
import jax
import jax.numpy as jnp
import numpy as np
from jax import lax

D = 256
TILE = 128
ROWS = 4096
TPP = 16
REC_DEV = 4096
CAP = 512
SLABS = 16
SLAB_NODES = 32768
RECORDS = 32768
N_BLK = 8
N_GRP = 16


def touch_ends(array, stream_key, smallest, largest):
    shape = array.shape
    place = [jax.random.randint(jax.random.fold_in(stream_key, axis), (), 0, shape[axis]) for axis in range(len(shape))]
    array = array.at[tuple(place)].set(smallest)
    longest = shape.index(max(shape))
    place[longest] = (place[longest] + 1) % shape[longest]
    return array.at[tuple(place)].set(largest)


def shard_levels(rng, dims, shards, low, top_value):
    def one(dim, shards_of):
        heights = jax.random.uniform(jax.random.fold_in(jax.random.fold_in(rng, 6), dim), (shards_of,), jnp.float32, low / len(shards), top_value / len(shards))
        return jnp.repeat(jnp.exp(heights), dims[dim] // shards_of).reshape((-1,) + (1,) * (len(dims) - dim - 1))

    gain = one(*shards[0])
    for cut in shards[1:]:
        gain = gain * one(*cut)
    return gain


def routed_block(stream_key, own, number, rows, number_of, top, most, skew):
    order = jax.random.permutation(stream_key, number_of)
    heavy_load, common = load_shares(number_of, rows * top, most, skew, True), load_shares(number_of, rows * top, most, skew, False)
    places = jnp.arange(number_of)

    def named(tallies, offset_by):
        used = int((tallies > 0).sum())
        fixed = max(1, used // 4)
        passed = fixed + (places - fixed + offset_by * (used - fixed)) % max(1, number_of - fixed)
        return jnp.zeros((number_of,), jnp.int32).at[order[jnp.where(places < fixed, places, passed)]].set(jnp.asarray(tallies, jnp.int32))

    tallies = jnp.where(number % 4 == 0, named(heavy_load, number // 4), named(common, number - number // 4 - 1))
    mixed = jax.random.permutation(jax.random.fold_in(own, 3), number_of)
    donor, taker = mixed[0:number_of // 2 * 2:2], mixed[1:number_of // 2 * 2:2]
    room = jnp.minimum(tallies[donor] - 1, most - tallies[taker]) // 2
    room = jnp.where((donor == order[0]) | (taker == order[0]) | (tallies[taker] == 0), 0, jnp.maximum(room, 0))
    passed = jax.random.randint(jax.random.fold_in(own, 4), (number_of // 2,), 0, 1 << 20) % (room + 1)
    tallies = tallies.at[donor].add(-passed).at[taker].add(passed)
    labels = jnp.searchsorted(jnp.cumsum(tallies), jnp.arange(rows * top), side="right").astype(jnp.int32)
    listing = labels.reshape(top, rows).T
    listing = listing[jax.random.permutation(jax.random.fold_in(own, 1), rows)]
    offset_by = jax.random.randint(jax.random.fold_in(own, 2), (rows, 1), 0, top)
    return jnp.take_along_axis(listing, (jnp.arange(top)[None, :] + offset_by) % top, axis=1)


def load_shares(number_of, total, most, skew, full):
    loads = [(1 << 20) // math.isqrt(standing ** skew) + 1 for standing in range(1, number_of + 1)]
    largest = most if full else min(most, max(-(-total // number_of), total * loads[0] // sum(loads)))
    least = 1 if total - largest >= number_of - 1 else 0
    given, rest = [largest] + [least] * (number_of - 1), total - largest - least * (number_of - 1)
    while rest > 0:
        free = [i for i in range(1, number_of) if given[i] < largest] or [i for i in range(1, number_of) if given[i] < most]
        pool, remaining = sum([loads[i] for i in free]), rest
        for i in free:
            more = min(most - given[i], max(1, remaining * loads[i] // pool), rest)
            given[i] = given[i] + more
            rest = rest - more
    return np.array(given)


def bell_draw(stream_key, extent, scale, bound, shards=(), kind=jnp.bfloat16):
    level = shard_levels(stream_key, extent, shards, -0.22, 0.18) if shards else 1.0
    values = jax.random.normal(stream_key, extent, jnp.float32) * scale * level
    return jnp.minimum(jnp.maximum(values, -bound), bound).astype(kind)


def setup_inputs(seed: int = 0) -> dict:
    key_list = jax.random.split(jax.random.key(seed), 13)
    grad_out = bell_draw(key_list[0], (SLABS, SLAB_NODES, D), 1.0, 6.0, ((0, 16), (1, 8)))
    pre_act = bell_draw(key_list[1], (SLABS, SLAB_NODES, D), 1.5, 6.0, ((0, 16), (1, 8)))
    node_feats = bell_draw(key_list[2], (SLABS, SLAB_NODES, D), 1.0, 6.0, ((0, 16), (1, 8)))
    w_message = bell_draw(key_list[3], (D, D), D ** -0.5, 0.375)
    w_update = bell_draw(key_list[4], (D, D), D ** -0.5, 0.375)
    tile_vals = bell_draw(key_list[5], (SLABS, N_BLK, N_BLK, TPP, TILE, TILE), (N_BLK * TPP * TILE * TILE // ROWS) ** -0.5, 0.25, ((0, 16), (1, 8)))
    tile_rows = touch_ends(jax.random.randint(key_list[6], (SLABS, N_BLK, N_BLK, TPP), 0, ROWS // TILE), jax.random.fold_in(key_list[6], 1), 0, (ROWS // TILE) - 1).astype(jnp.int32)
    tile_cols = touch_ends(jax.random.randint(key_list[7], (SLABS, N_BLK, N_BLK, TPP), 0, ROWS // TILE), jax.random.fold_in(key_list[7], 1), 0, (ROWS // TILE) - 1).astype(jnp.int32)
    rec_slab_keys = jax.random.split(jax.random.fold_in(key_list[8], 1), SLABS * RECORDS // REC_DEV)
    rec_slab_turns = jax.random.permutation(jax.random.fold_in(key_list[8], 3), SLABS * RECORDS // REC_DEV)
    rec_slab = jax.vmap(lambda own, number: routed_block(jax.random.fold_in(key_list[8], 2), own, number, REC_DEV, N_GRP, 1, CAP, 2))(rec_slab_keys, rec_slab_turns).reshape((SLABS, RECORDS, 1))
    rec_local = touch_ends(jax.random.randint(key_list[9], (SLABS, RECORDS), 0, ROWS), jax.random.fold_in(key_list[9], 1), 0, ROWS - 1).astype(jnp.int32)
    rec_remote = touch_ends(jax.random.randint(key_list[10], (SLABS, RECORDS), 0, ROWS), jax.random.fold_in(key_list[10], 1), 0, ROWS - 1).astype(jnp.int32)
    rec_weight = jnp.clip(jnp.exp(math.log(2.0) - 2.0794415 * jax.random.uniform(key_list[11], (SLABS, RECORDS), jnp.float32) ** shard_levels(key_list[11], (SLABS, RECORDS), ((0, 16), (1, 8)), -0.2, 0.2)), 0.25, 2.0)
    return {"grad_out": grad_out, "pre_act": pre_act, "node_feats": node_feats, "w_message": w_message, "w_update": w_update, "tile_vals": tile_vals, "tile_rows": tile_rows, "tile_cols": tile_cols, "rec_slab": rec_slab, "rec_local": rec_local, "rec_remote": rec_remote, "rec_weight": rec_weight}


def silu_slope(value):
    sig = jax.nn.sigmoid(value)
    return sig * (1.0 + value * (1.0 - sig))

def reference(grad_out, pre_act, node_feats, w_message, w_update, tile_vals, tile_rows, tile_cols, rec_slab, rec_local, rec_remote, rec_weight):
    part_of = (jnp.arange(RECORDS) // REC_DEV).astype(jnp.int32)
    dest_slab = rec_slab[:, :, 0].astype(jnp.int32)
    dest_row = (part_of[None, :] * ROWS + rec_remote).astype(jnp.int32)
    src_row = (part_of[None, :] * ROWS + rec_local).astype(jnp.int32)

    def add_slab(index, accum):
        picked = grad_out[index][src_row[index]].astype(jnp.float32)
        term = (rec_weight[index][:, None] * picked).astype(jnp.bfloat16).astype(jnp.float32)
        return accum.at[dest_slab[index], dest_row[index]].add(term)
    grad_h = lax.fori_loop(0, SLABS, add_slab, grad_out.astype(jnp.float32)).astype(jnp.bfloat16)

    def one_slab(items):
        slab_h, slab_pre, slab_x, slab_tiles, slab_rows, slab_cols = items
        pre = slab_pre.astype(jnp.float32)
        act = jax.nn.silu(pre).astype(jnp.bfloat16)
        back = jnp.dot(slab_h, w_update.T, preferred_element_type=jnp.float32)
        grad_pre = (back * silu_slope(pre)).astype(jnp.bfloat16)
        panels = grad_pre.reshape(N_BLK, ROWS // TILE, TILE, D)

        def one_column(col_items):
            tiles, rows_here, cols_here = col_items
            chosen = panels[jnp.arange(N_BLK)[:, None], rows_here]
            contrib = jnp.einsum('rtij,rtid->rtjd', tiles.astype(jnp.float32), chosen.astype(jnp.float32))
            empty = jnp.zeros((ROWS // TILE, TILE, D), jnp.float32)
            return empty.at[cols_here.reshape(-1)].add(contrib.reshape(-1, TILE, D))
        spread = lax.map(one_column, (slab_tiles, slab_rows, slab_cols))
        spread = spread.reshape(SLAB_NODES, D).astype(jnp.bfloat16)
        feats = (slab_h.astype(jnp.float32) + jnp.dot(spread, w_message.T, preferred_element_type=jnp.float32)).astype(jnp.bfloat16)
        msg_term = jnp.dot(slab_x.T, spread, preferred_element_type=jnp.float32)
        upd_term = jnp.dot(act.T, slab_h, preferred_element_type=jnp.float32)
        return (feats, msg_term, upd_term)
    grad_feats, msg_terms, upd_terms = lax.map(one_slab, (grad_h, pre_act, node_feats, tile_vals, tile_rows, tile_cols))
    scale = 1.0 / jnp.sqrt(jnp.float32(SLABS * SLAB_NODES))
    return (grad_feats, lax.optimization_barrier(jnp.sum(msg_terms, axis=0)) * scale, lax.optimization_barrier(jnp.sum(upd_terms, axis=0)) * scale)
```

```python
import functools

import jax
import jax.numpy as jnp
from jax import lax
from jax.experimental import pallas as pl
from jax.experimental.pallas import tpu as pltpu
from jax.sharding import PartitionSpec as P

F32 = jnp.float32
BF16 = jnp.bfloat16
MESH = pl.DeviceIdType.MESH
NT = (((1,), (1,)), ((), ()))
TN = (((0,), (0,)), ((), ()))
EXT = 16
VMEM_LIMIT = 56 * 1024 * 1024


def iota(shape, dim):
    return lax.broadcasted_iota(jnp.int32, shape, dim)


def prep_kernel(slab_ref, local_ref, remote_ref, weight_ref, grad_ref, out_ref, node_ref, scale_ref, ext_ref):
    slabs, cap = node_ref.shape[0], node_ref.shape[1]
    chunks = slab_ref.shape[0]
    nodes = grad_ref.shape[0]

    @pl.when(pl.program_id(0) == 0)
    def _():
        slab = slab_ref[...]
        ids = iota((chunks, slabs, 128), 1)
        choose = jnp.where(ids == slab[:, None, :], 1.0, 0.0)
        flat = choose.reshape(chunks * slabs, 128)
        flat16 = flat.astype(BF16)
        upper = jnp.where(iota((128, 128), 0) < iota((128, 128), 1), 1.0, 0.0).astype(BF16)
        prefix = jnp.dot(flat16, upper, preferred_element_type=F32)
        totals = jnp.dot(flat16, jnp.ones((128, 128), BF16), preferred_element_type=F32)
        size = chunks * slabs
        row, col = iota((size, size), 0), iota((size, size), 1)
        earlier = (col < row) & (lax.rem(col, slabs) == lax.rem(row, slabs))
        offset = jnp.dot(jnp.where(earlier, 1.0, 0.0).astype(BF16), totals.astype(BF16), preferred_element_type=F32)
        place = ((prefix + offset) * flat).reshape(chunks, slabs, 128).sum(axis=1).astype(jnp.int32)
        remote, local, weight = remote_ref[...], local_ref[...], weight_ref[...]
        first = weight.astype(BF16).astype(F32)
        second = (weight - first).astype(BF16).astype(F32)
        third = weight - first - second
        values = [
            (remote // 64).astype(F32),
            (remote % 64).astype(F32),
            (local // 64).astype(F32),
            (local % 64).astype(F32),
            first,
            second,
            third,
            jnp.ones_like(weight),
        ]
        table = jnp.zeros((len(values) * slabs, cap), F32)
        for c in range(chunks):
            left = jnp.concatenate([choose[c] * v[c : c + 1] for v in values], axis=0).astype(BF16)
            right = jnp.where(iota((cap, 128), 0) == place[c : c + 1], 1.0, 0.0).astype(BF16)
            table += lax.dot_general(left, right, NT, preferred_element_type=F32)
        valid = table[7 * slabs : 8 * slabs]
        upper_part = jnp.where(valid > 0.5, table[:slabs], 64.0)
        lower_part = table[slabs : 2 * slabs]
        half = cap // 2
        for s in range(slabs):
            rows = [part[s : s + 1, q * half : (q + 1) * half] for part in (upper_part, lower_part) for q in range(2)]
            block = jnp.concatenate(rows + [jnp.zeros((EXT - 4, half), F32)], axis=0)
            ext_ref[s] = block.astype(BF16)
        turned = jnp.transpose(table)
        for s in range(slabs):
            at = lambda v: turned[:, v * slabs + s : v * slabs + s + 1]
            node_ref[s] = jnp.broadcast_to((at(2) * 64.0 + at(3)).astype(jnp.int32), (cap, 128))
            scale_ref[s] = jnp.broadcast_to(at(4) + at(5) + at(6), (cap, 128))

    s = pl.program_id(0)
    wide = 1024
    node = node_ref[s]
    lane = iota((cap, 128), 1)
    total = jnp.zeros((cap, grad_ref.shape[1]), F32)
    for k in range(nodes // wide):
        pieces = [
            jnp.where(node == lane + (k * wide + j * 128), 1.0, 0.0).astype(BF16) for j in range(wide // 128)
        ]
        total += jnp.dot(
            jnp.concatenate(pieces, axis=1), grad_ref[k * wide : (k + 1) * wide], preferred_element_type=F32
        )
    scale = scale_ref[s]
    out_ref[0, :cap] = (total * jnp.concatenate([scale, scale], axis=1)).astype(BF16)
    out_ref[0, cap:] = ext_ref[s]


def prep(slab, local, remote, weight, grad, slabs, cap):
    nodes, width = grad.shape
    whole = lambda a: pl.BlockSpec(a.shape, lambda i: (0,) * a.ndim)
    args = (slab, local, remote, weight, grad)
    return pl.pallas_call(
        prep_kernel,
        grid=(slabs,),
        out_shape=jax.ShapeDtypeStruct((slabs, cap + EXT, width), BF16),
        in_specs=[whole(a) for a in args],
        out_specs=pl.BlockSpec((1, cap + EXT, width), lambda i: (i, 0, 0)),
        scratch_shapes=[
            pltpu.VMEM((slabs, cap, 128), jnp.int32),
            pltpu.VMEM((slabs, cap, 128), F32),
            pltpu.VMEM((slabs, EXT, width), BF16),
        ],
        compiler_params=pltpu.CompilerParams(vmem_limit_bytes=VMEM_LIMIT),
        name="prep",
    )(*args)


def node_kernel(
    picks_ref, arrived_ref, grad_ref, pre_ref, w_ref, gradh_ref, upd_ref, packed_ref, target_ref, gp_ref, sem
):
    slabs, cap = arrived_ref.shape[0], arrived_ref.shape[1] - EXT
    parts, picks = packed_ref.shape[0], packed_ref.shape[1]
    half = cap // 2
    tall = grad_ref.shape[0]
    i = pl.program_id(0)

    @pl.when(i == 0)
    def _():
        upd_ref[...] = jnp.zeros_like(upd_ref)
        for s in range(slabs):
            ext = arrived_ref[s, cap:].astype(F32)
            target_ref[s : s + 1, :half] = (ext[0:1] * 64.0 + ext[2:3]).astype(jnp.int32)
            target_ref[s : s + 1, half:] = (ext[1:2] * 64.0 + ext[3:4]).astype(jnp.int32)

    row = iota((tall, cap), 0) + i * tall
    total = grad_ref[...].astype(F32)
    for s in range(slabs):
        hot = jnp.where(row == target_ref[s : s + 1], 1.0, 0.0).astype(BF16)
        total += jnp.dot(hot, arrived_ref[s, :cap], preferred_element_type=F32)
    gradh = total.astype(BF16)
    gradh_ref[...] = gradh
    pre = pre_ref[...].astype(F32)
    sig = 1.0 / (1.0 + jnp.exp(-pre))
    act = (pre * sig).astype(BF16)
    slope = sig * (1.0 + pre * (1.0 - sig))
    upd_ref[...] += lax.dot_general(act, gradh, TN, preferred_element_type=F32)
    back = lax.dot_general(gradh, w_ref[...], NT, preferred_element_type=F32)
    gp_ref[pl.ds(pl.multiple_of(i * tall, tall), tall)] = (back * slope).astype(BF16)

    @pl.when(i == pl.num_programs(0) - 1)
    def _():
        def copy(n):
            c, t = n // picks, n % picks
            at = pl.multiple_of(picks_ref[c, t] * 128, 128)
            return pltpu.make_async_copy(gp_ref.at[pl.ds(at, 128)], packed_ref.at[c, t], sem)

        lax.fori_loop(0, parts * picks, lambda n, x: (copy(n).start(), x)[1], 0)
        lax.fori_loop(0, parts * picks, lambda n, x: (copy(n).wait(), x)[1], 0)


def node_step(picks, arrived, grad, pre, w_update):
    rows, width = grad.shape
    parts, count = picks.shape
    tall = 256
    tile = pl.BlockSpec((tall, width), lambda i, *_: (i, 0))
    return pl.pallas_call(
        node_kernel,
        grid_spec=pltpu.PrefetchScalarGridSpec(
            num_scalar_prefetch=1,
            grid=(rows // tall,),
            in_specs=[
                pl.BlockSpec(arrived.shape, lambda i, *_: (0, 0, 0)),
                tile,
                tile,
                pl.BlockSpec(w_update.shape, lambda i, *_: (0, 0)),
            ],
            out_specs=[tile, pl.BlockSpec((width, width), lambda i, *_: (0, 0)), pl.BlockSpec(memory_space=pl.ANY)],
            scratch_shapes=[
                pltpu.VMEM((arrived.shape[0], arrived.shape[1] - EXT), jnp.int32),
                pltpu.VMEM((rows, width), BF16),
                pltpu.SemaphoreType.DMA,
            ],
        ),
        out_shape=[
            jax.ShapeDtypeStruct((rows, width), BF16),
            jax.ShapeDtypeStruct((width, width), F32),
            jax.ShapeDtypeStruct((parts, count, 128, width), BF16),
        ],
        compiler_params=pltpu.CompilerParams(vmem_limit_bytes=VMEM_LIMIT),
        name="node_step",
    )(picks, arrived, grad, pre, w_update)


def tile_kernel(cols_ref, got_ref, tiles_ref, gradh_ref, feats_ref, w_ref, out_ref, msg_ref, total_ref):
    r = pl.program_id(0)
    picks = got_ref.shape[1]

    @pl.when(r == 0)
    def _():
        total_ref[...] = jnp.zeros_like(total_ref)

    for t in range(picks):
        part = lax.dot_general(tiles_ref[0, t], got_ref[0, t], TN, preferred_element_type=F32)
        at = pl.ds(pl.multiple_of(cols_ref[r, t] * 128, 128), 128)
        total_ref[at] += part

    @pl.when(r == pl.num_programs(0) - 1)
    def _():
        msg = jnp.zeros(msg_ref.shape, F32)
        tall = 512
        for k in range(total_ref.shape[0] // tall):
            at = slice(k * tall, (k + 1) * tall)
            spread = total_ref[at].astype(BF16)
            msg += lax.dot_general(feats_ref[at], spread, TN, preferred_element_type=F32)
            down = lax.dot_general(spread, w_ref[...], NT, preferred_element_type=F32)
            out_ref[at] = (gradh_ref[at].astype(F32) + down).astype(BF16)
        msg_ref[...] = msg


def tile_step(cols, got, tiles, gradh, feats, w_message):
    parts, picks = cols.shape
    rows, width = gradh.shape
    whole = lambda a: pl.BlockSpec(a.shape, lambda i, *_: (0,) * a.ndim)
    return pl.pallas_call(
        tile_kernel,
        grid_spec=pltpu.PrefetchScalarGridSpec(
            num_scalar_prefetch=1,
            grid=(parts,),
            in_specs=[
                pl.BlockSpec((1, picks, 128, width), lambda i, *_: (i, 0, 0, 0)),
                pl.BlockSpec((1, picks, 128, 128), lambda i, *_: (i, 0, 0, 0)),
                whole(gradh),
                whole(feats),
                whole(w_message),
            ],
            out_specs=[whole(gradh), pl.BlockSpec((width, width), lambda i, *_: (0, 0))],
            scratch_shapes=[pltpu.VMEM((rows, width), F32)],
        ),
        out_shape=[jax.ShapeDtypeStruct((rows, width), BF16), jax.ShapeDtypeStruct((width, width), F32)],
        compiler_params=pltpu.CompilerParams(vmem_limit_bytes=VMEM_LIMIT),
        name="tile_step",
    )(cols, got, tiles, gradh, feats, w_message)


def reduce_kernel(
    parts, slabs, factor, msg_ref, upd_ref, out_msg_ref, out_upd_ref,
    mine_ref, in1, mid, in2, part_ref, all2, done, all1, s1, r1, s2, r2, s3, r3, s4, r4,
):
    b, g = lax.axis_index("blk"), lax.axis_index("grp")
    width = msg_ref.shape[0]
    rows = 2 * width // parts
    barrier = pltpu.get_barrier_semaphore()
    for k in range(1, parts):
        pl.semaphore_signal(barrier, inc=1, device_id={"blk": lax.rem(b + k, parts)}, device_id_type=MESH)
    for k in range(1, slabs):
        pl.semaphore_signal(barrier, inc=1, device_id={"grp": lax.rem(g + k, slabs)}, device_id_type=MESH)
    for k in range(parts // 2):
        mine_ref[k] = msg_ref[k * rows : (k + 1) * rows]
        mine_ref[parts // 2 + k] = upd_ref[k * rows : (k + 1) * rows]
    pl.semaphore_wait(barrier, parts + slabs - 2)

    def exchange(n, axis, me, src, dst, send, recv):
        copies = []
        for k in range(1, n):
            peer = lax.rem(me + k, n)
            copy = pltpu.make_async_remote_copy(
                src(peer), dst(k), send.at[k - 1], recv.at[k - 1], device_id={axis: peer}, device_id_type=MESH
            )
            copy.start()
            copies.append(copy)
        for copy in copies:
            copy.wait_recv()
        return copies

    sent = exchange(parts, "blk", b, lambda p: mine_ref.at[p], lambda k: in1.at[k - 1], s1, r1)
    total = mine_ref[b]
    for k in range(parts - 1):
        total += in1[k]
    for n in range(slabs):
        mid[n] = total[n // 2 * 8 : n // 2 * 8 + 8, n % 2 * 128 : n % 2 * 128 + 128]
    sent += exchange(slabs, "grp", g, lambda p: mid.at[p], lambda k: in2.at[k - 1], s2, r2)
    piece = mid[g]
    for k in range(slabs - 1):
        piece += in2[k]
    part_ref[...] = piece * factor
    all2[g] = piece * factor
    sent += exchange(slabs, "grp", g, lambda p: part_ref, lambda k: all2.at[g], s3, r3)
    for n in range(slabs):
        done[n // 2 * 8 : n // 2 * 8 + 8, n % 2 * 128 : n % 2 * 128 + 128] = all2[n]
    all1[b] = done[...]
    sent += exchange(parts, "blk", b, lambda p: done, lambda k: all1.at[b], s4, r4)
    for k in range(parts // 2):
        out_msg_ref[k * rows : (k + 1) * rows] = all1[k]
        out_upd_ref[k * rows : (k + 1) * rows] = all1[parts // 2 + k]
    for copy in sent:
        copy.wait_send()


def reduce_step(msg, upd, parts, slabs, factor):
    width = msg.shape[0]
    rows = 2 * width // parts
    vmem = pl.BlockSpec(memory_space=pltpu.VMEM)
    dma = pltpu.SemaphoreType.DMA
    return pl.pallas_call(
        functools.partial(reduce_kernel, parts, slabs, factor),
        out_shape=[jax.ShapeDtypeStruct(msg.shape, F32)] * 2,
        in_specs=[vmem] * 2,
        out_specs=[vmem] * 2,
        scratch_shapes=[
            pltpu.VMEM((parts, rows, width), F32),
            pltpu.VMEM((parts - 1, rows, width), F32),
            pltpu.VMEM((slabs, 8, 128), F32),
            pltpu.VMEM((slabs - 1, 8, 128), F32),
            pltpu.VMEM((8, 128), F32),
            pltpu.VMEM((slabs, 8, 128), F32),
            pltpu.VMEM((rows, width), F32),
            pltpu.VMEM((parts, rows, width), F32),
            dma((parts - 1,)), dma((parts - 1,)),
            dma((slabs - 1,)), dma((slabs - 1,)),
            dma((slabs - 1,)), dma((slabs - 1,)),
            dma((parts - 1,)), dma((parts - 1,)),
        ],
        compiler_params=pltpu.CompilerParams(collective_id=0, has_side_effects=True, vmem_limit_bytes=VMEM_LIMIT),
        name="reduce_step",
    )(msg, upd)


def local(
    grad_out, pre_act, node_feats, w_message, w_update, tile_vals, tile_rows, tile_cols,
    rec_slab, rec_local, rec_remote, rec_weight,
):
    grad = grad_out[0]
    rows, width = grad.shape
    slabs = lax.axis_size("grp")
    parts = lax.axis_size("blk")
    mine = lax.axis_index("blk")
    records = rec_local.shape[1]
    cap = 2 * records // slabs
    lanes = lambda a: a.reshape(records // 128, 128)
    outgoing = prep(
        lanes(rec_slab), lanes(rec_local), lanes(rec_remote), lanes(rec_weight), grad, slabs, cap
    )
    arrived = lax.all_to_all(outgoing, "grp", split_axis=0, concat_axis=0, tiled=True)
    picks = lax.dynamic_index_in_dim(tile_rows[0], mine, 1, False)
    gradh, upd, packed = node_step(picks, arrived, grad, pre_act[0], w_update)
    got = lax.all_to_all(packed, "blk", split_axis=0, concat_axis=0, tiled=True)
    feats, msg = tile_step(tile_cols[0, 0], got, tile_vals[0, 0], gradh, node_feats[0], w_message)
    factor = float((slabs * parts * rows) ** -0.5)
    msg, upd = reduce_step(msg, upd, parts, slabs, factor)
    return (feats[None], msg, upd)


def solution(mesh):
    placed = (
        P("grp", "blk", None),
        P("grp", "blk", None),
        P("grp", "blk", None),
        P(),
        P(),
        P("grp", "blk", None, None, None, None),
        P("grp", None, None, None),
        P("grp", "blk", None, None),
        P("grp", "blk", None),
        P("grp", "blk"),
        P("grp", "blk"),
        P("grp", "blk"),
    )
    return jax.shard_map(
        local,
        mesh=mesh,
        in_specs=placed,
        out_specs=(P("grp", "blk", None), P(), P()),
        check_vma=False,
    )
```

```python
import functools

import jax
import jax.numpy as jnp
from jax import lax
from jax.experimental import pallas as pl
from jax.experimental.pallas import tpu as pltpu
from jax.sharding import PartitionSpec as P

F32 = jnp.float32
BF16 = jnp.bfloat16
MESH = pl.DeviceIdType.MESH
NT = (((1,), (1,)), ((), ()))
TN = (((0,), (0,)), ((), ()))
EXT = 16
VMEM_LIMIT = 56 * 1024 * 1024


def iota(shape, dim):
    return lax.broadcasted_iota(jnp.int32, shape, dim)


def index_tables(slab_ref, local_ref, remote_ref, weight_ref, node_ref, scale_ref, ext_ref):
    slabs, cap = node_ref.shape[0], node_ref.shape[1]
    chunks = slab_ref.shape[0]
    slab = slab_ref[...]
    ids = iota((chunks, slabs, 128), 1)
    choose = jnp.where(ids == slab[:, None, :], 1.0, 0.0)
    flat = choose.reshape(chunks * slabs, 128)
    flat16 = flat.astype(BF16)
    upper = jnp.where(iota((128, 128), 0) < iota((128, 128), 1), 1.0, 0.0).astype(BF16)
    prefix = jnp.dot(flat16, upper, preferred_element_type=F32)
    totals = jnp.dot(flat16, jnp.ones((128, 128), BF16), preferred_element_type=F32)
    size = chunks * slabs
    row, col = iota((size, size), 0), iota((size, size), 1)
    earlier = (col < row) & (lax.rem(col, slabs) == lax.rem(row, slabs))
    offset = jnp.dot(jnp.where(earlier, 1.0, 0.0).astype(BF16), totals.astype(BF16), preferred_element_type=F32)
    place = ((prefix + offset) * flat).reshape(chunks, slabs, 128).sum(axis=1).astype(jnp.int32)
    remote, local, weight = remote_ref[...], local_ref[...], weight_ref[...]
    first = weight.astype(BF16).astype(F32)
    second = (weight - first).astype(BF16).astype(F32)
    third = weight - first - second
    values = [
        (remote // 64).astype(F32),
        (remote % 64).astype(F32),
        (local // 64).astype(F32),
        (local % 64).astype(F32),
        first,
        second,
        third,
        jnp.ones_like(weight),
    ]
    table = jnp.zeros((len(values) * slabs, cap), F32)
    for c in range(chunks):
        left = jnp.concatenate([choose[c] * v[c : c + 1] for v in values], axis=0).astype(BF16)
        right = jnp.where(iota((cap, 128), 0) == place[c : c + 1], 1.0, 0.0).astype(BF16)
        table += lax.dot_general(left, right, NT, preferred_element_type=F32)
    valid = table[7 * slabs : 8 * slabs]
    upper_part = jnp.where(valid > 0.5, table[:slabs], 64.0)
    lower_part = table[slabs : 2 * slabs]
    half = cap // 2
    for s in range(slabs):
        rows = [part[s : s + 1, q * half : (q + 1) * half] for part in (upper_part, lower_part) for q in range(2)]
        block = jnp.concatenate(rows + [jnp.zeros((EXT - 4, half), F32)], axis=0)
        ext_ref[s] = block.astype(BF16)
    turned = jnp.transpose(table)
    for s in range(slabs):
        at = lambda v: turned[:, v * slabs + s : v * slabs + s + 1]
        node_ref[s] = jnp.broadcast_to((at(2) * 64.0 + at(3)).astype(jnp.int32), (cap, 128))
        scale_ref[s] = jnp.broadcast_to(at(4) + at(5) + at(6), (cap, 128))


FAR = ((2, 1), (1, 1), (3, 1), (0, 1), (2, 0), (1, 0), (3, 0))


def main_kernel(
    parts, slabs,
    picks_ref, slab_ref, local_ref, remote_ref, weight_ref, w_ref, grad_hbm, pre_hbm,
    gradh_hbm, upd_ref, got_hbm,
    node_ref, scale_ref, ext_ref, out_buf, in_buf, grad_ref, pre_ref, gradh_ref, acc_ref, gp_ref, stage_ref,
    load_sem, rec_send, rec_recv, blk_send, blk_recv, store_sem,
):
    b, g = lax.axis_index("blk"), lax.axis_index("grp")
    y, xh = b // 2, b % 2
    xl, z, core = g // 8, (g // 2) % 4, g % 2
    cap = node_ref.shape[1]
    half = cap // 2
    nodes, width = acc_ref.shape
    picks = stage_ref.shape[1]

    load_grad = pltpu.make_async_copy(grad_hbm, grad_ref, load_sem.at[0])
    load_pre = pltpu.make_async_copy(pre_hbm, pre_ref, load_sem.at[1])
    load_grad.start()
    load_pre.start()

    def rec_peer(n):
        q = n // 4
        dz, dx, dc = (n % 4 + 1) % 4, 1 - n // 8, (q + q // 2) % 2
        return ((xl + dx) % 2 * 4 + (z + dz) % 4) * 2 + (core + dc) % 2

    def blk_peer(n):
        dy, dx = FAR[n]
        return (y + dy) % 4 * 2 + (xh + dx) % 2

    barrier = pltpu.get_barrier_semaphore()
    for n in range(slabs - 1):
        pl.semaphore_signal(barrier, inc=1, device_id={"grp": rec_peer(n)}, device_id_type=MESH)
    for n in range(parts - 1):
        pl.semaphore_signal(barrier, inc=1, device_id={"blk": blk_peer(n)}, device_id_type=MESH)

    index_tables(slab_ref, local_ref, remote_ref, weight_ref, node_ref, scale_ref, ext_ref)
    load_grad.wait()
    pl.semaphore_wait(barrier, slabs + parts - 2)

    def rec_copy(n):
        return pltpu.make_async_remote_copy(
            out_buf.at[n], in_buf.at[n], rec_send.at[n], rec_recv.at[n],
            device_id={"grp": rec_peer(n)}, device_id_type=MESH,
        )

    own = slabs - 1
    own_copy = pltpu.make_async_copy(out_buf.at[own], in_buf.at[own], rec_recv.at[own])
    wide = 1024

    def gather(n, _):
        s = rec_peer(n)
        node = node_ref[s]
        total = jnp.zeros((cap, width), F32)
        for k in range(nodes // wide):
            pieces = [
                jnp.where(node == iota((1, 128), 1) + (k * wide + j * 128), 1.0, 0.0).astype(BF16)
                for j in range(wide // 128)
            ]
            total += jnp.dot(
                jnp.concatenate(pieces, axis=1), grad_ref[k * wide : (k + 1) * wide], preferred_element_type=F32
            )
        scale = scale_ref[s]
        out_buf[n, :cap] = (total * jnp.concatenate([scale, scale], axis=1)).astype(BF16)
        out_buf[n, cap:] = ext_ref[s]

        @pl.when(n < own)
        def _():
            rec_copy(n).start()

        return 0

    lax.fori_loop(0, slabs, gather, 0)
    own_copy.start()
    acc_ref[...] = grad_ref[...].astype(F32)
    own_copy.wait()

    tall = 512

    def scatter(m, _):
        n = (m + own) % slabs

        @pl.when(m > 0)
        def _():
            rec_copy(n).wait_recv()

        ext = in_buf[n, cap:].astype(F32)
        targets = [(ext[q : q + 1] * 64.0 + ext[2 + q : 3 + q]).astype(jnp.int32) for q in range(2)]
        block = in_buf[n, :cap]

        def rows(i, _):
            at = pl.ds(pl.multiple_of(i * tall, tall), tall)
            row = iota((tall, 128), 0)
            pieces = [
                jnp.where(row == targets[j // 2][:, j % 2 * 128 : j % 2 * 128 + 128] - i * tall, 1.0, 0.0).astype(BF16)
                for j in range(cap // 128)
            ]
            acc_ref[at] += jnp.dot(jnp.concatenate(pieces, axis=1), block, preferred_element_type=F32)
            return 0

        lax.fori_loop(0, nodes // tall, rows, 0)
        return 0

    lax.fori_loop(0, slabs, scatter, 0)

    load_pre.wait()
    upd_ref[...] = jnp.zeros_like(upd_ref)

    def finish(i, _):
        at = pl.ds(pl.multiple_of(i * 256, 256), 256)
        gradh = acc_ref[at].astype(BF16)
        gradh_ref[at] = gradh
        pre = pre_ref[at].astype(F32)
        sig = 1.0 / (1.0 + jnp.exp(-pre))
        act = (pre * sig).astype(BF16)
        slope = sig * (1.0 + pre * (1.0 - sig))
        back = lax.dot_general(gradh, w_ref[...], NT, preferred_element_type=F32)
        gp_ref[pl.ds(i * 2, 2)] = (back * slope).astype(BF16).reshape(2, 128, width)
        upd_ref[...] += lax.dot_general(act, gradh, TN, preferred_element_type=F32)
        return 0

    lax.fori_loop(0, nodes // 256, finish, 0)
    store_gradh = pltpu.make_async_copy(gradh_ref, gradh_hbm, store_sem.at[0])
    store_gradh.start()

    def pack(n, c):
        def one(t, _):
            stage_ref[n, t] = gp_ref[picks_ref[c, b, t]]
            return 0

        lax.fori_loop(0, picks, one, 0)

    sends = []
    for n in range(parts - 1):
        pack(n, blk_peer(n))
        copy = pltpu.make_async_remote_copy(
            stage_ref.at[n], got_hbm.at[b], blk_send.at[n], blk_recv.at[n],
            device_id={"blk": blk_peer(n)}, device_id_type=MESH,
        )
        copy.start()
        sends.append(copy)
    pack(parts - 1, b)
    keep = pltpu.make_async_copy(stage_ref.at[parts - 1], got_hbm.at[b], store_sem.at[1])
    keep.start()
    lax.fori_loop(0, slabs - 1, lambda n, x: (rec_copy(n).wait_send(), x)[1], 0)
    for copy in sends:
        copy.wait()
    keep.wait()
    store_gradh.wait()


def main_step(picks, slab, local, remote, weight, w_update, grad, pre, slabs, parts, cap):
    nodes, width = grad.shape
    count = picks.shape[-1]
    vmem = pl.BlockSpec(memory_space=pltpu.VMEM)
    hbm = pl.BlockSpec(memory_space=pl.ANY)
    dma = pltpu.SemaphoreType.DMA
    return pl.pallas_call(
        functools.partial(main_kernel, parts, slabs),
        out_shape=[
            jax.ShapeDtypeStruct((nodes, width), BF16),
            jax.ShapeDtypeStruct((width, width), F32),
            jax.ShapeDtypeStruct((parts, count, 128, width), BF16),
        ],
        in_specs=[pl.BlockSpec(memory_space=pltpu.SMEM)] + [vmem] * 5 + [hbm] * 2,
        out_specs=[hbm, vmem, hbm],
        scratch_shapes=[
            pltpu.VMEM((slabs, cap, 128), jnp.int32),
            pltpu.VMEM((slabs, cap, 128), F32),
            pltpu.VMEM((slabs, EXT, width), BF16),
            pltpu.VMEM((slabs, cap + EXT, width), BF16),
            pltpu.VMEM((slabs, cap + EXT, width), BF16),
            pltpu.VMEM((nodes, width), BF16),
            pltpu.VMEM((nodes, width), BF16),
            pltpu.VMEM((nodes, width), BF16),
            pltpu.VMEM((nodes, width), F32),
            pltpu.VMEM((nodes // 128, 128, width), BF16),
            pltpu.VMEM((parts, count, 128, width), BF16),
            dma((2,)), dma((slabs - 1,)), dma((slabs,)), dma((parts - 1,)), dma((parts - 1,)), dma((2,)),
        ],
        compiler_params=pltpu.CompilerParams(collective_id=1, has_side_effects=True, vmem_limit_bytes=VMEM_LIMIT),
        name="main_step",
    )(picks, slab, local, remote, weight, w_update, grad, pre)


def tile_kernel(cols_ref, got_ref, tiles_ref, gradh_ref, feats_ref, w_ref, out_ref, msg_ref, total_ref):
    r = pl.program_id(0)
    picks = got_ref.shape[1]

    @pl.when(r == 0)
    def _():
        total_ref[...] = jnp.zeros_like(total_ref)

    for t in range(picks):
        part = lax.dot_general(tiles_ref[0, t], got_ref[0, t], TN, preferred_element_type=F32)
        at = pl.ds(pl.multiple_of(cols_ref[r, t] * 128, 128), 128)
        total_ref[at] += part

    @pl.when(r == pl.num_programs(0) - 1)
    def _():
        msg = jnp.zeros(msg_ref.shape, F32)
        tall = 512
        for k in range(total_ref.shape[0] // tall):
            at = slice(k * tall, (k + 1) * tall)
            spread = total_ref[at].astype(BF16)
            msg += lax.dot_general(feats_ref[at], spread, TN, preferred_element_type=F32)
            down = lax.dot_general(spread, w_ref[...], NT, preferred_element_type=F32)
            out_ref[at] = (gradh_ref[at].astype(F32) + down).astype(BF16)
        msg_ref[...] = msg


def tile_step(cols, got, tiles, gradh, feats, w_message):
    parts, picks = cols.shape
    rows, width = gradh.shape
    whole = lambda a: pl.BlockSpec(a.shape, lambda i, *_: (0,) * a.ndim)
    return pl.pallas_call(
        tile_kernel,
        grid_spec=pltpu.PrefetchScalarGridSpec(
            num_scalar_prefetch=1,
            grid=(parts,),
            in_specs=[
                pl.BlockSpec((1, picks, 128, width), lambda i, *_: (i, 0, 0, 0)),
                pl.BlockSpec((1, picks, 128, 128), lambda i, *_: (i, 0, 0, 0)),
                whole(gradh),
                whole(feats),
                whole(w_message),
            ],
            out_specs=[whole(gradh), pl.BlockSpec((width, width), lambda i, *_: (0, 0))],
            scratch_shapes=[pltpu.VMEM((rows, width), F32)],
        ),
        out_shape=[jax.ShapeDtypeStruct((rows, width), BF16), jax.ShapeDtypeStruct((width, width), F32)],
        compiler_params=pltpu.CompilerParams(vmem_limit_bytes=VMEM_LIMIT),
        name="tile_step",
    )(cols, got, tiles, gradh, feats, w_message)


def reduce_kernel(
    parts, slabs, factor, msg_ref, upd_ref, out_msg_ref, out_upd_ref,
    mine_ref, in1, mid, in2, part_ref, all2, done, all1, s1, r1, s2, r2, s3, r3, s4, r4,
):
    b, g = lax.axis_index("blk"), lax.axis_index("grp")
    width = msg_ref.shape[0]
    rows = 2 * width // parts
    barrier = pltpu.get_barrier_semaphore()
    for k in range(1, parts):
        pl.semaphore_signal(barrier, inc=1, device_id={"blk": lax.rem(b + k, parts)}, device_id_type=MESH)
    for k in range(1, slabs):
        pl.semaphore_signal(barrier, inc=1, device_id={"grp": lax.rem(g + k, slabs)}, device_id_type=MESH)
    for k in range(parts // 2):
        mine_ref[k] = msg_ref[k * rows : (k + 1) * rows]
        mine_ref[parts // 2 + k] = upd_ref[k * rows : (k + 1) * rows]
    pl.semaphore_wait(barrier, parts + slabs - 2)

    def exchange(n, axis, me, src, dst, send, recv):
        copies = []
        for k in range(1, n):
            peer = lax.rem(me + k, n)
            copy = pltpu.make_async_remote_copy(
                src(peer), dst(k), send.at[k - 1], recv.at[k - 1], device_id={axis: peer}, device_id_type=MESH
            )
            copy.start()
            copies.append(copy)
        for copy in copies:
            copy.wait_recv()
        return copies

    sent = exchange(parts, "blk", b, lambda p: mine_ref.at[p], lambda k: in1.at[k - 1], s1, r1)
    total = mine_ref[b]
    for k in range(parts - 1):
        total += in1[k]
    for n in range(slabs):
        mid[n] = total[n // 2 * 8 : n // 2 * 8 + 8, n % 2 * 128 : n % 2 * 128 + 128]
    sent += exchange(slabs, "grp", g, lambda p: mid.at[p], lambda k: in2.at[k - 1], s2, r2)
    piece = mid[g]
    for k in range(slabs - 1):
        piece += in2[k]
    part_ref[...] = piece * factor
    all2[g] = piece * factor
    sent += exchange(slabs, "grp", g, lambda p: part_ref, lambda k: all2.at[g], s3, r3)
    for n in range(slabs):
        done[n // 2 * 8 : n // 2 * 8 + 8, n % 2 * 128 : n % 2 * 128 + 128] = all2[n]
    all1[b] = done[...]
    sent += exchange(parts, "blk", b, lambda p: done, lambda k: all1.at[b], s4, r4)
    for k in range(parts // 2):
        out_msg_ref[k * rows : (k + 1) * rows] = all1[k]
        out_upd_ref[k * rows : (k + 1) * rows] = all1[parts // 2 + k]
    for copy in sent:
        copy.wait_send()


def reduce_step(msg, upd, parts, slabs, factor):
    width = msg.shape[0]
    rows = 2 * width // parts
    vmem = pl.BlockSpec(memory_space=pltpu.VMEM)
    dma = pltpu.SemaphoreType.DMA
    return pl.pallas_call(
        functools.partial(reduce_kernel, parts, slabs, factor),
        out_shape=[jax.ShapeDtypeStruct(msg.shape, F32)] * 2,
        in_specs=[vmem] * 2,
        out_specs=[vmem] * 2,
        scratch_shapes=[
            pltpu.VMEM((parts, rows, width), F32),
            pltpu.VMEM((parts - 1, rows, width), F32),
            pltpu.VMEM((slabs, 8, 128), F32),
            pltpu.VMEM((slabs - 1, 8, 128), F32),
            pltpu.VMEM((8, 128), F32),
            pltpu.VMEM((slabs, 8, 128), F32),
            pltpu.VMEM((rows, width), F32),
            pltpu.VMEM((parts, rows, width), F32),
            dma((parts - 1,)), dma((parts - 1,)),
            dma((slabs - 1,)), dma((slabs - 1,)),
            dma((slabs - 1,)), dma((slabs - 1,)),
            dma((parts - 1,)), dma((parts - 1,)),
        ],
        compiler_params=pltpu.CompilerParams(collective_id=0, has_side_effects=True, vmem_limit_bytes=VMEM_LIMIT),
        name="reduce_step",
    )(msg, upd)


def local(
    grad_out, pre_act, node_feats, w_message, w_update, tile_vals, tile_rows, tile_cols,
    rec_slab, rec_local, rec_remote, rec_weight,
):
    grad = grad_out[0]
    rows, width = grad.shape
    slabs = lax.axis_size("grp")
    parts = lax.axis_size("blk")
    records = rec_local.shape[1]
    cap = 2 * records // slabs
    lanes = lambda a: a.reshape(records // 128, 128)
    gradh, upd, got = main_step(
        tile_rows[0], lanes(rec_slab), lanes(rec_local), lanes(rec_remote), lanes(rec_weight),
        w_update, grad, pre_act[0], slabs, parts, cap,
    )
    feats, msg = tile_step(tile_cols[0, 0], got, tile_vals[0, 0], gradh, node_feats[0], w_message)
    factor = float((slabs * parts * rows) ** -0.5)
    msg, upd = reduce_step(msg, upd, parts, slabs, factor)
    return (feats[None], msg, upd)


def solution(mesh):
    placed = (
        P("grp", "blk", None),
        P("grp", "blk", None),
        P("grp", "blk", None),
        P(),
        P(),
        P("grp", "blk", None, None, None, None),
        P("grp", None, None, None),
        P("grp", "blk", None, None),
        P("grp", "blk", None),
        P("grp", "blk"),
        P("grp", "blk"),
        P("grp", "blk"),
    )
    return jax.shard_map(
        local,
        mesh=mesh,
        in_specs=placed,
        out_specs=(P("grp", "blk", None), P(), P()),
        check_vma=False,
    )
```

```python
import functools

import jax
import jax.numpy as jnp
from jax import lax
from jax.experimental import pallas as pl
from jax.experimental.pallas import tpu as pltpu
from jax.sharding import PartitionSpec as P

F32 = jnp.float32
BF16 = jnp.bfloat16
MESH = pl.DeviceIdType.MESH
NT = (((1,), (1,)), ((), ()))
TN = (((0,), (0,)), ((), ()))
EXT = 16
VMEM_LIMIT = 56 * 1024 * 1024


def iota(shape, dim):
    return lax.broadcasted_iota(jnp.int32, shape, dim)


def index_tables(slab_ref, local_ref, remote_ref, weight_ref, node_ref, scale_ref, ext_ref):
    slabs, cap = node_ref.shape[0], node_ref.shape[1]
    chunks = slab_ref.shape[0]
    slab = slab_ref[...]
    ids = iota((chunks, slabs, 128), 1)
    choose = jnp.where(ids == slab[:, None, :], 1.0, 0.0)
    flat = choose.reshape(chunks * slabs, 128)
    flat16 = flat.astype(BF16)
    upper = jnp.where(iota((128, 128), 0) < iota((128, 128), 1), 1.0, 0.0).astype(BF16)
    prefix = jnp.dot(flat16, upper, preferred_element_type=F32)
    totals = jnp.dot(flat16, jnp.ones((128, 128), BF16), preferred_element_type=F32)
    size = chunks * slabs
    row, col = iota((size, size), 0), iota((size, size), 1)
    earlier = (col < row) & (lax.rem(col, slabs) == lax.rem(row, slabs))
    offset = jnp.dot(jnp.where(earlier, 1.0, 0.0).astype(BF16), totals.astype(BF16), preferred_element_type=F32)
    place = ((prefix + offset) * flat).reshape(chunks, slabs, 128).sum(axis=1).astype(jnp.int32)
    remote, local, weight = remote_ref[...], local_ref[...], weight_ref[...]
    first = weight.astype(BF16).astype(F32)
    second = (weight - first).astype(BF16).astype(F32)
    third = weight - first - second
    values = [
        (remote // 256).astype(F32),
        (remote % 256).astype(F32),
        (local // 64).astype(F32),
        (local % 64).astype(F32),
        first,
        second,
        third,
        jnp.ones_like(weight),
    ]
    table = jnp.zeros((len(values) * slabs, cap), F32)
    for c in range(chunks):
        left = jnp.concatenate([choose[c] * v[c : c + 1] for v in values], axis=0).astype(BF16)
        right = jnp.where(iota((cap, 128), 0) == place[c : c + 1], 1.0, 0.0).astype(BF16)
        table += lax.dot_general(left, right, NT, preferred_element_type=F32)
    valid = table[7 * slabs : 8 * slabs]
    upper_part = jnp.where(valid > 0.5, table[:slabs], 64.0)
    lower_part = table[slabs : 2 * slabs]
    half = cap // 2
    for s in range(slabs):
        rows = [part[s : s + 1, q * half : (q + 1) * half] for part in (upper_part, lower_part) for q in range(2)]
        block = jnp.concatenate(rows + [jnp.zeros((EXT - 4, half), F32)], axis=0)
        ext_ref[s] = block.astype(BF16)
    turned = jnp.transpose(table)
    for s in range(slabs):
        at = lambda v: turned[:, v * slabs + s : v * slabs + s + 1]
        node_ref[s] = jnp.broadcast_to((at(2) * 64.0 + at(3)).astype(jnp.int32), (cap, 128))
        scale_ref[s] = jnp.broadcast_to(at(4) + at(5) + at(6), (cap, 128))


def sum_scratch(parts, slabs, width):
    rows = width // parts
    dma = pltpu.SemaphoreType.DMA
    return [
        pltpu.VMEM((parts, rows, width), F32),
        pltpu.VMEM((parts - 1, rows, width), F32),
        pltpu.VMEM((slabs, 8, 128), F32),
        pltpu.VMEM((slabs - 1, 8, 128), F32),
        pltpu.VMEM((8, 128), F32),
        pltpu.VMEM((slabs, 8, 128), F32),
        pltpu.VMEM((rows, width), F32),
        pltpu.VMEM((parts, rows, width), F32),
        dma((parts - 1,)), dma((parts - 1,)),
        dma((slabs - 1,)), dma((slabs - 1,)),
        dma((slabs - 1,)), dma((slabs - 1,)),
        dma((parts - 1,)), dma((parts - 1,)),
    ]


def sum_stages(parts, slabs, factor, term_ref, out_ref, scratch):
    mine, in1, mid, in2, part, all2, done, all1, s1, r1, s2, r2, s3, r3, s4, r4 = scratch
    b, g = lax.axis_index("blk"), lax.axis_index("grp")
    width = term_ref.shape[0]
    rows = width // parts
    sent = []

    def exchange(n, axis, me, src, dst, send, recv):
        copies = []
        for k in range(1, n):
            peer = lax.rem(me + k, n)
            copy = pltpu.make_async_remote_copy(
                src(peer), dst(k), send.at[k - 1], recv.at[k - 1], device_id={axis: peer}, device_id_type=MESH
            )
            copy.start()
            copies.append(copy)
        sent.extend(copies)
        return copies

    def begin():
        for k in range(parts):
            mine[k] = term_ref[k * rows : (k + 1) * rows]
        mid[...] = jnp.zeros_like(mid)
        return exchange(parts, "blk", b, lambda p: mine.at[p], lambda k: in1.at[k - 1], s1, r1)

    def end(copies):
        for copy in copies:
            copy.wait_recv()
        total = mine[b]
        for k in range(parts - 1):
            total += in1[k]
        high = rows * 2 // slabs
        spots = [(slice(n // 2 * high, (n // 2 + 1) * high), slice(n % 2 * 128, n % 2 * 128 + 128)) for n in range(slabs)]
        for n in range(slabs):
            mid[n, :high] = total[spots[n]]
        for copy in exchange(slabs, "grp", g, lambda p: mid.at[p], lambda k: in2.at[k - 1], s2, r2):
            copy.wait_recv()
        piece = mid[g]
        for k in range(slabs - 1):
            piece += in2[k]
        part[...] = piece * factor
        all2[g] = piece * factor
        for copy in exchange(slabs, "grp", g, lambda p: part, lambda k: all2.at[g], s3, r3):
            copy.wait_recv()
        for n in range(slabs):
            done[spots[n]] = all2[n, :high]
        all1[b] = done[...]
        for copy in exchange(parts, "blk", b, lambda p: done, lambda k: all1.at[b], s4, r4):
            copy.wait_recv()
        for k in range(parts):
            out_ref[k * rows : (k + 1) * rows] = all1[k]
        for copy in sent:
            copy.wait_send()

    return begin, end


def reduce_kernel(parts, slabs, factor, term_ref, out_ref, *scratch):
    b, g = lax.axis_index("blk"), lax.axis_index("grp")
    barrier = pltpu.get_barrier_semaphore()
    for k in range(1, parts):
        pl.semaphore_signal(barrier, inc=1, device_id={"blk": lax.rem(b + k, parts)}, device_id_type=MESH)
    for k in range(1, slabs):
        pl.semaphore_signal(barrier, inc=1, device_id={"grp": lax.rem(g + k, slabs)}, device_id_type=MESH)
    begin, end = sum_stages(parts, slabs, factor, term_ref, out_ref, scratch)
    pl.semaphore_wait(barrier, parts + slabs - 2)
    end(begin())


def reduce_step(term, parts, slabs, factor):
    vmem = pl.BlockSpec(memory_space=pltpu.VMEM)
    return pl.pallas_call(
        functools.partial(reduce_kernel, parts, slabs, factor),
        out_shape=jax.ShapeDtypeStruct(term.shape, F32),
        in_specs=[vmem],
        out_specs=vmem,
        scratch_shapes=sum_scratch(parts, slabs, term.shape[0]),
        compiler_params=pltpu.CompilerParams(collective_id=0, has_side_effects=True, vmem_limit_bytes=VMEM_LIMIT),
        name="reduce_step",
    )(term)


FAR = ((2, 1), (1, 1), (3, 1), (0, 1), (2, 0), (1, 0), (3, 0))


def main_kernel(
    parts, slabs, factor,
    picks_ref, slab_ref, local_ref, remote_ref, weight_ref, w_ref, grad_hbm, pre_hbm,
    gradh_hbm, upd_ref, got_hbm,
    node_ref, scale_ref, ext_ref, out_buf, in_buf, grad_ref, pre_ref, gradh_ref, acc_ref, gp_ref, stage_ref,
    load_sem, rec_send, rec_recv, blk_send, blk_recv, store_sem, term_ref, *scratch,
):
    b, g = lax.axis_index("blk"), lax.axis_index("grp")
    y, xh = b // 2, b % 2
    xl, z, core = g // 8, (g // 2) % 4, g % 2
    cap = node_ref.shape[1]
    half = cap // 2
    nodes, width = acc_ref.shape
    picks = stage_ref.shape[1]

    load_grad = pltpu.make_async_copy(grad_hbm, grad_ref, load_sem.at[0])
    load_pre = pltpu.make_async_copy(pre_hbm, pre_ref, load_sem.at[1])
    load_grad.start()
    load_pre.start()

    def rec_peer(n):
        q = n // 4
        dz, dx, dc = (n % 4 + 1) % 4, 1 - n // 8, (q + q // 2) % 2
        return ((xl + dx) % 2 * 4 + (z + dz) % 4) * 2 + (core + dc) % 2

    def blk_peer(n):
        dy, dx = FAR[n]
        return (y + dy) % 4 * 2 + (xh + dx) % 2

    barrier = pltpu.get_barrier_semaphore()
    for n in range(slabs - 1):
        pl.semaphore_signal(barrier, inc=1, device_id={"grp": rec_peer(n)}, device_id_type=MESH)
    for n in range(parts - 1):
        pl.semaphore_signal(barrier, inc=1, device_id={"blk": blk_peer(n)}, device_id_type=MESH)

    index_tables(slab_ref, local_ref, remote_ref, weight_ref, node_ref, scale_ref, ext_ref)
    load_grad.wait()
    pl.semaphore_wait(barrier, slabs + parts - 2)

    def rec_copy(n):
        return pltpu.make_async_remote_copy(
            out_buf.at[n], in_buf.at[n], rec_send.at[n], rec_recv.at[n],
            device_id={"grp": rec_peer(n)}, device_id_type=MESH,
        )

    own = slabs - 1
    own_copy = pltpu.make_async_copy(out_buf.at[own], in_buf.at[own], rec_recv.at[own])
    wide = 1024

    def gather(n, _):
        s = rec_peer(n)
        node = node_ref[s]
        total = jnp.zeros((cap, width), F32)
        for k in range(nodes // wide):
            pieces = [
                jnp.where(node == iota((1, 128), 1) + (k * wide + j * 128), 1.0, 0.0).astype(BF16)
                for j in range(wide // 128)
            ]
            total += jnp.dot(
                jnp.concatenate(pieces, axis=1), grad_ref[k * wide : (k + 1) * wide], preferred_element_type=F32
            )
        scale = scale_ref[s]
        out_buf[n, :cap] = (total * jnp.concatenate([scale, scale], axis=1)).astype(BF16)
        out_buf[n, cap:] = ext_ref[s]

        @pl.when(n < own)
        def _():
            rec_copy(n).start()

        return 0

    lax.fori_loop(0, slabs, gather, 0)
    own_copy.start()
    acc_ref[...] = grad_ref[...].astype(F32)
    own_copy.wait()

    tall = 1024

    def scatter(m, _):
        n = (m + own) % slabs

        @pl.when(m > 0)
        def _():
            rec_copy(n).wait_recv()

        ext = in_buf[n, cap:].astype(F32)
        lane = lambda q: jnp.concatenate([ext[q : q + 1], ext[q + 1 : q + 2]], axis=1).astype(jnp.int32)
        high, low = lane(0), lane(2)
        base = jnp.where(iota((256, cap), 0) == low, 1.0, 0.0).astype(BF16).reshape(16, 16, cap)
        block = in_buf[n, :cap]
        for i in range(nodes // tall):
            pieces = []
            for c in range(i * tall // 256, (i + 1) * tall // 256):
                mask = jnp.where(jnp.broadcast_to(high, (16, cap)) == c, 1.0, 0.0).astype(BF16)
                pieces.append((base * mask[None]).reshape(256, cap))
            at = slice(i * tall, (i + 1) * tall)
            acc_ref[at] += jnp.dot(jnp.concatenate(pieces, axis=0), block, preferred_element_type=F32)
        return 0

    lax.fori_loop(0, slabs, scatter, 0)

    load_pre.wait()
    term_ref[...] = jnp.zeros_like(term_ref)

    def finish(i, _):
        at = pl.ds(pl.multiple_of(i * 256, 256), 256)
        gradh = acc_ref[at].astype(BF16)
        gradh_ref[at] = gradh
        pre = pre_ref[at].astype(F32)
        sig = 1.0 / (1.0 + jnp.exp(-pre))
        act = (pre * sig).astype(BF16)
        slope = sig * (1.0 + pre * (1.0 - sig))
        back = lax.dot_general(gradh, w_ref[...], NT, preferred_element_type=F32)
        gp_ref[pl.ds(i * 2, 2)] = (back * slope).astype(BF16).reshape(2, 128, width)
        term_ref[...] += lax.dot_general(act, gradh, TN, preferred_element_type=F32)
        return 0

    lax.fori_loop(0, nodes // 256, finish, 0)
    store_gradh = pltpu.make_async_copy(gradh_ref, gradh_hbm, store_sem.at[0])
    store_gradh.start()
    begin, end = sum_stages(parts, slabs, factor, term_ref, upd_ref, scratch)
    first = begin()

    def pack(n, c):
        def one(t, _):
            stage_ref[n, t] = gp_ref[picks_ref[c, b, t]]
            return 0

        lax.fori_loop(0, picks, one, 0)

    sends = []
    for n in range(parts - 1):
        pack(n, blk_peer(n))
        copy = pltpu.make_async_remote_copy(
            stage_ref.at[n], got_hbm.at[b], blk_send.at[n], blk_recv.at[n],
            device_id={"blk": blk_peer(n)}, device_id_type=MESH,
        )
        copy.start()
        sends.append(copy)
    pack(parts - 1, b)
    keep = pltpu.make_async_copy(stage_ref.at[parts - 1], got_hbm.at[b], store_sem.at[1])
    keep.start()
    end(first)
    lax.fori_loop(0, slabs - 1, lambda n, x: (rec_copy(n).wait_send(), x)[1], 0)
    for copy in sends:
        copy.wait()
    keep.wait()
    store_gradh.wait()


def main_step(picks, slab, local, remote, weight, w_update, grad, pre, slabs, parts, cap, factor):
    nodes, width = grad.shape
    count = picks.shape[-1]
    vmem = pl.BlockSpec(memory_space=pltpu.VMEM)
    hbm = pl.BlockSpec(memory_space=pl.ANY)
    dma = pltpu.SemaphoreType.DMA
    return pl.pallas_call(
        functools.partial(main_kernel, parts, slabs, factor),
        out_shape=[
            jax.ShapeDtypeStruct((nodes, width), BF16),
            jax.ShapeDtypeStruct((width, width), F32),
            jax.ShapeDtypeStruct((parts, count, 128, width), BF16),
        ],
        in_specs=[pl.BlockSpec(memory_space=pltpu.SMEM)] + [vmem] * 5 + [hbm] * 2,
        out_specs=[hbm, vmem, hbm],
        scratch_shapes=[
            pltpu.VMEM((slabs, cap, 128), jnp.int32),
            pltpu.VMEM((slabs, cap, 128), F32),
            pltpu.VMEM((slabs, EXT, width), BF16),
            pltpu.VMEM((slabs, cap + EXT, width), BF16),
            pltpu.VMEM((slabs, cap + EXT, width), BF16),
            pltpu.VMEM((nodes, width), BF16),
            pltpu.VMEM((nodes, width), BF16),
            pltpu.VMEM((nodes, width), BF16),
            pltpu.VMEM((nodes, width), F32),
            pltpu.VMEM((nodes // 128, 128, width), BF16),
            pltpu.VMEM((parts, count, 128, width), BF16),
            dma((2,)), dma((slabs - 1,)), dma((slabs,)), dma((parts - 1,)), dma((parts - 1,)), dma((2,)),
            pltpu.VMEM((width, width), F32),
        ]
        + sum_scratch(parts, slabs, width),
        compiler_params=pltpu.CompilerParams(collective_id=1, has_side_effects=True, vmem_limit_bytes=VMEM_LIMIT),
        name="main_step",
    )(picks, slab, local, remote, weight, w_update, grad, pre)


def tile_kernel(cols_ref, got_ref, tiles_ref, gradh_ref, feats_ref, w_ref, out_ref, msg_ref, total_ref):
    r = pl.program_id(0)
    picks = got_ref.shape[1]

    @pl.when(r == 0)
    def _():
        total_ref[...] = jnp.zeros_like(total_ref)

    for t in range(picks):
        part = lax.dot_general(tiles_ref[0, t], got_ref[0, t], TN, preferred_element_type=F32)
        at = pl.ds(pl.multiple_of(cols_ref[r, t] * 128, 128), 128)
        total_ref[at] += part

    @pl.when(r == pl.num_programs(0) - 1)
    def _():
        msg = jnp.zeros(msg_ref.shape, F32)
        tall = 512
        for k in range(total_ref.shape[0] // tall):
            at = slice(k * tall, (k + 1) * tall)
            spread = total_ref[at].astype(BF16)
            msg += lax.dot_general(feats_ref[at], spread, TN, preferred_element_type=F32)
            down = lax.dot_general(spread, w_ref[...], NT, preferred_element_type=F32)
            out_ref[at] = (gradh_ref[at].astype(F32) + down).astype(BF16)
        msg_ref[...] = msg


def tile_step(cols, got, tiles, gradh, feats, w_message):
    parts, picks = cols.shape
    rows, width = gradh.shape
    whole = lambda a: pl.BlockSpec(a.shape, lambda i, *_: (0,) * a.ndim)
    return pl.pallas_call(
        tile_kernel,
        grid_spec=pltpu.PrefetchScalarGridSpec(
            num_scalar_prefetch=1,
            grid=(parts,),
            in_specs=[
                pl.BlockSpec((1, picks, 128, width), lambda i, *_: (i, 0, 0, 0)),
                pl.BlockSpec((1, picks, 128, 128), lambda i, *_: (i, 0, 0, 0)),
                whole(gradh),
                whole(feats),
                whole(w_message),
            ],
            out_specs=[whole(gradh), pl.BlockSpec((width, width), lambda i, *_: (0, 0))],
            scratch_shapes=[pltpu.VMEM((rows, width), F32)],
        ),
        out_shape=[jax.ShapeDtypeStruct((rows, width), BF16), jax.ShapeDtypeStruct((width, width), F32)],
        compiler_params=pltpu.CompilerParams(vmem_limit_bytes=VMEM_LIMIT),
        name="tile_step",
    )(cols, got, tiles, gradh, feats, w_message)


def local(
    grad_out, pre_act, node_feats, w_message, w_update, tile_vals, tile_rows, tile_cols,
    rec_slab, rec_local, rec_remote, rec_weight,
):
    grad = grad_out[0]
    rows, width = grad.shape
    slabs = lax.axis_size("grp")
    parts = lax.axis_size("blk")
    records = rec_local.shape[1]
    cap = 2 * records // slabs
    factor = float((slabs * parts * rows) ** -0.5)
    lanes = lambda a: a.reshape(records // 128, 128)
    gradh, upd, got = main_step(
        tile_rows[0], lanes(rec_slab), lanes(rec_local), lanes(rec_remote), lanes(rec_weight),
        w_update, grad, pre_act[0], slabs, parts, cap, factor,
    )
    feats, msg = tile_step(tile_cols[0, 0], got, tile_vals[0, 0], gradh, node_feats[0], w_message)
    msg = reduce_step(msg, parts, slabs, factor)
    return (feats[None], msg, upd)


def solution(mesh):
    placed = (
        P("grp", "blk", None),
        P("grp", "blk", None),
        P("grp", "blk", None),
        P(),
        P(),
        P("grp", "blk", None, None, None, None),
        P("grp", None, None, None),
        P("grp", "blk", None, None),
        P("grp", "blk", None),
        P("grp", "blk"),
        P("grp", "blk"),
        P("grp", "blk"),
    )
    return jax.shard_map(
        local,
        mesh=mesh,
        in_specs=placed,
        out_specs=(P("grp", "blk", None), P(), P()),
        check_vma=False,
    )
```

```python
import functools

import jax
import jax.numpy as jnp
from jax import lax
from jax.experimental import pallas as pl
from jax.experimental.pallas import tpu as pltpu
from jax.sharding import PartitionSpec as P

F32 = jnp.float32
BF16 = jnp.bfloat16
MESH = pl.DeviceIdType.MESH
NT = (((1,), (1,)), ((), ()))
TN = (((0,), (0,)), ((), ()))
EXT = 16
VMEM_LIMIT = 56 * 1024 * 1024


def iota(shape, dim):
    return lax.broadcasted_iota(jnp.int32, shape, dim)


def index_tables(slab_ref, local_ref, remote_ref, weight_ref, node_ref, scale_ref, ext_ref):
    slabs, cap = node_ref.shape[0], node_ref.shape[1]
    chunks = slab_ref.shape[0]
    slab = slab_ref[...]
    ids = iota((chunks, slabs, 128), 1)
    choose = jnp.where(ids == slab[:, None, :], 1.0, 0.0)
    flat = choose.reshape(chunks * slabs, 128)
    flat16 = flat.astype(BF16)
    upper = jnp.where(iota((128, 128), 0) < iota((128, 128), 1), 1.0, 0.0).astype(BF16)
    prefix = jnp.dot(flat16, upper, preferred_element_type=F32)
    totals = jnp.dot(flat16, jnp.ones((128, 128), BF16), preferred_element_type=F32)
    size = chunks * slabs
    row, col = iota((size, size), 0), iota((size, size), 1)
    earlier = (col < row) & (lax.rem(col, slabs) == lax.rem(row, slabs))
    offset = jnp.dot(jnp.where(earlier, 1.0, 0.0).astype(BF16), totals.astype(BF16), preferred_element_type=F32)
    place = ((prefix + offset) * flat).reshape(chunks, slabs, 128).sum(axis=1).astype(jnp.int32)
    remote, local, weight = remote_ref[...], local_ref[...], weight_ref[...]
    first = weight.astype(BF16).astype(F32)
    second = (weight - first).astype(BF16).astype(F32)
    third = weight - first - second
    values = [
        (remote // 256).astype(F32),
        (remote % 256).astype(F32),
        (local // 64).astype(F32),
        (local % 64).astype(F32),
        first,
        second,
        third,
        jnp.ones_like(weight),
    ]
    table = jnp.zeros((len(values) * slabs, cap), F32)
    for c in range(chunks):
        left = jnp.concatenate([choose[c] * v[c : c + 1] for v in values], axis=0).astype(BF16)
        right = jnp.where(iota((cap, 128), 0) == place[c : c + 1], 1.0, 0.0).astype(BF16)
        table += lax.dot_general(left, right, NT, preferred_element_type=F32)
    valid = table[7 * slabs : 8 * slabs]
    upper_part = jnp.where(valid > 0.5, table[:slabs], 64.0)
    lower_part = table[slabs : 2 * slabs]
    half = cap // 2
    for s in range(slabs):
        rows = [part[s : s + 1, q * half : (q + 1) * half] for part in (upper_part, lower_part) for q in range(2)]
        block = jnp.concatenate(rows + [jnp.zeros((EXT - 4, half), F32)], axis=0)
        ext_ref[s] = block.astype(BF16)
    turned = jnp.transpose(table)
    for s in range(slabs):
        at = lambda v: turned[:, v * slabs + s : v * slabs + s + 1]
        node_ref[s] = jnp.broadcast_to((at(2) * 64.0 + at(3)).astype(jnp.int32), (cap, 128))
        scale_ref[s] = jnp.broadcast_to(at(4) + at(5) + at(6), (cap, 128))


def sum_scratch(parts, slabs, width):
    rows = 2 * width // parts
    dma = pltpu.SemaphoreType.DMA
    return [
        pltpu.VMEM((parts, rows, width), F32),
        pltpu.VMEM((parts - 1, rows, width), F32),
        pltpu.VMEM((slabs, 8, 128), F32),
        pltpu.VMEM((slabs - 1, 8, 128), F32),
        pltpu.VMEM((8, 128), F32),
        pltpu.VMEM((slabs, 8, 128), F32),
        pltpu.VMEM((rows, width), F32),
        pltpu.VMEM((parts, rows, width), F32),
        dma((parts - 1,)), dma((parts - 1,)),
        dma((slabs - 1,)), dma((slabs - 1,)),
        dma((slabs - 1,)), dma((slabs - 1,)),
        dma((parts - 1,)), dma((parts - 1,)),
    ]


def sum_stages(parts, slabs, factor, term_refs, out_refs, scratch):
    mine, in1, mid, in2, part, all2, done, all1, s1, r1, s2, r2, s3, r3, s4, r4 = scratch
    b, g = lax.axis_index("blk"), lax.axis_index("grp")
    rows, half = mine.shape[1], parts // 2
    sent = []

    def exchange(n, axis, me, src, dst, send, recv):
        copies = []
        for k in range(1, n):
            peer = lax.rem(me + k, n)
            copy = pltpu.make_async_remote_copy(
                src(peer), dst(k), send.at[k - 1], recv.at[k - 1], device_id={axis: peer}, device_id_type=MESH
            )
            copy.start()
            copies.append(copy)
        sent.extend(copies)
        return copies

    def begin():
        for k in range(parts):
            mine[k] = term_refs[k // half][k % half * rows : (k % half + 1) * rows]
        return exchange(parts, "blk", b, lambda p: mine.at[p], lambda k: in1.at[k - 1], s1, r1)

    def end(copies):
        for copy in copies:
            copy.wait_recv()
        total = mine[b]
        for k in range(parts - 1):
            total += in1[k]
        high = rows * 2 // slabs
        spots = [(slice(n // 2 * high, (n // 2 + 1) * high), slice(n % 2 * 128, n % 2 * 128 + 128)) for n in range(slabs)]
        for n in range(slabs):
            mid[n] = total[spots[n]]
        for copy in exchange(slabs, "grp", g, lambda p: mid.at[p], lambda k: in2.at[k - 1], s2, r2):
            copy.wait_recv()
        piece = mid[g]
        for k in range(slabs - 1):
            piece += in2[k]
        part[...] = piece * factor
        all2[g] = piece * factor
        for copy in exchange(slabs, "grp", g, lambda p: part, lambda k: all2.at[g], s3, r3):
            copy.wait_recv()
        for n in range(slabs):
            done[spots[n]] = all2[n]
        all1[b] = done[...]
        for copy in exchange(parts, "blk", b, lambda p: done, lambda k: all1.at[b], s4, r4):
            copy.wait_recv()
        for k in range(parts):
            out_refs[k // half][k % half * rows : (k % half + 1) * rows] = all1[k]
        for copy in sent:
            copy.wait_send()

    return begin, end


def reduce_kernel(parts, slabs, factor, msg_ref, upd_ref, out_msg_ref, out_upd_ref, *scratch):
    b, g = lax.axis_index("blk"), lax.axis_index("grp")
    barrier = pltpu.get_barrier_semaphore()
    for k in range(1, parts):
        pl.semaphore_signal(barrier, inc=1, device_id={"blk": lax.rem(b + k, parts)}, device_id_type=MESH)
    for k in range(1, slabs):
        pl.semaphore_signal(barrier, inc=1, device_id={"grp": lax.rem(g + k, slabs)}, device_id_type=MESH)
    begin, end = sum_stages(parts, slabs, factor, (msg_ref, upd_ref), (out_msg_ref, out_upd_ref), scratch)
    pl.semaphore_wait(barrier, parts + slabs - 2)
    end(begin())


def reduce_step(msg, upd, parts, slabs, factor):
    vmem = pl.BlockSpec(memory_space=pltpu.VMEM)
    return pl.pallas_call(
        functools.partial(reduce_kernel, parts, slabs, factor),
        out_shape=[jax.ShapeDtypeStruct(msg.shape, F32)] * 2,
        in_specs=[vmem] * 2,
        out_specs=[vmem] * 2,
        scratch_shapes=sum_scratch(parts, slabs, msg.shape[0]),
        compiler_params=pltpu.CompilerParams(collective_id=0, has_side_effects=True, vmem_limit_bytes=VMEM_LIMIT),
        name="reduce_step",
    )(msg, upd)


FAR = ((2, 1), (1, 1), (3, 1), (0, 1), (2, 0), (1, 0), (3, 0))


def main_kernel(
    parts, slabs,
    picks_ref, slab_ref, local_ref, remote_ref, weight_ref, w_ref, grad_hbm, pre_hbm,
    gradh_hbm, upd_ref, got_hbm,
    node_ref, scale_ref, ext_ref, out_buf, in_buf, grad_ref, pre_ref, gradh_ref, acc_ref, gp_ref, stage_ref,
    load_sem, rec_send, rec_recv, blk_send, blk_recv, store_sem,
):
    b, g = lax.axis_index("blk"), lax.axis_index("grp")
    y, xh = b // 2, b % 2
    xl, z, core = g // 8, (g // 2) % 4, g % 2
    cap = node_ref.shape[1]
    half = cap // 2
    nodes, width = acc_ref.shape
    picks = stage_ref.shape[1]

    load_grad = pltpu.make_async_copy(grad_hbm, grad_ref, load_sem.at[0])
    load_pre = pltpu.make_async_copy(pre_hbm, pre_ref, load_sem.at[1])
    load_grad.start()
    load_pre.start()

    def rec_peer(n):
        q = n // 4
        dz, dx, dc = (n % 4 + 1) % 4, 1 - n // 8, (q + q // 2) % 2
        return ((xl + dx) % 2 * 4 + (z + dz) % 4) * 2 + (core + dc) % 2

    def blk_peer(n):
        dy, dx = FAR[n]
        return (y + dy) % 4 * 2 + (xh + dx) % 2

    barrier = pltpu.get_barrier_semaphore()
    for n in range(slabs - 1):
        pl.semaphore_signal(barrier, inc=1, device_id={"grp": rec_peer(n)}, device_id_type=MESH)
    for n in range(parts - 1):
        pl.semaphore_signal(barrier, inc=1, device_id={"blk": blk_peer(n)}, device_id_type=MESH)

    index_tables(slab_ref, local_ref, remote_ref, weight_ref, node_ref, scale_ref, ext_ref)
    load_grad.wait()
    pl.semaphore_wait(barrier, slabs + parts - 2)

    def rec_copy(n):
        return pltpu.make_async_remote_copy(
            out_buf.at[n], in_buf.at[n], rec_send.at[n], rec_recv.at[n],
            device_id={"grp": rec_peer(n)}, device_id_type=MESH,
        )

    own = slabs - 1
    own_copy = pltpu.make_async_copy(out_buf.at[own], in_buf.at[own], rec_recv.at[own])
    wide = 1024

    def gather(n, _):
        s = rec_peer(n)
        node = node_ref[s]
        total = jnp.zeros((cap, width), F32)
        for k in range(nodes // wide):
            pieces = [
                jnp.where(node == iota((1, 128), 1) + (k * wide + j * 128), 1.0, 0.0).astype(BF16)
                for j in range(wide // 128)
            ]
            total += jnp.dot(
                jnp.concatenate(pieces, axis=1), grad_ref[k * wide : (k + 1) * wide], preferred_element_type=F32
            )
        scale = scale_ref[s]
        out_buf[n, :cap] = (total * jnp.concatenate([scale, scale], axis=1)).astype(BF16)
        out_buf[n, cap:] = ext_ref[s]

        @pl.when(n < own)
        def _():
            rec_copy(n).start()

        return 0

    lax.fori_loop(0, slabs, gather, 0)
    own_copy.start()
    acc_ref[...] = grad_ref[...].astype(F32)
    own_copy.wait()

    tall = 1024

    def scatter(m, _):
        n = (m + own) % slabs

        @pl.when(m > 0)
        def _():
            rec_copy(n).wait_recv()

        ext = in_buf[n, cap:].astype(F32)
        lane = lambda q: jnp.concatenate([ext[q : q + 1], ext[q + 1 : q + 2]], axis=1).astype(jnp.int32)
        high, low = lane(0), lane(2)
        base = jnp.where(iota((256, cap), 0) == low, 1.0, 0.0).astype(BF16).reshape(16, 16, cap)
        block = in_buf[n, :cap]
        for i in range(nodes // tall):
            pieces = []
            for c in range(i * tall // 256, (i + 1) * tall // 256):
                mask = jnp.where(jnp.broadcast_to(high, (16, cap)) == c, 1.0, 0.0).astype(BF16)
                pieces.append((base * mask[None]).reshape(256, cap))
            at = slice(i * tall, (i + 1) * tall)
            acc_ref[at] += jnp.dot(jnp.concatenate(pieces, axis=0), block, preferred_element_type=F32)
        return 0

    lax.fori_loop(0, slabs, scatter, 0)

    load_pre.wait()
    upd_ref[...] = jnp.zeros_like(upd_ref)

    def finish(i, _):
        at = pl.ds(pl.multiple_of(i * 256, 256), 256)
        gradh = acc_ref[at].astype(BF16)
        gradh_ref[at] = gradh
        pre = pre_ref[at].astype(F32)
        sig = 1.0 / (1.0 + jnp.exp(-pre))
        act = (pre * sig).astype(BF16)
        slope = sig * (1.0 + pre * (1.0 - sig))
        back = lax.dot_general(gradh, w_ref[...], NT, preferred_element_type=F32)
        gp_ref[pl.ds(i * 2, 2)] = (back * slope).astype(BF16).reshape(2, 128, width)
        upd_ref[...] += lax.dot_general(act, gradh, TN, preferred_element_type=F32)
        return 0

    lax.fori_loop(0, nodes // 256, finish, 0)
    store_gradh = pltpu.make_async_copy(gradh_ref, gradh_hbm, store_sem.at[0])
    store_gradh.start()

    def pack(n, c):
        def one(t, _):
            stage_ref[n, t] = gp_ref[picks_ref[c, b, t]]
            return 0

        lax.fori_loop(0, picks, one, 0)

    sends = []
    for n in range(parts - 1):
        pack(n, blk_peer(n))
        copy = pltpu.make_async_remote_copy(
            stage_ref.at[n], got_hbm.at[b], blk_send.at[n], blk_recv.at[n],
            device_id={"blk": blk_peer(n)}, device_id_type=MESH,
        )
        copy.start()
        sends.append(copy)
    pack(parts - 1, b)
    keep = pltpu.make_async_copy(stage_ref.at[parts - 1], got_hbm.at[b], store_sem.at[1])
    keep.start()
    lax.fori_loop(0, slabs - 1, lambda n, x: (rec_copy(n).wait_send(), x)[1], 0)
    for copy in sends:
        copy.wait()
    keep.wait()
    store_gradh.wait()


def main_step(picks, slab, local, remote, weight, w_update, grad, pre, slabs, parts, cap):
    nodes, width = grad.shape
    count = picks.shape[-1]
    vmem = pl.BlockSpec(memory_space=pltpu.VMEM)
    hbm = pl.BlockSpec(memory_space=pl.ANY)
    dma = pltpu.SemaphoreType.DMA
    return pl.pallas_call(
        functools.partial(main_kernel, parts, slabs),
        out_shape=[
            jax.ShapeDtypeStruct((nodes, width), BF16),
            jax.ShapeDtypeStruct((width, width), F32),
            jax.ShapeDtypeStruct((parts, count, 128, width), BF16),
        ],
        in_specs=[pl.BlockSpec(memory_space=pltpu.SMEM)] + [vmem] * 5 + [hbm] * 2,
        out_specs=[hbm, vmem, hbm],
        scratch_shapes=[
            pltpu.VMEM((slabs, cap, 128), jnp.int32),
            pltpu.VMEM((slabs, cap, 128), F32),
            pltpu.VMEM((slabs, EXT, width), BF16),
            pltpu.VMEM((slabs, cap + EXT, width), BF16),
            pltpu.VMEM((slabs, cap + EXT, width), BF16),
            pltpu.VMEM((nodes, width), BF16),
            pltpu.VMEM((nodes, width), BF16),
            pltpu.VMEM((nodes, width), BF16),
            pltpu.VMEM((nodes, width), F32),
            pltpu.VMEM((nodes // 128, 128, width), BF16),
            pltpu.VMEM((parts, count, 128, width), BF16),
            dma((2,)), dma((slabs - 1,)), dma((slabs,)), dma((parts - 1,)), dma((parts - 1,)), dma((2,)),
        ],
        compiler_params=pltpu.CompilerParams(collective_id=1, has_side_effects=True, vmem_limit_bytes=VMEM_LIMIT),
        name="main_step",
    )(picks, slab, local, remote, weight, w_update, grad, pre)


def tile_kernel(cols_ref, got_ref, tiles_ref, gradh_ref, feats_ref, w_ref, out_ref, msg_ref, total_ref):
    r = pl.program_id(0)
    picks = got_ref.shape[1]

    @pl.when(r == 0)
    def _():
        total_ref[...] = jnp.zeros_like(total_ref)

    for t in range(picks):
        part = lax.dot_general(tiles_ref[0, t], got_ref[0, t], TN, preferred_element_type=F32)
        at = pl.ds(pl.multiple_of(cols_ref[r, t] * 128, 128), 128)
        total_ref[at] += part

    @pl.when(r == pl.num_programs(0) - 1)
    def _():
        msg = jnp.zeros(msg_ref.shape, F32)
        tall = 512
        for k in range(total_ref.shape[0] // tall):
            at = slice(k * tall, (k + 1) * tall)
            spread = total_ref[at].astype(BF16)
            msg += lax.dot_general(feats_ref[at], spread, TN, preferred_element_type=F32)
            down = lax.dot_general(spread, w_ref[...], NT, preferred_element_type=F32)
            out_ref[at] = (gradh_ref[at].astype(F32) + down).astype(BF16)
        msg_ref[...] = msg


def tile_step(cols, got, tiles, gradh, feats, w_message):
    parts, picks = cols.shape
    rows, width = gradh.shape
    whole = lambda a: pl.BlockSpec(a.shape, lambda i, *_: (0,) * a.ndim)
    return pl.pallas_call(
        tile_kernel,
        grid_spec=pltpu.PrefetchScalarGridSpec(
            num_scalar_prefetch=1,
            grid=(parts,),
            in_specs=[
                pl.BlockSpec((1, picks, 128, width), lambda i, *_: (i, 0, 0, 0)),
                pl.BlockSpec((1, picks, 128, 128), lambda i, *_: (i, 0, 0, 0)),
                whole(gradh),
                whole(feats),
                whole(w_message),
            ],
            out_specs=[whole(gradh), pl.BlockSpec((width, width), lambda i, *_: (0, 0))],
            scratch_shapes=[pltpu.VMEM((rows, width), F32)],
        ),
        out_shape=[jax.ShapeDtypeStruct((rows, width), BF16), jax.ShapeDtypeStruct((width, width), F32)],
        compiler_params=pltpu.CompilerParams(vmem_limit_bytes=VMEM_LIMIT),
        name="tile_step",
    )(cols, got, tiles, gradh, feats, w_message)


def local(
    grad_out, pre_act, node_feats, w_message, w_update, tile_vals, tile_rows, tile_cols,
    rec_slab, rec_local, rec_remote, rec_weight,
):
    grad = grad_out[0]
    rows, width = grad.shape
    slabs = lax.axis_size("grp")
    parts = lax.axis_size("blk")
    records = rec_local.shape[1]
    cap = 2 * records // slabs
    factor = float((slabs * parts * rows) ** -0.5)
    lanes = lambda a: a.reshape(records // 128, 128)
    gradh, upd, got = main_step(
        tile_rows[0], lanes(rec_slab), lanes(rec_local), lanes(rec_remote), lanes(rec_weight),
        w_update, grad, pre_act[0], slabs, parts, cap,
    )
    feats, msg = tile_step(tile_cols[0, 0], got, tile_vals[0, 0], gradh, node_feats[0], w_message)
    msg, upd = reduce_step(msg, upd, parts, slabs, factor)
    return (feats[None], msg, upd)


def solution(mesh):
    placed = (
        P("grp", "blk", None),
        P("grp", "blk", None),
        P("grp", "blk", None),
        P(),
        P(),
        P("grp", "blk", None, None, None, None),
        P("grp", None, None, None),
        P("grp", "blk", None, None),
        P("grp", "blk", None),
        P("grp", "blk"),
        P("grp", "blk"),
        P("grp", "blk"),
    )
    return jax.shard_map(
        local,
        mesh=mesh,
        in_specs=placed,
        out_specs=(P("grp", "blk", None), P(), P()),
        check_vma=False,
    )
```

```python
import functools

import jax
import jax.numpy as jnp
from jax import lax
from jax.experimental import pallas as pl
from jax.experimental.pallas import tpu as pltpu
from jax.sharding import PartitionSpec as P

F32 = jnp.float32
BF16 = jnp.bfloat16
MESH = pl.DeviceIdType.MESH
NT = (((1,), (1,)), ((), ()))
TN = (((0,), (0,)), ((), ()))
EXT = 16
VMEM_LIMIT = 61 * 1024 * 1024


def iota(shape, dim):
    return lax.broadcasted_iota(jnp.int32, shape, dim)


def index_tables(slab_ref, local_ref, remote_ref, weight_ref, node_ref, scale_ref, ext_ref):
    slabs, cap = node_ref.shape[0], node_ref.shape[1]
    chunks = slab_ref.shape[0]
    slab = slab_ref[...]
    ids = iota((chunks, slabs, 128), 1)
    choose = jnp.where(ids == slab[:, None, :], 1.0, 0.0)
    flat = choose.reshape(chunks * slabs, 128)
    flat16 = flat.astype(BF16)
    upper = jnp.where(iota((128, 128), 0) < iota((128, 128), 1), 1.0, 0.0).astype(BF16)
    prefix = jnp.dot(flat16, upper, preferred_element_type=F32)
    totals = jnp.dot(flat16, jnp.ones((128, 128), BF16), preferred_element_type=F32)
    size = chunks * slabs
    row, col = iota((size, size), 0), iota((size, size), 1)
    earlier = (col < row) & (lax.rem(col, slabs) == lax.rem(row, slabs))
    offset = jnp.dot(jnp.where(earlier, 1.0, 0.0).astype(BF16), totals.astype(BF16), preferred_element_type=F32)
    place = ((prefix + offset) * flat).reshape(chunks, slabs, 128).sum(axis=1).astype(jnp.int32)
    remote, local, weight = remote_ref[...], local_ref[...], weight_ref[...]
    first = weight.astype(BF16).astype(F32)
    second = (weight - first).astype(BF16).astype(F32)
    third = weight - first - second
    values = [
        (remote // 256).astype(F32),
        (remote % 256).astype(F32),
        (local // 64).astype(F32),
        (local % 64).astype(F32),
        first,
        second,
        third,
        jnp.ones_like(weight),
    ]
    table = jnp.zeros((len(values) * slabs, cap), F32)
    for c in range(chunks):
        left = jnp.concatenate([choose[c] * v[c : c + 1] for v in values], axis=0).astype(BF16)
        right = jnp.where(iota((cap, 128), 0) == place[c : c + 1], 1.0, 0.0).astype(BF16)
        table += lax.dot_general(left, right, NT, preferred_element_type=F32)
    valid = table[7 * slabs : 8 * slabs]
    upper_part = jnp.where(valid > 0.5, table[:slabs], 64.0)
    lower_part = table[slabs : 2 * slabs]
    half = cap // 2
    for s in range(slabs):
        rows = [part[s : s + 1, q * half : (q + 1) * half] for part in (upper_part, lower_part) for q in range(2)]
        block = jnp.concatenate(rows + [jnp.zeros((EXT - 4, half), F32)], axis=0)
        ext_ref[s] = block.astype(BF16)
    turned = jnp.transpose(table)
    for s in range(slabs):
        at = lambda v: turned[:, v * slabs + s : v * slabs + s + 1]
        node_ref[s] = jnp.broadcast_to((at(2) * 64.0 + at(3)).astype(jnp.int32), (cap, 128))
        scale_ref[s] = jnp.broadcast_to(at(4) + at(5) + at(6), (cap, 128))


def sum_scratch(parts, slabs, width):
    rows = 2 * width // parts
    dma = pltpu.SemaphoreType.DMA
    return [
        pltpu.VMEM((parts, rows, width), F32),
        pltpu.VMEM((parts - 1, rows, width), F32),
        pltpu.VMEM((slabs, 8, 128), F32),
        pltpu.VMEM((slabs - 1, 8, 128), F32),
        pltpu.VMEM((8, 128), F32),
        pltpu.VMEM((slabs, 8, 128), F32),
        pltpu.VMEM((rows, width), F32),
        pltpu.VMEM((parts, rows, width), F32),
        dma((parts - 1,)), dma((parts - 1,)),
        dma((slabs - 1,)), dma((slabs - 1,)),
        dma((slabs - 1,)), dma((slabs - 1,)),
        dma((parts - 1,)), dma((parts - 1,)),
    ]


def sum_stages(parts, slabs, factor, term_refs, out_refs, scratch):
    mine, in1, mid, in2, part, all2, done, all1, s1, r1, s2, r2, s3, r3, s4, r4 = scratch
    b, g = lax.axis_index("blk"), lax.axis_index("grp")
    rows, half = mine.shape[1], parts // 2
    sent = []

    def exchange(n, axis, me, src, dst, send, recv):
        copies = []
        for k in range(1, n):
            peer = lax.rem(me + k, n)
            copy = pltpu.make_async_remote_copy(
                src(peer), dst(k), send.at[k - 1], recv.at[k - 1], device_id={axis: peer}, device_id_type=MESH
            )
            copy.start()
            copies.append(copy)
        sent.extend(copies)
        return copies

    def begin():
        for k in range(parts):
            mine[k] = term_refs[k // half][k % half * rows : (k % half + 1) * rows]
        return exchange(parts, "blk", b, lambda p: mine.at[p], lambda k: in1.at[k - 1], s1, r1)

    def end(copies):
        for copy in copies:
            copy.wait_recv()
        total = mine[b]
        for k in range(parts - 1):
            total += in1[k]
        high = rows * 2 // slabs
        spots = [(slice(n // 2 * high, (n // 2 + 1) * high), slice(n % 2 * 128, n % 2 * 128 + 128)) for n in range(slabs)]
        for n in range(slabs):
            mid[n] = total[spots[n]]
        for copy in exchange(slabs, "grp", g, lambda p: mid.at[p], lambda k: in2.at[k - 1], s2, r2):
            copy.wait_recv()
        piece = mid[g]
        for k in range(slabs - 1):
            piece += in2[k]
        part[...] = piece * factor
        all2[g] = piece * factor
        for copy in exchange(slabs, "grp", g, lambda p: part, lambda k: all2.at[g], s3, r3):
            copy.wait_recv()
        for n in range(slabs):
            done[spots[n]] = all2[n]
        all1[b] = done[...]
        for copy in exchange(parts, "blk", b, lambda p: done, lambda k: all1.at[b], s4, r4):
            copy.wait_recv()
        for k in range(parts):
            out_refs[k // half][k % half * rows : (k % half + 1) * rows] = all1[k]
        for copy in sent:
            copy.wait_send()

    return begin, end


def column_order(cols_ref, order_ref):
    count = cols_ref.shape[1]
    cols = jnp.broadcast_to(cols_ref[...].astype(F32), (count, count))
    across, down = iota((count, count), 1).astype(F32), iota((count, count), 0).astype(F32)
    turned = jnp.transpose(cols)
    ones = lambda hit: jnp.where(hit, 1.0, 0.0)
    total = lambda x: jnp.sum(x, axis=0, keepdims=True)
    rank = total(ones(turned * count + down < cols * count + across))
    ranks = jnp.transpose(jnp.broadcast_to(rank, (count, count)))
    hit = ones(ranks == across)
    order = total(hit * down)
    here = total(hit * turned)
    before = total(ones(ranks == across - 1.0) * (turned + 1.0)) - 1.0
    last = jnp.maximum(total(ones(turned <= across)) - 1.0, 0.0)
    named = jnp.minimum(total(ones(turned == across)), 1.0)
    rows = [order, ones(here == before), last, named, jnp.zeros((4, count), F32)]
    order_ref[...] = jnp.concatenate(rows, axis=0).astype(jnp.int32)


FAR = ((2, 1), (1, 1), (3, 1), (0, 1), (2, 0), (1, 0), (3, 0))


def main_kernel(
    parts, slabs, factor,
    picks_ref, slab_ref, local_ref, remote_ref, weight_ref, cols_ref, w_ref, grad_hbm, pre_hbm, feats_hbm, tiles_hbm,
    gradh_hbm, spread_hbm, out_msg_ref, out_upd_ref,
    node_ref, scale_ref, ext_ref, out_buf, in_buf, grad_ref, pre_ref, acc_ref, gp_ref, stage_ref, got_ref,
    tiles_ref, run_ref, turned_ref, order_ref, order_smem, msg_ref, upd_ref,
    load_sem, rec_send, rec_recv, blk_send, blk_recv, store_sem, *scratch,
):
    b, g = lax.axis_index("blk"), lax.axis_index("grp")
    y, xh = b // 2, b % 2
    xl, z, core = g // 8, (g // 2) % 4, g % 2
    cap = node_ref.shape[1]
    nodes, width = acc_ref.shape
    picks = stage_ref.shape[1]

    load_grad = pltpu.make_async_copy(grad_hbm, grad_ref, load_sem.at[0])
    load_pre = pltpu.make_async_copy(pre_hbm, pre_ref, load_sem.at[1])
    load_tiles = pltpu.make_async_copy(tiles_hbm, tiles_ref, load_sem.at[2])
    load_feats = pltpu.make_async_copy(feats_hbm, pre_ref, load_sem.at[3])
    load_grad.start()
    load_pre.start()
    load_tiles.start()

    def rec_peer(n):
        q = n // 4
        dz, dx, dc = (n % 4 + 1) % 4, 1 - n // 8, (q + q // 2) % 2
        return ((xl + dx) % 2 * 4 + (z + dz) % 4) * 2 + (core + dc) % 2

    def blk_peer(n):
        dy, dx = FAR[n]
        return (y + dy) % 4 * 2 + (xh + dx) % 2

    barrier = pltpu.get_barrier_semaphore()
    for n in range(slabs - 1):
        pl.semaphore_signal(barrier, inc=1, device_id={"grp": rec_peer(n)}, device_id_type=MESH)
    for n in range(parts - 1):
        pl.semaphore_signal(barrier, inc=1, device_id={"blk": blk_peer(n)}, device_id_type=MESH)

    index_tables(slab_ref, local_ref, remote_ref, weight_ref, node_ref, scale_ref, ext_ref)
    load_grad.wait()
    pl.semaphore_wait(barrier, slabs + parts - 2)

    def rec_copy(n):
        return pltpu.make_async_remote_copy(
            out_buf.at[n], in_buf.at[n], rec_send.at[n], rec_recv.at[n],
            device_id={"grp": rec_peer(n)}, device_id_type=MESH,
        )

    own = slabs - 1
    own_copy = pltpu.make_async_copy(out_buf.at[own], in_buf.at[own], rec_recv.at[own])
    wide = 1024

    def gather(n, _):
        s = rec_peer(n)
        node = node_ref[s]
        total = jnp.zeros((cap, width), F32)
        for k in range(nodes // wide):
            pieces = [
                jnp.where(node == iota((1, 128), 1) + (k * wide + j * 128), 1.0, 0.0).astype(BF16)
                for j in range(wide // 128)
            ]
            total += jnp.dot(
                jnp.concatenate(pieces, axis=1), grad_ref[k * wide : (k + 1) * wide], preferred_element_type=F32
            )
        scale = scale_ref[s]
        out_buf[n, :cap] = (total * jnp.concatenate([scale, scale], axis=1)).astype(BF16)
        out_buf[n, cap:] = ext_ref[s]

        @pl.when(n < own)
        def _():
            rec_copy(n).start()

        return 0

    lax.fori_loop(0, slabs, gather, 0)
    own_copy.start()
    acc_ref[...] = grad_ref[...].astype(F32)
    own_copy.wait()

    tall = 1024

    def scatter(m, _):
        n = (m + own) % slabs

        @pl.when(m > 0)
        def _():
            rec_copy(n).wait_recv()

        ext = in_buf[n, cap:].astype(F32)
        lane = lambda q: jnp.concatenate([ext[q : q + 1], ext[q + 1 : q + 2]], axis=1).astype(jnp.int32)
        high, low = lane(0), lane(2)
        base = jnp.where(iota((256, cap), 0) == low, 1.0, 0.0).astype(BF16).reshape(16, 16, cap)
        block = in_buf[n, :cap]
        for i in range(nodes // tall):
            pieces = []
            for c in range(i * tall // 256, (i + 1) * tall // 256):
                mask = jnp.where(jnp.broadcast_to(high, (16, cap)) == c, 1.0, 0.0).astype(BF16)
                pieces.append((base * mask[None]).reshape(256, cap))
            at = slice(i * tall, (i + 1) * tall)
            acc_ref[at] += jnp.dot(jnp.concatenate(pieces, axis=0), block, preferred_element_type=F32)
        return 0

    lax.fori_loop(0, slabs, scatter, 0)

    load_pre.wait()
    upd_ref[...] = jnp.zeros_like(upd_ref)

    def finish(i, _):
        at = pl.ds(pl.multiple_of(i * 256, 256), 256)
        gradh = acc_ref[at].astype(BF16)
        grad_ref[at] = gradh
        pre = pre_ref[at].astype(F32)
        sig = 1.0 / (1.0 + jnp.exp(-pre))
        act = (pre * sig).astype(BF16)
        slope = sig * (1.0 + pre * (1.0 - sig))
        back = lax.dot_general(gradh, w_ref[...], NT, preferred_element_type=F32)
        gp_ref[pl.ds(i * 2, 2)] = (back * slope).astype(BF16).reshape(2, 128, width)
        upd_ref[...] += lax.dot_general(act, gradh, TN, preferred_element_type=F32)
        return 0

    lax.fori_loop(0, nodes // 256, finish, 0)
    load_feats.start()
    store_gradh = pltpu.make_async_copy(grad_ref, gradh_hbm, store_sem.at[0])
    store_gradh.start()

    def pack(to_ref, at, c):
        def one(t, _):
            to_ref[at + t] = gp_ref[picks_ref[c, b, t]]
            return 0

        lax.fori_loop(0, picks, one, 0)

    sends = []
    for n in range(parts - 1):
        pack(stage_ref.at[n], 0, blk_peer(n))
        copy = pltpu.make_async_remote_copy(
            stage_ref.at[n], got_ref.at[pl.ds(b * picks, picks)], blk_send.at[n], blk_recv.at[n],
            device_id={"blk": blk_peer(n)}, device_id_type=MESH,
        )
        copy.start()
        sends.append(copy)
    pack(got_ref, b * picks, b)

    column_order(cols_ref, order_ref)
    to_smem = pltpu.make_async_copy(order_ref, order_smem, store_sem.at[1])
    to_smem.start()
    load_tiles.wait()
    tiles = parts * picks

    def turn(k, _):
        tiles_ref[k] = jnp.transpose(tiles_ref[k])
        return 0

    lax.fori_loop(0, tiles, turn, 0)
    load_feats.wait()

    def turn_feats(k, _):
        at = pl.ds(pl.multiple_of(k * 256, 256), 256)
        turned_ref[k] = jnp.transpose(pre_ref[at])
        return 0

    lax.fori_loop(0, nodes // 256, turn_feats, 0)
    to_smem.wait()
    lax.fori_loop(0, slabs - 1, lambda n, x: (rec_copy(n).wait_send(), x)[1], 0)
    store_gradh.wait()
    for copy in sends:
        copy.wait()

    group = 8

    def products(m, total):
        for q in range(group):
            k = m * group + q
            f = lax.clamp(0, order_smem[0, k], tiles - 1)
            part = jnp.dot(tiles_ref[f], got_ref[f], preferred_element_type=F32)
            total = total * order_smem[1, k].astype(F32) + part
            run_ref[k] = total.astype(BF16)
        return total

    lax.fori_loop(0, tiles // group, products, jnp.zeros((128, width), F32))

    def settle(j, _):
        last = run_ref[lax.clamp(0, order_smem[2, j], tiles - 1)]
        gp_ref[j] = (last.astype(F32) * order_smem[3, j].astype(F32)).astype(BF16)
        return 0

    lax.fori_loop(0, nodes // 128, settle, 0)
    store_spread = pltpu.make_async_copy(gp_ref, spread_hbm, store_sem.at[2])
    store_spread.start()
    msg = jnp.zeros((width, width), F32)
    for k in range(nodes // 256):
        msg += jnp.dot(turned_ref[k], gp_ref[2 * k : 2 * k + 2].reshape(256, width), preferred_element_type=F32)
    msg_ref[...] = msg
    begin, end = sum_stages(parts, slabs, factor, (msg_ref, upd_ref), (out_msg_ref, out_upd_ref), scratch)
    end(begin())
    store_spread.wait()


def main_step(picks, slab, local, remote, weight, cols, w_update, grad, pre, feats, tiles, slabs, parts, cap, factor):
    nodes, width = grad.shape
    count = picks.shape[-1]
    vmem = pl.BlockSpec(memory_space=pltpu.VMEM)
    hbm = pl.BlockSpec(memory_space=pl.ANY)
    dma = pltpu.SemaphoreType.DMA
    panels = jax.ShapeDtypeStruct((nodes // 128, 128, width), BF16)
    square = jax.ShapeDtypeStruct((width, width), F32)
    return pl.pallas_call(
        functools.partial(main_kernel, parts, slabs, factor),
        out_shape=[jax.ShapeDtypeStruct((nodes, width), BF16), panels, square, square],
        in_specs=[pl.BlockSpec(memory_space=pltpu.SMEM)] + [vmem] * 6 + [hbm] * 4,
        out_specs=[hbm, hbm, vmem, vmem],
        scratch_shapes=[
            pltpu.VMEM((slabs, cap, 128), jnp.int32),
            pltpu.VMEM((slabs, cap, 128), F32),
            pltpu.VMEM((slabs, EXT, width), BF16),
            pltpu.VMEM((slabs, cap + EXT, width), BF16),
            pltpu.VMEM((slabs, cap + EXT, width), BF16),
            pltpu.VMEM((nodes, width), BF16),
            pltpu.VMEM((nodes, width), BF16),
            pltpu.VMEM((nodes, width), F32),
            pltpu.VMEM((nodes // 128, 128, width), BF16),
            pltpu.VMEM((parts - 1, count, 128, width), BF16),
            pltpu.VMEM((parts * count, 128, width), BF16),
            pltpu.VMEM((parts * count, 128, 128), BF16),
            pltpu.VMEM((parts * count, 128, width), BF16),
            pltpu.VMEM((nodes // 256, width, 256), BF16),
            pltpu.VMEM((8, parts * count), jnp.int32),
            pltpu.SMEM((8, parts * count), jnp.int32),
            pltpu.VMEM((width, width), F32),
            pltpu.VMEM((width, width), F32),
            dma((4,)), dma((slabs - 1,)), dma((slabs,)), dma((parts - 1,)), dma((parts - 1,)), dma((3,)),
        ]
        + sum_scratch(parts, slabs, width),
        compiler_params=pltpu.CompilerParams(collective_id=0, has_side_effects=True, vmem_limit_bytes=VMEM_LIMIT),
        name="main_step",
    )(picks, slab, local, remote, weight, cols, w_update, grad, pre, feats, tiles)


def final_kernel(gradh_ref, spread_ref, w_ref, msg_ref, upd_ref, out_ref, out_msg_ref, out_upd_ref):
    down = lax.dot_general(spread_ref[...], w_ref[...], NT, preferred_element_type=F32)
    out_ref[...] = (gradh_ref[...].astype(F32) + down).astype(BF16)

    @pl.when(pl.program_id(0) == 0)
    def _():
        out_msg_ref[...] = msg_ref[...]
        out_upd_ref[...] = upd_ref[...]


def final_step(gradh, spread, w_message, msg, upd):
    rows, width = gradh.shape
    tall = rows // 4
    tile = pl.BlockSpec((tall, width), lambda i: (i, 0))
    square = pl.BlockSpec((width, width), lambda i: (0, 0))
    return pl.pallas_call(
        final_kernel,
        grid=(rows // tall,),
        out_shape=[jax.ShapeDtypeStruct(gradh.shape, BF16)] + [jax.ShapeDtypeStruct(msg.shape, F32)] * 2,
        in_specs=[tile, tile, square, square, square],
        out_specs=[tile, square, square],
        compiler_params=pltpu.CompilerParams(vmem_limit_bytes=VMEM_LIMIT),
        name="final_step",
    )(gradh, spread, w_message, msg, upd)


def local(
    grad_out, pre_act, node_feats, w_message, w_update, tile_vals, tile_rows, tile_cols,
    rec_slab, rec_local, rec_remote, rec_weight,
):
    grad = grad_out[0]
    rows, width = grad.shape
    slabs = lax.axis_size("grp")
    parts = lax.axis_size("blk")
    records = rec_local.shape[1]
    cap = 2 * records // slabs
    factor = float((slabs * parts * rows) ** -0.5)
    lanes = lambda a: a.reshape(records // 128, 128)
    tiles = tile_vals[0, 0]
    count = tiles.shape[0] * tiles.shape[1]
    gradh, spread, msg, upd = main_step(
        tile_rows[0], lanes(rec_slab), lanes(rec_local), lanes(rec_remote), lanes(rec_weight),
        tile_cols[0, 0].reshape(1, count), w_update, grad, pre_act[0], node_feats[0],
        tiles.reshape(count, *tiles.shape[2:]), slabs, parts, cap, factor,
    )
    feats, msg, upd = final_step(gradh, spread.reshape(rows, width), w_message, msg, upd)
    return (feats[None], msg, upd)


def solution(mesh):
    placed = (
        P("grp", "blk", None),
        P("grp", "blk", None),
        P("grp", "blk", None),
        P(),
        P(),
        P("grp", "blk", None, None, None, None),
        P("grp", None, None, None),
        P("grp", "blk", None, None),
        P("grp", "blk", None),
        P("grp", "blk"),
        P("grp", "blk"),
        P("grp", "blk"),
    )
    return jax.shard_map(
        local,
        mesh=mesh,
        in_specs=placed,
        out_specs=(P("grp", "blk", None), P(), P()),
        check_vma=False,
    )
```

```python
import functools

import jax
import jax.numpy as jnp
from jax import lax
from jax.experimental import pallas as pl
from jax.experimental.pallas import tpu as pltpu
from jax.sharding import PartitionSpec as P

F32 = jnp.float32
BF16 = jnp.bfloat16
MESH = pl.DeviceIdType.MESH
NT = (((1,), (1,)), ((), ()))
TN = (((0,), (0,)), ((), ()))
EXT = 16
VMEM_LIMIT = 61 * 1024 * 1024


def iota(shape, dim):
    return lax.broadcasted_iota(jnp.int32, shape, dim)


def index_tables(slab_ref, local_ref, remote_ref, weight_ref, node_ref, scale_ref, ext_ref):
    slabs, cap = node_ref.shape[0], node_ref.shape[1]
    chunks = slab_ref.shape[0]
    slab = slab_ref[...]
    ids = iota((chunks, slabs, 128), 1)
    choose = jnp.where(ids == slab[:, None, :], 1.0, 0.0)
    flat = choose.reshape(chunks * slabs, 128)
    flat16 = flat.astype(BF16)
    upper = jnp.where(iota((128, 128), 0) < iota((128, 128), 1), 1.0, 0.0).astype(BF16)
    prefix = jnp.dot(flat16, upper, preferred_element_type=F32)
    totals = jnp.dot(flat16, jnp.ones((128, 128), BF16), preferred_element_type=F32)
    size = chunks * slabs
    row, col = iota((size, size), 0), iota((size, size), 1)
    earlier = (col < row) & (lax.rem(col, slabs) == lax.rem(row, slabs))
    offset = jnp.dot(jnp.where(earlier, 1.0, 0.0).astype(BF16), totals.astype(BF16), preferred_element_type=F32)
    place = ((prefix + offset) * flat).reshape(chunks, slabs, 128).sum(axis=1).astype(jnp.int32)
    remote, local, weight = remote_ref[...], local_ref[...], weight_ref[...]
    first = weight.astype(BF16).astype(F32)
    second = (weight - first).astype(BF16).astype(F32)
    third = weight - first - second
    values = [
        (remote // 256).astype(F32),
        (remote % 256).astype(F32),
        (local // 64).astype(F32),
        (local % 64).astype(F32),
        first,
        second,
        third,
        jnp.ones_like(weight),
    ]
    table = jnp.zeros((len(values) * slabs, cap), F32)
    for c in range(chunks):
        left = jnp.concatenate([choose[c] * v[c : c + 1] for v in values], axis=0).astype(BF16)
        right = jnp.where(iota((cap, 128), 0) == place[c : c + 1], 1.0, 0.0).astype(BF16)
        table += lax.dot_general(left, right, NT, preferred_element_type=F32)
    valid = table[7 * slabs : 8 * slabs]
    upper_part = jnp.where(valid > 0.5, table[:slabs], 64.0)
    lower_part = table[slabs : 2 * slabs]
    half = cap // 2
    for s in range(slabs):
        rows = [part[s : s + 1, q * half : (q + 1) * half] for part in (upper_part, lower_part) for q in range(2)]
        block = jnp.concatenate(rows + [jnp.zeros((EXT - 4, half), F32)], axis=0)
        ext_ref[s] = block.astype(BF16)
    turned = jnp.transpose(table)
    for s in range(slabs):
        at = lambda v: turned[:, v * slabs + s : v * slabs + s + 1]
        node_ref[s] = jnp.broadcast_to((at(2) * 64.0 + at(3)).astype(jnp.int32), (cap, 128))
        scale_ref[s] = jnp.broadcast_to(at(4) + at(5) + at(6), (cap, 128))


def sum_scratch(parts, slabs, width):
    rows = width // parts
    dma = pltpu.SemaphoreType.DMA
    return [
        pltpu.VMEM((parts, rows, width), F32),
        pltpu.VMEM((parts - 1, rows, width), F32),
        pltpu.VMEM((slabs, 8, 128), F32),
        pltpu.VMEM((slabs - 1, 8, 128), F32),
        pltpu.VMEM((8, 128), F32),
        pltpu.VMEM((slabs, 8, 128), F32),
        pltpu.VMEM((rows, width), F32),
        pltpu.VMEM((parts, rows, width), F32),
        dma((parts - 1,)), dma((parts - 1,)),
        dma((slabs - 1,)), dma((slabs - 1,)),
        dma((slabs - 1,)), dma((slabs - 1,)),
        dma((parts - 1,)), dma((parts - 1,)),
    ]


def sum_stages(parts, slabs, factor, term_ref, out_ref, scratch):
    mine, in1, mid, in2, part, all2, done, all1, s1, r1, s2, r2, s3, r3, s4, r4 = scratch
    b, g = lax.axis_index("blk"), lax.axis_index("grp")
    rows = mine.shape[1]
    high = rows * 2 // slabs
    spots = [(slice(n // 2 * high, (n // 2 + 1) * high), slice(n % 2 * 128, n % 2 * 128 + 128)) for n in range(slabs)]
    flights = []

    def exchange(n, axis, me, src, dst, send, recv):
        copies = []
        for k in range(1, n):
            peer = lax.rem(me + k, n)
            copy = pltpu.make_async_remote_copy(
                src(peer), dst(k), send.at[k - 1], recv.at[k - 1], device_id={axis: peer}, device_id_type=MESH
            )
            copy.start()
            copies.append(copy)
        flights.append(copies)

    def landed():
        for copy in flights[-1]:
            copy.wait_recv()

    def split_blk():
        mid[...] = jnp.zeros_like(mid)
        for k in range(parts):
            mine[k] = term_ref[k * rows : (k + 1) * rows]
        exchange(parts, "blk", b, lambda p: mine.at[p], lambda k: in1.at[k - 1], s1, r1)

    def split_grp():
        landed()
        total = mine[b]
        for k in range(parts - 1):
            total += in1[k]
        for n in range(slabs):
            mid[n, :high] = total[spots[n]]
        exchange(slabs, "grp", g, lambda p: mid.at[p], lambda k: in2.at[k - 1], s2, r2)

    def join_grp():
        landed()
        piece = mid[g]
        for k in range(slabs - 1):
            piece += in2[k]
        part[...] = piece * factor
        all2[g] = piece * factor
        exchange(slabs, "grp", g, lambda p: part, lambda k: all2.at[g], s3, r3)

    def join_blk():
        landed()
        for n in range(slabs):
            done[spots[n]] = all2[n, :high]
        all1[b] = done[...]
        exchange(parts, "blk", b, lambda p: done, lambda k: all1.at[b], s4, r4)

    def finish():
        landed()
        for k in range(parts):
            out_ref[k * rows : (k + 1) * rows] = all1[k]
        for copies in flights:
            for copy in copies:
                copy.wait_send()

    return split_blk, split_grp, join_grp, join_blk, finish


def column_order(cols_ref, order_ref):
    parts, picks = cols_ref.shape
    count = parts * picks
    repeat = jnp.where(iota((picks, count), 1) % picks == iota((picks, count), 0), 1.0, 0.0).astype(BF16)
    wide = jnp.dot(cols_ref[...].astype(F32).astype(BF16), repeat, preferred_element_type=F32)
    own = jnp.where(iota((parts, count), 1) // picks == iota((parts, count), 0), wide, 0.0)
    cols = jnp.broadcast_to(jnp.sum(own, axis=0, keepdims=True), (count, count))
    across, down = iota((count, count), 1).astype(F32), iota((count, count), 0).astype(F32)
    turned = jnp.transpose(cols)
    ones = lambda hit: jnp.where(hit, 1.0, 0.0)
    total = lambda x: jnp.sum(x, axis=0, keepdims=True)
    rank = total(ones(turned * count + down < cols * count + across))
    ranks = jnp.transpose(jnp.broadcast_to(rank, (count, count)))
    hit = ones(ranks == across)
    order = total(hit * down)
    here = total(hit * turned)
    before = total(ones(ranks == across - 1.0) * (turned + 1.0)) - 1.0
    last = jnp.maximum(total(ones(turned <= across)) - 1.0, 0.0)
    named = jnp.minimum(total(ones(turned == across)), 1.0)
    rows = [order, ones(here == before), last, named, jnp.zeros((4, count), F32)]
    order_ref[...] = jnp.concatenate(rows, axis=0).astype(jnp.int32)


FAR = ((2, 1), (1, 1), (3, 1), (0, 1), (2, 0), (1, 0), (3, 0))


def main_kernel(
    parts, slabs, factor,
    picks_ref, slab_ref, local_ref, remote_ref, weight_ref, cols_ref, w_ref, grad_hbm, pre_hbm, feats_hbm, tiles_hbm,
    gradh_hbm, spread_hbm, out_msg_ref, out_upd_ref,
    node_ref, scale_ref, ext_ref, out_buf, in_buf, grad_ref, pre_ref, acc_ref, gp_ref, stage_ref, got_ref,
    tiles_ref, run_ref, turned_ref, order_ref, order_smem, msg_ref, upd_ref,
    load_sem, rec_send, rec_recv, blk_send, blk_recv, store_sem, *scratch,
):
    b, g = lax.axis_index("blk"), lax.axis_index("grp")
    y, xh = b // 2, b % 2
    xl, z, core = g // 8, (g // 2) % 4, g % 2
    cap = node_ref.shape[1]
    nodes, width = acc_ref.shape
    picks = stage_ref.shape[1]

    load_grad = pltpu.make_async_copy(grad_hbm, grad_ref, load_sem.at[0])
    load_pre = pltpu.make_async_copy(pre_hbm, pre_ref, load_sem.at[1])
    load_tiles = pltpu.make_async_copy(tiles_hbm, tiles_ref, load_sem.at[2])
    load_feats = pltpu.make_async_copy(feats_hbm, pre_ref, load_sem.at[3])
    load_grad.start()
    load_pre.start()
    load_tiles.start()

    def rec_peer(n):
        q = n // 4
        dz, dx, dc = (n % 4 + 1) % 4, 1 - n // 8, (q + q // 2) % 2
        return ((xl + dx) % 2 * 4 + (z + dz) % 4) * 2 + (core + dc) % 2

    def blk_peer(n):
        dy, dx = FAR[n]
        return (y + dy) % 4 * 2 + (xh + dx) % 2

    barrier = pltpu.get_barrier_semaphore()
    for n in range(slabs - 1):
        pl.semaphore_signal(barrier, inc=1, device_id={"grp": rec_peer(n)}, device_id_type=MESH)
    for n in range(parts - 1):
        pl.semaphore_signal(barrier, inc=1, device_id={"blk": blk_peer(n)}, device_id_type=MESH)

    index_tables(slab_ref, local_ref, remote_ref, weight_ref, node_ref, scale_ref, ext_ref)
    load_grad.wait()
    pl.semaphore_wait(barrier, slabs + parts - 2)

    def rec_copy(n):
        return pltpu.make_async_remote_copy(
            out_buf.at[n], in_buf.at[n], rec_send.at[n], rec_recv.at[n],
            device_id={"grp": rec_peer(n)}, device_id_type=MESH,
        )

    own = slabs - 1
    own_copy = pltpu.make_async_copy(out_buf.at[own], in_buf.at[own], rec_recv.at[own])
    wide = 1024

    def gather(n, _):
        s = rec_peer(n)
        node = node_ref[s]
        total = jnp.zeros((cap, width), F32)
        for k in range(nodes // wide):
            pieces = [
                jnp.where(node == iota((1, 128), 1) + (k * wide + j * 128), 1.0, 0.0).astype(BF16)
                for j in range(wide // 128)
            ]
            total += jnp.dot(
                jnp.concatenate(pieces, axis=1), grad_ref[k * wide : (k + 1) * wide], preferred_element_type=F32
            )
        scale = scale_ref[s]
        out_buf[n, :cap] = (total * jnp.concatenate([scale, scale], axis=1)).astype(BF16)
        out_buf[n, cap:] = ext_ref[s]

        @pl.when(n < own)
        def _():
            rec_copy(n).start()

        return 0

    lax.fori_loop(0, slabs, gather, 0)
    own_copy.start()
    acc_ref[...] = grad_ref[...].astype(F32)
    own_copy.wait()

    tall = 1024

    def scatter(m, _):
        n = (m + own) % slabs

        @pl.when(m > 0)
        def _():
            rec_copy(n).wait_recv()

        ext = in_buf[n, cap:].astype(F32)
        lane = lambda q: jnp.concatenate([ext[q : q + 1], ext[q + 1 : q + 2]], axis=1).astype(jnp.int32)
        high, low = lane(0), lane(2)
        base = jnp.where(iota((256, cap), 0) == low, 1.0, 0.0).astype(BF16).reshape(16, 16, cap)
        block = in_buf[n, :cap]
        for i in range(nodes // tall):
            pieces = []
            for c in range(i * tall // 256, (i + 1) * tall // 256):
                mask = jnp.where(jnp.broadcast_to(high, (16, cap)) == c, 1.0, 0.0).astype(BF16)
                pieces.append((base * mask[None]).reshape(256, cap))
            at = slice(i * tall, (i + 1) * tall)
            acc_ref[at] += jnp.dot(jnp.concatenate(pieces, axis=0), block, preferred_element_type=F32)
        return 0

    lax.fori_loop(0, slabs, scatter, 0)

    load_pre.wait()
    upd_ref[...] = jnp.zeros_like(upd_ref)

    def finish(i, _):
        at = pl.ds(pl.multiple_of(i * 256, 256), 256)
        gradh = acc_ref[at].astype(BF16)
        grad_ref[at] = gradh
        pre = pre_ref[at].astype(F32)
        sig = 1.0 / (1.0 + jnp.exp(-pre))
        act = (pre * sig).astype(BF16)
        slope = sig * (1.0 + pre * (1.0 - sig))
        back = lax.dot_general(gradh, w_ref[...], NT, preferred_element_type=F32)
        gp_ref[pl.ds(i * 2, 2)] = (back * slope).astype(BF16).reshape(2, 128, width)
        upd_ref[...] += lax.dot_general(act, gradh, TN, preferred_element_type=F32)
        return 0

    lax.fori_loop(0, nodes // 256, finish, 0)
    load_feats.start()
    store_gradh = pltpu.make_async_copy(grad_ref, gradh_hbm, store_sem.at[0])
    store_gradh.start()

    def pack(to_ref, at, c):
        def one(t, _):
            to_ref[at + t] = gp_ref[picks_ref[c, b, t]]
            return 0

        lax.fori_loop(0, picks, one, 0)

    sends = []
    for n in range(parts - 1):
        pack(stage_ref.at[n], 0, blk_peer(n))
        copy = pltpu.make_async_remote_copy(
            stage_ref.at[n], got_ref.at[pl.ds(b * picks, picks)], blk_send.at[n], blk_recv.at[n],
            device_id={"blk": blk_peer(n)}, device_id_type=MESH,
        )
        copy.start()
        sends.append(copy)
    pack(got_ref, b * picks, b)

    column_order(cols_ref, order_ref)
    to_smem = pltpu.make_async_copy(order_ref, order_smem, store_sem.at[1])
    to_smem.start()
    load_tiles.wait()
    tiles = parts * picks

    def turn(k, _):
        tiles_ref[k] = jnp.transpose(tiles_ref[k])
        return 0

    lax.fori_loop(0, tiles, turn, 0)
    load_feats.wait()

    def turn_feats(k, _):
        at = pl.ds(pl.multiple_of(k * 256, 256), 256)
        turned_ref[k] = jnp.transpose(pre_ref[at])
        return 0

    lax.fori_loop(0, nodes // 256, turn_feats, 0)
    to_smem.wait()
    lax.fori_loop(0, slabs - 1, lambda n, x: (rec_copy(n).wait_send(), x)[1], 0)
    store_gradh.wait()
    for copy in sends:
        copy.wait()

    half = len(scratch) // 2
    upd_sum = sum_stages(parts, slabs, factor, upd_ref, out_upd_ref, scratch[:half])
    msg_sum = sum_stages(parts, slabs, factor, msg_ref, out_msg_ref, scratch[half:])
    upd_sum[0]()
    group = 8

    def products(m, total):
        for q in range(group):
            k = m * group + q
            f = lax.clamp(0, order_smem[0, k], tiles - 1)
            part = jnp.dot(tiles_ref[f], got_ref[f], preferred_element_type=F32)
            total = total * order_smem[1, k].astype(F32) + part
            run_ref[k] = total.astype(BF16)
        return total

    lax.fori_loop(0, tiles // group, products, jnp.zeros((128, width), F32))

    def settle(j, _):
        last = run_ref[lax.clamp(0, order_smem[2, j], tiles - 1)]
        gp_ref[j] = (last.astype(F32) * order_smem[3, j].astype(F32)).astype(BF16)
        return 0

    lax.fori_loop(0, nodes // 128, settle, 0)
    store_spread = pltpu.make_async_copy(gp_ref, spread_hbm, store_sem.at[2])
    store_spread.start()
    upd_sum[1]()
    msg = jnp.zeros((width, width), F32)
    for k in range(nodes // 256):
        msg += jnp.dot(turned_ref[k], gp_ref[2 * k : 2 * k + 2].reshape(256, width), preferred_element_type=F32)
    msg_ref[...] = msg
    msg_sum[0]()
    upd_sum[2]()
    msg_sum[1]()
    upd_sum[3]()
    msg_sum[2]()
    msg_sum[3]()
    upd_sum[4]()
    msg_sum[4]()
    store_spread.wait()


def main_step(picks, slab, local, remote, weight, cols, w_update, grad, pre, feats, tiles, slabs, parts, cap, factor):
    nodes, width = grad.shape
    count = picks.shape[-1]
    vmem = pl.BlockSpec(memory_space=pltpu.VMEM)
    hbm = pl.BlockSpec(memory_space=pl.ANY)
    dma = pltpu.SemaphoreType.DMA
    panels = jax.ShapeDtypeStruct((nodes // 128, 128, width), BF16)
    square = jax.ShapeDtypeStruct((width, width), F32)
    return pl.pallas_call(
        functools.partial(main_kernel, parts, slabs, factor),
        out_shape=[jax.ShapeDtypeStruct((nodes, width), BF16), panels, square, square],
        in_specs=[pl.BlockSpec(memory_space=pltpu.SMEM)] + [vmem] * 6 + [hbm] * 4,
        out_specs=[hbm, hbm, vmem, vmem],
        scratch_shapes=[
            pltpu.VMEM((slabs, cap, 128), jnp.int32),
            pltpu.VMEM((slabs, cap, 128), F32),
            pltpu.VMEM((slabs, EXT, width), BF16),
            pltpu.VMEM((slabs, cap + EXT, width), BF16),
            pltpu.VMEM((slabs, cap + EXT, width), BF16),
            pltpu.VMEM((nodes, width), BF16),
            pltpu.VMEM((nodes, width), BF16),
            pltpu.VMEM((nodes, width), F32),
            pltpu.VMEM((nodes // 128, 128, width), BF16),
            pltpu.VMEM((parts - 1, count, 128, width), BF16),
            pltpu.VMEM((parts * count, 128, width), BF16),
            pltpu.VMEM((parts * count, 128, 128), BF16),
            pltpu.VMEM((parts * count, 128, width), BF16),
            pltpu.VMEM((nodes // 256, width, 256), BF16),
            pltpu.VMEM((8, parts * count), jnp.int32),
            pltpu.SMEM((8, parts * count), jnp.int32),
            pltpu.VMEM((width, width), F32),
            pltpu.VMEM((width, width), F32),
            dma((4,)), dma((slabs - 1,)), dma((slabs,)), dma((parts - 1,)), dma((parts - 1,)), dma((3,)),
        ]
        + sum_scratch(parts, slabs, width) * 2,
        compiler_params=pltpu.CompilerParams(collective_id=0, has_side_effects=True, vmem_limit_bytes=VMEM_LIMIT),
        name="main_step",
    )(picks, slab, local, remote, weight, cols, w_update, grad, pre, feats, tiles)


def final_kernel(gradh_ref, spread_ref, w_ref, msg_ref, upd_ref, out_ref, out_msg_ref, out_upd_ref):
    down = lax.dot_general(spread_ref[...], w_ref[...], NT, preferred_element_type=F32)
    out_ref[...] = (gradh_ref[...].astype(F32) + down).astype(BF16)

    @pl.when(pl.program_id(0) == 0)
    def _():
        out_msg_ref[...] = msg_ref[...]
        out_upd_ref[...] = upd_ref[...]


def final_step(gradh, spread, w_message, msg, upd):
    rows, width = gradh.shape
    tall = rows // 4
    tile = pl.BlockSpec((tall, width), lambda i: (i, 0))
    square = pl.BlockSpec((width, width), lambda i: (0, 0))
    return pl.pallas_call(
        final_kernel,
        grid=(rows // tall,),
        out_shape=[jax.ShapeDtypeStruct(gradh.shape, BF16)] + [jax.ShapeDtypeStruct(msg.shape, F32)] * 2,
        in_specs=[tile, tile, square, square, square],
        out_specs=[tile, square, square],
        compiler_params=pltpu.CompilerParams(vmem_limit_bytes=VMEM_LIMIT),
        name="final_step",
    )(gradh, spread, w_message, msg, upd)


def local(
    grad_out, pre_act, node_feats, w_message, w_update, tile_vals, tile_rows, tile_cols,
    rec_slab, rec_local, rec_remote, rec_weight,
):
    grad = grad_out[0]
    rows, width = grad.shape
    slabs = lax.axis_size("grp")
    parts = lax.axis_size("blk")
    records = rec_local.shape[1]
    cap = 2 * records // slabs
    factor = float((slabs * parts * rows) ** -0.5)
    lanes = lambda a: a.reshape(records // 128, 128)
    tiles = tile_vals[0, 0]
    count = tiles.shape[0] * tiles.shape[1]
    gradh, spread, msg, upd = main_step(
        tile_rows[0], lanes(rec_slab), lanes(rec_local), lanes(rec_remote), lanes(rec_weight),
        tile_cols[0, 0], w_update, grad, pre_act[0], node_feats[0],
        tiles.reshape(count, *tiles.shape[2:]), slabs, parts, cap, factor,
    )
    feats, msg, upd = final_step(gradh, spread.reshape(rows, width), w_message, msg, upd)
    return (feats[None], msg, upd)


def solution(mesh):
    placed = (
        P("grp", "blk", None),
        P("grp", "blk", None),
        P("grp", "blk", None),
        P(),
        P(),
        P("grp", "blk", None, None, None, None),
        P("grp", None, None, None),
        P("grp", "blk", None, None),
        P("grp", "blk", None),
        P("grp", "blk"),
        P("grp", "blk"),
        P("grp", "blk"),
    )
    return jax.shard_map(
        local,
        mesh=mesh,
        in_specs=placed,
        out_specs=(P("grp", "blk", None), P(), P()),
        check_vma=False,
    )
```

```python
import functools

import jax
import jax.numpy as jnp
from jax import lax
from jax.experimental import pallas as pl
from jax.experimental.pallas import tpu as pltpu
from jax.sharding import PartitionSpec as P

F32 = jnp.float32
BF16 = jnp.bfloat16
MESH = pl.DeviceIdType.MESH
NT = (((1,), (1,)), ((), ()))
TN = (((0,), (0,)), ((), ()))
EXT = 16
VMEM_LIMIT = 61 * 1024 * 1024


def iota(shape, dim):
    return lax.broadcasted_iota(jnp.int32, shape, dim)


def index_tables(slab_ref, local_ref, remote_ref, weight_ref, pair_ref, ext_ref):
    slabs, cap = ext_ref.shape[0], pair_ref.shape[0]
    chunks = slab_ref.shape[0]
    slab = slab_ref[...]
    ids = iota((chunks, slabs, 128), 1)
    choose = jnp.where(ids == slab[:, None, :], 1.0, 0.0)
    flat = choose.reshape(chunks * slabs, 128)
    flat16 = flat.astype(BF16)
    upper = jnp.where(iota((128, 128), 0) < iota((128, 128), 1), 1.0, 0.0).astype(BF16)
    prefix = jnp.dot(flat16, upper, preferred_element_type=F32)
    totals = jnp.dot(flat16, jnp.ones((128, 128), BF16), preferred_element_type=F32)
    size = chunks * slabs
    row, col = iota((size, size), 0), iota((size, size), 1)
    earlier = (col < row) & (lax.rem(col, slabs) == lax.rem(row, slabs))
    offset = jnp.dot(jnp.where(earlier, 1.0, 0.0).astype(BF16), totals.astype(BF16), preferred_element_type=F32)
    place = ((prefix + offset) * flat).reshape(chunks, slabs, 128).sum(axis=1).astype(jnp.int32)
    remote, local, weight = remote_ref[...], local_ref[...], weight_ref[...]
    first = weight.astype(BF16).astype(F32)
    second = (weight - first).astype(BF16).astype(F32)
    third = weight - first - second
    values = [
        (remote // 256).astype(F32),
        (remote % 256).astype(F32),
        (local // 64).astype(F32),
        (local % 64).astype(F32),
        first,
        second,
        third,
        jnp.ones_like(weight),
    ]
    table = jnp.zeros((len(values) * slabs, cap), F32)
    for c in range(chunks):
        left = jnp.concatenate([choose[c] * v[c : c + 1] for v in values], axis=0).astype(BF16)
        right = jnp.where(iota((cap, 128), 0) == place[c : c + 1], 1.0, 0.0).astype(BF16)
        table += lax.dot_general(left, right, NT, preferred_element_type=F32)
    valid = table[7 * slabs : 8 * slabs]
    upper_part = jnp.where(valid > 0.5, table[:slabs], 64.0)
    lower_part = table[slabs : 2 * slabs]
    half = cap // 2
    for s in range(slabs):
        rows = [part[s : s + 1, q * half : (q + 1) * half] for part in (upper_part, lower_part) for q in range(2)]
        block = jnp.concatenate(rows + [jnp.zeros((EXT - 4, half), F32)], axis=0)
        ext_ref[s] = block.astype(BF16)
    row = lambda v: table[v * slabs : (v + 1) * slabs]
    node, scale = row(2) * 64.0 + row(3), row(4) + row(5) + row(6)
    empty = jnp.zeros((128 - 2 * slabs, cap), F32)
    pair_ref[...] = jnp.transpose(jnp.concatenate([node, scale, empty], axis=0))


def sum_scratch(parts, slabs, width):
    rows = width // parts
    dma = pltpu.SemaphoreType.DMA
    return [
        pltpu.VMEM((parts, rows, width), F32),
        pltpu.VMEM((parts - 1, rows, width), F32),
        pltpu.VMEM((slabs, 8, 128), F32),
        pltpu.VMEM((slabs - 1, 8, 128), F32),
        pltpu.VMEM((8, 128), F32),
        pltpu.VMEM((slabs, 8, 128), F32),
        pltpu.VMEM((rows, width), F32),
        pltpu.VMEM((parts, rows, width), F32),
        dma((parts - 1,)), dma((parts - 1,)),
        dma((slabs - 1,)), dma((slabs - 1,)),
        dma((slabs - 1,)), dma((slabs - 1,)),
        dma((parts - 1,)), dma((parts - 1,)),
    ]


def sum_stages(parts, slabs, factor, term_ref, out_ref, scratch):
    mine, in1, mid, in2, part, all2, done, all1, s1, r1, s2, r2, s3, r3, s4, r4 = scratch
    b, g = lax.axis_index("blk"), lax.axis_index("grp")
    rows = mine.shape[1]
    high = rows * 2 // slabs
    spots = [(slice(n // 2 * high, (n // 2 + 1) * high), slice(n % 2 * 128, n % 2 * 128 + 128)) for n in range(slabs)]
    flights = []

    def exchange(n, axis, me, src, dst, send, recv):
        copies = []
        for k in range(1, n):
            peer = lax.rem(me + k, n)
            copy = pltpu.make_async_remote_copy(
                src(peer), dst(k), send.at[k - 1], recv.at[k - 1], device_id={axis: peer}, device_id_type=MESH
            )
            copy.start()
            copies.append(copy)
        flights.append(copies)

    def landed():
        for copy in flights[-1]:
            copy.wait_recv()

    def split_blk():
        mid[...] = jnp.zeros_like(mid)
        for k in range(parts):
            mine[k] = term_ref[k * rows : (k + 1) * rows]
        exchange(parts, "blk", b, lambda p: mine.at[p], lambda k: in1.at[k - 1], s1, r1)

    def split_grp():
        landed()
        total = mine[b]
        for k in range(parts - 1):
            total += in1[k]
        for n in range(slabs):
            mid[n, :high] = total[spots[n]]
        exchange(slabs, "grp", g, lambda p: mid.at[p], lambda k: in2.at[k - 1], s2, r2)

    def join_grp():
        landed()
        piece = mid[g]
        for k in range(slabs - 1):
            piece += in2[k]
        part[...] = piece * factor
        all2[g] = piece * factor
        exchange(slabs, "grp", g, lambda p: part, lambda k: all2.at[g], s3, r3)

    def join_blk():
        landed()
        for n in range(slabs):
            done[spots[n]] = all2[n, :high]
        all1[b] = done[...]
        exchange(parts, "blk", b, lambda p: done, lambda k: all1.at[b], s4, r4)

    def finish():
        landed()
        for k in range(parts):
            out_ref[k * rows : (k + 1) * rows] = all1[k]
        for copies in flights:
            for copy in copies:
                copy.wait_send()

    return split_blk, split_grp, join_grp, join_blk, finish


def column_order(cols_ref, order_ref):
    parts, picks = cols_ref.shape
    count = parts * picks
    repeat = jnp.where(iota((picks, count), 1) % picks == iota((picks, count), 0), 1.0, 0.0).astype(BF16)
    wide = jnp.dot(cols_ref[...].astype(F32).astype(BF16), repeat, preferred_element_type=F32)
    own = jnp.where(iota((parts, count), 1) // picks == iota((parts, count), 0), wide, 0.0)
    cols = jnp.broadcast_to(jnp.sum(own, axis=0, keepdims=True), (count, count))
    across, down = iota((count, count), 1).astype(F32), iota((count, count), 0).astype(F32)
    turned = jnp.transpose(cols)
    ones = lambda hit: jnp.where(hit, 1.0, 0.0)
    total = lambda x: jnp.sum(x, axis=0, keepdims=True)
    rank = total(ones(turned * count + down < cols * count + across))
    ranks = jnp.transpose(jnp.broadcast_to(rank, (count, count)))
    hit = ones(ranks == across)
    order = total(hit * down)
    here = total(hit * turned)
    before = total(ones(ranks == across - 1.0) * (turned + 1.0)) - 1.0
    last = jnp.maximum(total(ones(turned <= across)) - 1.0, 0.0)
    named = jnp.minimum(total(ones(turned == across)), 1.0)
    rows = [order, ones(here == before), last, named, jnp.zeros((4, count), F32)]
    order_ref[...] = jnp.concatenate(rows, axis=0).astype(jnp.int32)


SPLIT = 80


def main_kernel(
    parts, slabs, factor,
    picks_ref, slab_ref, local_ref, remote_ref, weight_ref, cols_ref, w_ref, grad_hbm, pre_hbm, feats_hbm, tiles_hbm,
    gradh_hbm, spread_hbm, out_msg_ref, out_upd_ref,
    pair_ref, ext_ref, out_buf, in_buf, grad_ref, pre_ref, acc_ref, gp_ref,
    near_ref, far_ref, side_ref, stage_a, stage_b, got_ref,
    tiles_ref, run_ref, turned_ref, order_ref, order_smem, msg_ref, upd_ref,
    load_sem, rec_send, rec_recv, blk_send, blk_recv, store_sem, *scratch,
):
    b, g = lax.axis_index("blk"), lax.axis_index("grp")
    y, xh = b // 2, b % 2
    xl, z, core = g // 8, (g // 2) % 4, g % 2
    cap = pair_ref.shape[0]
    nodes, width = acc_ref.shape
    picks = stage_a.shape[1]

    load_grad = pltpu.make_async_copy(grad_hbm, grad_ref, load_sem.at[0])
    load_pre = pltpu.make_async_copy(pre_hbm, pre_ref, load_sem.at[1])
    load_tiles = pltpu.make_async_copy(tiles_hbm, tiles_ref, load_sem.at[2])
    load_feats = pltpu.make_async_copy(feats_hbm, pre_ref, load_sem.at[3])
    load_grad.start()
    load_pre.start()
    load_tiles.start()

    def rec_peer(n):
        q = n // 4
        dz, dx, dc = (n % 4 + 1) % 4, 1 - n // 8, (q + q // 2) % 2
        return ((xl + dx) % 2 * 4 + (z + dz) % 4) * 2 + (core + dc) % 2

    ring = parts // 2
    up, down, across, side = [(y + dy) % ring * 2 + (xh + dx) % 2 for dy, dx in ((1, 0), (ring - 1, 0), (2, 0), (0, 1))]

    barrier = pltpu.get_barrier_semaphore()
    for n in range(slabs - 1):
        pl.semaphore_signal(barrier, inc=1, device_id={"grp": rec_peer(n)}, device_id_type=MESH)
    for n in range(parts - 1):
        pl.semaphore_signal(barrier, inc=1, device_id={"blk": lax.rem(b + n + 1, parts)}, device_id_type=MESH)

    index_tables(slab_ref, local_ref, remote_ref, weight_ref, pair_ref, ext_ref)
    load_grad.wait()
    pl.semaphore_wait(barrier, slabs + parts - 2)

    def rec_copy(n):
        return pltpu.make_async_remote_copy(
            out_buf.at[n], in_buf.at[n], rec_send.at[n], rec_recv.at[n],
            device_id={"grp": rec_peer(n)}, device_id_type=MESH,
        )

    own = slabs - 1
    own_copy = pltpu.make_async_copy(out_buf.at[own], in_buf.at[own], rec_recv.at[own])
    wide = 1024

    def gather(n, _):
        s = rec_peer(n)
        lane = iota((cap, 128), 1)
        column = lambda at: jnp.sum(jnp.where(lane == at, pair_ref[...], 0.0), axis=1, keepdims=True)
        node = jnp.broadcast_to(column(s).astype(jnp.int32), (cap, 128))
        total = jnp.zeros((cap, width), F32)
        for k in range(nodes // wide):
            pieces = [
                jnp.where(node == iota((1, 128), 1) + (k * wide + j * 128), 1.0, 0.0).astype(BF16)
                for j in range(wide // 128)
            ]
            total += jnp.dot(
                jnp.concatenate(pieces, axis=1), grad_ref[k * wide : (k + 1) * wide], preferred_element_type=F32
            )
        out_buf[n, :cap] = (total * column(s + slabs)).astype(BF16)
        out_buf[n, cap:] = ext_ref[s]

        @pl.when(n < own)
        def _():
            rec_copy(n).start()

        return 0

    lax.fori_loop(0, slabs, gather, 0)
    own_copy.start()
    acc_ref[...] = grad_ref[...].astype(F32)
    own_copy.wait()

    tall = 1024

    def scatter(m, _):
        n = (m + own) % slabs

        @pl.when(m > 0)
        def _():
            rec_copy(n).wait_recv()

        ext = in_buf[n, cap:].astype(F32)
        lane = lambda q: jnp.concatenate([ext[q : q + 1], ext[q + 1 : q + 2]], axis=1).astype(jnp.int32)
        high, low = lane(0), lane(2)
        base = jnp.where(iota((256, cap), 0) == low, 1.0, 0.0).astype(BF16).reshape(16, 16, cap)
        block = in_buf[n, :cap]
        for i in range(nodes // tall):
            pieces = []
            for c in range(i * tall // 256, (i + 1) * tall // 256):
                mask = jnp.where(jnp.broadcast_to(high, (16, cap)) == c, 1.0, 0.0).astype(BF16)
                pieces.append((base * mask[None]).reshape(256, cap))
            at = slice(i * tall, (i + 1) * tall)
            acc_ref[at] += jnp.dot(jnp.concatenate(pieces, axis=0), block, preferred_element_type=F32)
        return 0

    lax.fori_loop(0, slabs, scatter, 0)

    load_pre.wait()
    upd_ref[...] = jnp.zeros_like(upd_ref)

    def finish(i, _):
        at = pl.ds(pl.multiple_of(i * 256, 256), 256)
        gradh = acc_ref[at].astype(BF16)
        grad_ref[at] = gradh
        pre = pre_ref[at].astype(F32)
        sig = 1.0 / (1.0 + jnp.exp(-pre))
        act = (pre * sig).astype(BF16)
        slope = sig * (1.0 + pre * (1.0 - sig))
        back = lax.dot_general(gradh, w_ref[...], NT, preferred_element_type=F32)
        gp_ref[pl.ds(i * 2, 2)] = (back * slope).astype(BF16).reshape(2, 128, width)
        upd_ref[...] += lax.dot_general(act, gradh, TN, preferred_element_type=F32)
        return 0

    copies = {}

    def send(m, src, dst, peer):
        copies[m] = pltpu.make_async_remote_copy(
            src, dst, blk_send.at[m], blk_recv.at[m], device_id={"blk": peer}, device_id_type=MESH
        )
        copies[m].start()

    panels = nodes // 128
    low, high = pl.ds(0, panels // 2), pl.ds(panels // 2, panels // 2)
    rows_a, rows_b = pl.ds(0, SPLIT), pl.ds(SPLIT, 128 - SPLIT)
    lax.fori_loop(0, nodes // 512, finish, 0)
    send(0, gp_ref.at[low, rows_a], near_ref.at[0, low], up)
    lax.fori_loop(nodes // 512, nodes // 256, finish, 0)
    send(1, gp_ref.at[high, rows_a], near_ref.at[1, high], down)
    send(4, gp_ref.at[:, rows_b], side_ref, side)
    send(2, gp_ref.at[high, rows_a], near_ref.at[0, high], up)
    send(3, gp_ref.at[low, rows_a], near_ref.at[1, low], down)
    load_feats.start()
    store_gradh = pltpu.make_async_copy(grad_ref, gradh_hbm, store_sem.at[0])
    store_gradh.start()

    def pack(store, load, c, r):
        def one(t, _):
            store(t, load(picks_ref[c, r, t]))
            return 0

        lax.fori_loop(0, picks, one, 0)

    def to_stage(ref, n):
        def store(t, value):
            ref[n, t] = value

        return store

    def to_got(r, rows):
        def store(t, value):
            got_ref[r * picks + t, rows] = value

        return store

    top, rest, whole = slice(0, SPLIT), slice(SPLIT, 128), slice(0, 128)
    place = lambda r, rows: got_ref.at[pl.ds(r * picks, picks), rows]
    near = [lambda i: near_ref[0, i], lambda i: near_ref[1, i]]
    pack(to_stage(stage_a, 0), lambda i: gp_ref[i, top], side, b)
    send(5, stage_a.at[0], place(b, rows_a), side)
    copies[0].wait_recv()
    copies[1].wait_recv()
    send(6, near_ref.at[0, low], far_ref.at[low], up)
    send(7, near_ref.at[1, high], far_ref.at[high], down)
    for n, peer in enumerate((up, down, across)):
        pack(to_stage(stage_b, n), lambda i: gp_ref[i, rest], peer, b)
        send(8 + n, stage_b.at[n], place(b, rows_b), peer)
    copies[2].wait_recv()
    copies[3].wait_recv()
    for n, r in enumerate((down, up)):
        pack(to_stage(stage_a, 1 + n), near[n], side, r)
        send(11 + n, stage_a.at[1 + n], place(r, rows_a), side)
    copies[4].wait_recv()
    for n, peer in enumerate((up, down, across)):
        pack(to_stage(stage_b, 3 + n), lambda i: side_ref[i], peer, side)
        send(13 + n, stage_b.at[3 + n], place(side, rows_b), peer)
    pack(to_got(b, whole), lambda i: gp_ref[i], b, b)
    pack(to_got(down, top), near[0], b, down)
    pack(to_got(up, top), near[1], b, up)
    pack(to_got(side, rest), lambda i: side_ref[i], b, side)

    column_order(cols_ref, order_ref)
    to_smem = pltpu.make_async_copy(order_ref, order_smem, store_sem.at[1])
    to_smem.start()
    load_tiles.wait()
    tiles = parts * picks

    def turn(k, _):
        tiles_ref[k] = jnp.transpose(tiles_ref[k])
        return 0

    lax.fori_loop(0, tiles, turn, 0)
    copies[6].wait_recv()
    copies[7].wait_recv()
    pack(to_stage(stage_a, 3), lambda i: far_ref[i], side, across)
    send(16, stage_a.at[3], place(across, rows_a), side)
    pack(to_got(across, top), lambda i: far_ref[i], b, across)
    load_feats.wait()

    def turn_feats(k, _):
        at = pl.ds(pl.multiple_of(k * 256, 256), 256)
        turned_ref[k] = jnp.transpose(pre_ref[at])
        return 0

    lax.fori_loop(0, nodes // 256, turn_feats, 0)
    to_smem.wait()
    lax.fori_loop(0, slabs - 1, lambda n, x: (rec_copy(n).wait_send(), x)[1], 0)
    store_gradh.wait()
    for m in (5, 8, 9, 10, 11, 12, 13, 14, 15, 16):
        copies[m].wait_recv()
    for m in range(len(copies)):
        copies[m].wait_send()

    half = len(scratch) // 2
    upd_sum = sum_stages(parts, slabs, factor, upd_ref, out_upd_ref, scratch[:half])
    msg_sum = sum_stages(parts, slabs, factor, msg_ref, out_msg_ref, scratch[half:])
    upd_sum[0]()
    group = 8

    def products(m, total):
        for q in range(group):
            k = m * group + q
            f = lax.clamp(0, order_smem[0, k], tiles - 1)
            part = jnp.dot(tiles_ref[f], got_ref[f], preferred_element_type=F32)
            total = total * order_smem[1, k].astype(F32) + part
            run_ref[k] = total.astype(BF16)
        return total

    lax.fori_loop(0, tiles // group, products, jnp.zeros((128, width), F32))

    def settle(j, _):
        last = run_ref[lax.clamp(0, order_smem[2, j], tiles - 1)]
        gp_ref[j] = (last.astype(F32) * order_smem[3, j].astype(F32)).astype(BF16)
        return 0

    lax.fori_loop(0, nodes // 128, settle, 0)
    store_spread = pltpu.make_async_copy(gp_ref, spread_hbm, store_sem.at[2])
    store_spread.start()
    upd_sum[1]()
    msg = jnp.zeros((width, width), F32)
    for k in range(nodes // 256):
        msg += jnp.dot(turned_ref[k], gp_ref[2 * k : 2 * k + 2].reshape(256, width), preferred_element_type=F32)
    msg_ref[...] = msg
    msg_sum[0]()
    upd_sum[2]()
    msg_sum[1]()
    upd_sum[3]()
    msg_sum[2]()
    msg_sum[3]()
    upd_sum[4]()
    msg_sum[4]()
    store_spread.wait()


def main_step(picks, slab, local, remote, weight, cols, w_update, grad, pre, feats, tiles, slabs, parts, cap, factor):
    nodes, width = grad.shape
    count = picks.shape[-1]
    vmem = pl.BlockSpec(memory_space=pltpu.VMEM)
    hbm = pl.BlockSpec(memory_space=pl.ANY)
    dma = pltpu.SemaphoreType.DMA
    panels = jax.ShapeDtypeStruct((nodes // 128, 128, width), BF16)
    square = jax.ShapeDtypeStruct((width, width), F32)
    return pl.pallas_call(
        functools.partial(main_kernel, parts, slabs, factor),
        out_shape=[jax.ShapeDtypeStruct((nodes, width), BF16), panels, square, square],
        in_specs=[pl.BlockSpec(memory_space=pltpu.SMEM)] + [vmem] * 6 + [hbm] * 4,
        out_specs=[hbm, hbm, vmem, vmem],
        scratch_shapes=[
            pltpu.VMEM((cap, 128), F32),
            pltpu.VMEM((slabs, EXT, width), BF16),
            pltpu.VMEM((slabs, cap + EXT, width), BF16),
            pltpu.VMEM((slabs, cap + EXT, width), BF16),
            pltpu.VMEM((nodes, width), BF16),
            pltpu.VMEM((nodes, width), BF16),
            pltpu.VMEM((nodes, width), F32),
            pltpu.VMEM((nodes // 128, 128, width), BF16),
            pltpu.VMEM((2, nodes // 128, SPLIT, width), BF16),
            pltpu.VMEM((nodes // 128, SPLIT, width), BF16),
            pltpu.VMEM((nodes // 128, 128 - SPLIT, width), BF16),
            pltpu.VMEM((4, count, SPLIT, width), BF16),
            pltpu.VMEM((6, count, 128 - SPLIT, width), BF16),
            pltpu.VMEM((parts * count, 128, width), BF16),
            pltpu.VMEM((parts * count, 128, 128), BF16),
            pltpu.VMEM((parts * count, 128, width), BF16),
            pltpu.VMEM((nodes // 256, width, 256), BF16),
            pltpu.VMEM((8, parts * count), jnp.int32),
            pltpu.SMEM((8, parts * count), jnp.int32),
            pltpu.VMEM((width, width), F32),
            pltpu.VMEM((width, width), F32),
            dma((4,)), dma((slabs - 1,)), dma((slabs,)), dma((17,)), dma((17,)), dma((3,)),
        ]
        + sum_scratch(parts, slabs, width) * 2,
        compiler_params=pltpu.CompilerParams(collective_id=0, has_side_effects=True, vmem_limit_bytes=VMEM_LIMIT),
        name="main_step",
    )(picks, slab, local, remote, weight, cols, w_update, grad, pre, feats, tiles)


def final_kernel(gradh_ref, spread_ref, w_ref, msg_ref, upd_ref, out_ref, out_msg_ref, out_upd_ref):
    down = lax.dot_general(spread_ref[...], w_ref[...], NT, preferred_element_type=F32)
    out_ref[...] = (gradh_ref[...].astype(F32) + down).astype(BF16)

    @pl.when(pl.program_id(0) == 0)
    def _():
        out_msg_ref[...] = msg_ref[...]
        out_upd_ref[...] = upd_ref[...]


def final_step(gradh, spread, w_message, msg, upd):
    rows, width = gradh.shape
    tall = rows // 4
    tile = pl.BlockSpec((tall, width), lambda i: (i, 0))
    square = pl.BlockSpec((width, width), lambda i: (0, 0))
    return pl.pallas_call(
        final_kernel,
        grid=(rows // tall,),
        out_shape=[jax.ShapeDtypeStruct(gradh.shape, BF16)] + [jax.ShapeDtypeStruct(msg.shape, F32)] * 2,
        in_specs=[tile, tile, square, square, square],
        out_specs=[tile, square, square],
        compiler_params=pltpu.CompilerParams(vmem_limit_bytes=VMEM_LIMIT),
        name="final_step",
    )(gradh, spread, w_message, msg, upd)


def local(
    grad_out, pre_act, node_feats, w_message, w_update, tile_vals, tile_rows, tile_cols,
    rec_slab, rec_local, rec_remote, rec_weight,
):
    grad = grad_out[0]
    rows, width = grad.shape
    slabs = lax.axis_size("grp")
    parts = lax.axis_size("blk")
    records = rec_local.shape[1]
    cap = 2 * records // slabs
    factor = float((slabs * parts * rows) ** -0.5)
    lanes = lambda a: a.reshape(records // 128, 128)
    tiles = tile_vals[0, 0]
    count = tiles.shape[0] * tiles.shape[1]
    gradh, spread, msg, upd = main_step(
        tile_rows[0], lanes(rec_slab), lanes(rec_local), lanes(rec_remote), lanes(rec_weight),
        tile_cols[0, 0], w_update, grad, pre_act[0], node_feats[0],
        tiles.reshape(count, *tiles.shape[2:]), slabs, parts, cap, factor,
    )
    feats, msg, upd = final_step(gradh, spread.reshape(rows, width), w_message, msg, upd)
    return (feats[None], msg, upd)


def solution(mesh):
    placed = (
        P("grp", "blk", None),
        P("grp", "blk", None),
        P("grp", "blk", None),
        P(),
        P(),
        P("grp", "blk", None, None, None, None),
        P("grp", None, None, None),
        P("grp", "blk", None, None),
        P("grp", "blk", None),
        P("grp", "blk"),
        P("grp", "blk"),
        P("grp", "blk"),
    )
    return jax.shard_map(
        local,
        mesh=mesh,
        in_specs=placed,
        out_specs=(P("grp", "blk", None), P(), P()),
        check_vma=False,
    )
```

```python
import functools

import jax
import jax.numpy as jnp
from jax import lax
from jax.experimental import pallas as pl
from jax.experimental.pallas import tpu as pltpu
from jax.sharding import PartitionSpec as P

F32 = jnp.float32
BF16 = jnp.bfloat16
MESH = pl.DeviceIdType.MESH
NT = (((1,), (1,)), ((), ()))
TN = (((0,), (0,)), ((), ()))
EXT = 16
VMEM_LIMIT = 61 * 1024 * 1024


def iota(shape, dim):
    return lax.broadcasted_iota(jnp.int32, shape, dim)


def index_tables(slab_ref, local_ref, remote_ref, weight_ref, pair_ref, ext_ref):
    slabs, cap = ext_ref.shape[0], pair_ref.shape[0]
    chunks = slab_ref.shape[0]
    slab = slab_ref[...]
    ids = iota((chunks, slabs, 128), 1)
    choose = jnp.where(ids == slab[:, None, :], 1.0, 0.0)
    flat = choose.reshape(chunks * slabs, 128)
    flat16 = flat.astype(BF16)
    upper = jnp.where(iota((128, 128), 0) < iota((128, 128), 1), 1.0, 0.0).astype(BF16)
    prefix = jnp.dot(flat16, upper, preferred_element_type=F32)
    totals = jnp.dot(flat16, jnp.ones((128, 128), BF16), preferred_element_type=F32)
    size = chunks * slabs
    row, col = iota((size, size), 0), iota((size, size), 1)
    earlier = (col < row) & (lax.rem(col, slabs) == lax.rem(row, slabs))
    offset = jnp.dot(jnp.where(earlier, 1.0, 0.0).astype(BF16), totals.astype(BF16), preferred_element_type=F32)
    place = ((prefix + offset) * flat).reshape(chunks, slabs, 128).sum(axis=1).astype(jnp.int32)
    remote, local, weight = remote_ref[...], local_ref[...], weight_ref[...]
    first = weight.astype(BF16).astype(F32)
    second = (weight - first).astype(BF16).astype(F32)
    third = weight - first - second
    values = [
        (remote // 256).astype(F32),
        (remote % 256).astype(F32),
        (local // 64).astype(F32),
        (local % 64).astype(F32),
        first,
        second,
        third,
        jnp.ones_like(weight),
    ]
    table = jnp.zeros((len(values) * slabs, cap), F32)
    for c in range(chunks):
        left = jnp.concatenate([choose[c] * v[c : c + 1] for v in values], axis=0).astype(BF16)
        right = jnp.where(iota((cap, 128), 0) == place[c : c + 1], 1.0, 0.0).astype(BF16)
        table += lax.dot_general(left, right, NT, preferred_element_type=F32)
    valid = table[7 * slabs : 8 * slabs]
    upper_part = jnp.where(valid > 0.5, table[:slabs], 64.0)
    lower_part = table[slabs : 2 * slabs]
    half = cap // 2
    for s in range(slabs):
        rows = [part[s : s + 1, q * half : (q + 1) * half] for part in (upper_part, lower_part) for q in range(2)]
        block = jnp.concatenate(rows + [jnp.zeros((EXT - 4, half), F32)], axis=0)
        ext_ref[s] = block.astype(BF16)
    row = lambda v: table[v * slabs : (v + 1) * slabs]
    node, scale = row(2) * 64.0 + row(3), row(4) + row(5) + row(6)
    empty = jnp.zeros((128 - 2 * slabs, cap), F32)
    pair_ref[...] = jnp.transpose(jnp.concatenate([node, scale, empty], axis=0))


def sum_scratch(parts, slabs, width):
    rows = width // parts
    dma = pltpu.SemaphoreType.DMA
    return [
        pltpu.VMEM((parts, rows, width), F32),
        pltpu.VMEM((parts - 1, rows, width), F32),
        pltpu.VMEM((slabs, 8, 128), F32),
        pltpu.VMEM((slabs - 1, 8, 128), F32),
        pltpu.VMEM((8, 128), F32),
        pltpu.VMEM((slabs, 8, 128), F32),
        pltpu.VMEM((rows, width), F32),
        pltpu.VMEM((parts, rows, width), F32),
        dma((parts - 1,)), dma((parts - 1,)),
        dma((slabs - 1,)), dma((slabs - 1,)),
        dma((slabs - 1,)), dma((slabs - 1,)),
        dma((parts - 1,)), dma((parts - 1,)),
    ]


def sum_stages(parts, slabs, factor, term_ref, out_ref, scratch):
    mine, in1, mid, in2, part, all2, done, all1, s1, r1, s2, r2, s3, r3, s4, r4 = scratch
    b, g = lax.axis_index("blk"), lax.axis_index("grp")
    rows = mine.shape[1]
    high = rows * 2 // slabs
    spots = [(slice(n // 2 * high, (n // 2 + 1) * high), slice(n % 2 * 128, n % 2 * 128 + 128)) for n in range(slabs)]
    flights = []

    def exchange(n, axis, me, src, dst, send, recv):
        copies = []
        for k in range(1, n):
            peer = lax.rem(me + k, n)
            copy = pltpu.make_async_remote_copy(
                src(peer), dst(k), send.at[k - 1], recv.at[k - 1], device_id={axis: peer}, device_id_type=MESH
            )
            copy.start()
            copies.append(copy)
        flights.append(copies)

    def landed():
        for copy in flights[-1]:
            copy.wait_recv()

    def split_blk():
        mid[...] = jnp.zeros_like(mid)
        for k in range(parts):
            mine[k] = term_ref[k * rows : (k + 1) * rows]
        exchange(parts, "blk", b, lambda p: mine.at[p], lambda k: in1.at[k - 1], s1, r1)

    def split_grp():
        landed()
        total = mine[b]
        for k in range(parts - 1):
            total += in1[k]
        for n in range(slabs):
            mid[n, :high] = total[spots[n]]
        exchange(slabs, "grp", g, lambda p: mid.at[p], lambda k: in2.at[k - 1], s2, r2)

    def join_grp():
        landed()
        piece = mid[g]
        for k in range(slabs - 1):
            piece += in2[k]
        part[...] = piece * factor
        all2[g] = piece * factor
        exchange(slabs, "grp", g, lambda p: part, lambda k: all2.at[g], s3, r3)

    def join_blk():
        landed()
        for n in range(slabs):
            done[spots[n]] = all2[n, :high]
        all1[b] = done[...]
        exchange(parts, "blk", b, lambda p: done, lambda k: all1.at[b], s4, r4)

    def finish():
        landed()
        for k in range(parts):
            out_ref[k * rows : (k + 1) * rows] = all1[k]
        for copies in flights:
            for copy in copies:
                copy.wait_send()

    return split_blk, split_grp, join_grp, join_blk, finish


def column_order(cols, early, order_ref):
    parts, picks = cols.shape
    count = parts * picks
    repeat = jnp.where(iota((picks, count), 1) % picks == iota((picks, count), 0), 1.0, 0.0).astype(BF16)
    wide = jnp.dot(cols.astype(F32).astype(BF16), repeat, preferred_element_type=F32)
    own = jnp.where(iota((parts, count), 1) // picks == iota((parts, count), 0), wide, 0.0)
    line = jnp.sum(own, axis=0, keepdims=True) + jnp.where(iota((1, count), 1) >= early, 32.0, 0.0)
    cols = jnp.broadcast_to(line, (count, count))
    across, down = iota((count, count), 1).astype(F32), iota((count, count), 0).astype(F32)
    turned = jnp.transpose(cols)
    ones = lambda hit: jnp.where(hit, 1.0, 0.0)
    total = lambda x: jnp.sum(x, axis=0, keepdims=True)
    rank = total(ones(turned * count + down < cols * count + across))
    ranks = jnp.transpose(jnp.broadcast_to(rank, (count, count)))
    hit = ones(ranks == across)
    order = total(hit * down)
    here = total(hit * turned)
    before = total(ones(ranks == across - 1.0) * (turned + 1.0)) - 1.0
    last = jnp.maximum(total(ones(turned <= across)) - 1.0, 0.0)
    named = jnp.minimum(total(ones(turned == across)), 1.0)
    rows = [order, ones(here == before), last, named, jnp.zeros((4, count), F32)]
    order_ref[...] = jnp.concatenate(rows, axis=0).astype(jnp.int32)


SPLIT = 80


def main_kernel(
    parts, slabs, factor,
    picks_ref, slab_ref, local_ref, remote_ref, weight_ref, cols_ref, w_ref, wm_ref, grad_hbm, pre_hbm, feats_hbm, tiles_hbm,
    out_hbm, out_msg_ref, out_upd_ref,
    pair_ref, ext_ref, out_buf, in_buf, grad_ref, pre_ref, acc_ref, slope_ref, gp_ref,
    near_ref, far_ref, side_ref, stage_a, stage_b, early_ref, late_ref,
    tiles_ref, run_ref, turned_ref, order_ref, order_smem, msg_ref, upd_ref,
    load_sem, tile_sem, rec_send, rec_recv, blk_send, blk_recv, store_sem, *scratch,
):
    b, g = lax.axis_index("blk"), lax.axis_index("grp")
    y, xh = b // 2, b % 2
    xl, z, core = g // 8, (g // 2) % 4, g % 2
    cap = pair_ref.shape[0]
    nodes, width = acc_ref.shape
    picks = stage_a.shape[1]

    load_grad = pltpu.make_async_copy(grad_hbm, grad_ref, load_sem.at[0])
    load_pre = pltpu.make_async_copy(pre_hbm, pre_ref, load_sem.at[1])
    load_feats = pltpu.make_async_copy(feats_hbm, pre_ref, load_sem.at[2])
    load_grad.start()
    load_pre.start()

    def rec_peer(n):
        q = n // 4
        dz, dx, dc = (n % 4 + 1) % 4, 1 - n // 8, (q + q // 2) % 2
        return ((xl + dx) % 2 * 4 + (z + dz) % 4) * 2 + (core + dc) % 2

    ring = parts // 2
    spot = lambda dy, dx: (y + dy) % ring * 2 + (xh + dx) % 2
    up, down, across, side = spot(1, 0), spot(ring - 1, 0), spot(2, 0), spot(0, 1)
    owners = (b, down, up, side, across, spot(ring - 1, 1), spot(1, 1), spot(2, 1))
    load_tiles = [
        pltpu.make_async_copy(
            tiles_hbm.at[pl.ds(r * picks, picks)], tiles_ref.at[pl.ds(k * picks, picks)], tile_sem.at[k]
        )
        for k, r in enumerate(owners)
    ]
    for load in load_tiles:
        load.start()

    barrier = pltpu.get_barrier_semaphore()
    for n in range(slabs - 1):
        pl.semaphore_signal(barrier, inc=1, device_id={"grp": rec_peer(n)}, device_id_type=MESH)
    for n in range(parts - 1):
        pl.semaphore_signal(barrier, inc=1, device_id={"blk": lax.rem(b + n + 1, parts)}, device_id_type=MESH)

    index_tables(slab_ref, local_ref, remote_ref, weight_ref, pair_ref, ext_ref)
    load_grad.wait()
    pl.semaphore_wait(barrier, slabs + parts - 2)

    def rec_copy(n):
        return pltpu.make_async_remote_copy(
            out_buf.at[n], in_buf.at[n], rec_send.at[n], rec_recv.at[n],
            device_id={"grp": rec_peer(n)}, device_id_type=MESH,
        )

    own = slabs - 1
    own_copy = pltpu.make_async_copy(out_buf.at[own], in_buf.at[own], rec_recv.at[own])
    wide = 1024

    def gather(n, _):
        s = rec_peer(n)
        lane = iota((cap, 128), 1)
        column = lambda at: jnp.sum(jnp.where(lane == at, pair_ref[...], 0.0), axis=1, keepdims=True)
        node = jnp.broadcast_to(column(s).astype(jnp.int32), (cap, 128))
        total = jnp.zeros((cap, width), F32)
        for k in range(nodes // wide):
            pieces = [
                jnp.where(node == iota((1, 128), 1) + (k * wide + j * 128), 1.0, 0.0).astype(BF16)
                for j in range(wide // 128)
            ]
            total += jnp.dot(
                jnp.concatenate(pieces, axis=1), grad_ref[k * wide : (k + 1) * wide], preferred_element_type=F32
            )
        out_buf[n, :cap] = (total * column(s + slabs)).astype(BF16)
        out_buf[n, cap:] = ext_ref[s]

        @pl.when(n < own)
        def _():
            rec_copy(n).start()

        return 0

    lax.fori_loop(0, slabs, gather, 0)
    own_copy.start()
    acc_ref[...] = grad_ref[...].astype(F32)
    load_pre.wait()

    def slopes(i, _):
        at = pl.ds(pl.multiple_of(i * 256, 256), 256)
        pre = pre_ref[at].astype(F32)
        sig = 1.0 / (1.0 + jnp.exp(-pre))
        slope_ref[at] = sig * (1.0 + pre * (1.0 - sig))
        turned_ref[i] = jnp.transpose((pre * sig).astype(BF16))
        return 0

    lax.fori_loop(0, nodes // 256, slopes, 0)
    load_feats.start()
    own_copy.wait()

    tall = 1024

    def scatter(m, _):
        n = (m + own) % slabs

        @pl.when(m > 0)
        def _():
            rec_copy(n).wait_recv()

        ext = in_buf[n, cap:].astype(F32)
        lane = lambda q: jnp.concatenate([ext[q : q + 1], ext[q + 1 : q + 2]], axis=1).astype(jnp.int32)
        high, low = lane(0), lane(2)
        base = jnp.where(iota((256, cap), 0) == low, 1.0, 0.0).astype(BF16).reshape(16, 16, cap)
        block = in_buf[n, :cap]
        for i in range(nodes // tall):
            pieces = []
            for c in range(i * tall // 256, (i + 1) * tall // 256):
                mask = jnp.where(jnp.broadcast_to(high, (16, cap)) == c, 1.0, 0.0).astype(BF16)
                pieces.append((base * mask[None]).reshape(256, cap))
            at = slice(i * tall, (i + 1) * tall)
            acc_ref[at] += jnp.dot(jnp.concatenate(pieces, axis=0), block, preferred_element_type=F32)
        return 0

    lax.fori_loop(0, slabs, scatter, 0)

    def finish(i, _):
        at = pl.ds(pl.multiple_of(i * 512, 512), 512)
        gradh = acc_ref[at].astype(BF16)
        grad_ref[at] = gradh
        back = lax.dot_general(gradh, w_ref[...], NT, preferred_element_type=F32)
        gp_ref[pl.ds(i * 4, 4)] = (back * slope_ref[at]).astype(BF16).reshape(4, 128, width)
        return 0

    copies = {}

    def send(m, src, dst, peer):
        copies[m] = pltpu.make_async_remote_copy(
            src, dst, blk_send.at[m], blk_recv.at[m], device_id={"blk": peer}, device_id_type=MESH
        )
        copies[m].start()

    panels = nodes // 128
    low, high = pl.ds(0, panels // 2), pl.ds(panels // 2, panels // 2)
    rows_a, rows_b = pl.ds(0, SPLIT), pl.ds(SPLIT, 128 - SPLIT)
    lax.fori_loop(0, nodes // 1024, finish, 0)
    send(0, gp_ref.at[low, rows_a], near_ref.at[0, low], up)
    lax.fori_loop(nodes // 1024, nodes // 512, finish, 0)
    send(1, gp_ref.at[high, rows_a], near_ref.at[1, high], down)
    send(4, gp_ref.at[:, rows_b], side_ref, side)
    send(2, gp_ref.at[high, rows_a], near_ref.at[0, high], up)
    send(3, gp_ref.at[low, rows_a], near_ref.at[1, low], down)
    def pack(store, load, c, r):
        def one(t, _):
            store(t, load(picks_ref[c, r, t]))
            return 0

        lax.fori_loop(0, picks, one, 0)

    def to_stage(ref, n):
        def store(t, value):
            ref[n, t] = value

        return store

    def to_early(slot, rows):
        def store(t, value):
            early_ref[slot * picks + t, rows] = value

        return store

    top, rest, whole = slice(0, SPLIT), slice(SPLIT, 128), slice(0, 128)
    place = lambda ref, slot, rows: ref.at[pl.ds(slot * picks, picks), rows]
    near = [lambda i: near_ref[0, i], lambda i: near_ref[1, i]]
    pack(to_stage(stage_a, 0), lambda i: gp_ref[i, top], side, b)
    send(5, stage_a.at[0], place(early_ref, 3, rows_a), side)
    copies[0].wait_recv()
    copies[1].wait_recv()
    send(6, near_ref.at[0, low], far_ref.at[low], up)
    send(7, near_ref.at[1, high], far_ref.at[high], down)
    for n, peer in enumerate((up, down, across)):
        pack(to_stage(stage_b, n), lambda i: gp_ref[i, rest], peer, b)
        send(8 + n, stage_b.at[n], place(early_ref, (1, 2, 4)[n], rows_b), peer)
    copies[2].wait_recv()
    copies[3].wait_recv()
    for n, r in enumerate((down, up)):
        pack(to_stage(stage_a, 1 + n), near[n], side, r)
        send(11 + n, stage_a.at[1 + n], place(late_ref, n, rows_a), side)
    copies[4].wait_recv()
    for n, peer in enumerate((up, down, across)):
        pack(to_stage(stage_b, 3 + n), lambda i: side_ref[i], peer, side)
        send(13 + n, stage_b.at[3 + n], place(late_ref, n, rows_b), peer)
    pack(to_early(0, whole), lambda i: gp_ref[i], b, b)
    pack(to_early(1, top), near[0], b, down)
    pack(to_early(2, top), near[1], b, up)
    pack(to_early(3, rest), lambda i: side_ref[i], b, side)

    cols = jnp.concatenate([cols_ref[pl.ds(r, 1)] for r in owners], axis=0)
    early = 5 * picks
    column_order(cols, early, order_ref)
    to_smem = pltpu.make_async_copy(order_ref, order_smem, store_sem.at[0])
    to_smem.start()
    for load in load_tiles:
        load.wait()
    tiles = parts * picks

    def turn(k, _):
        tiles_ref[k] = jnp.transpose(tiles_ref[k])
        return 0

    lax.fori_loop(0, tiles, turn, 0)
    copies[6].wait_recv()
    copies[7].wait_recv()
    pack(to_stage(stage_a, 3), lambda i: far_ref[i], side, across)
    send(16, stage_a.at[3], place(late_ref, 2, rows_a), side)
    pack(to_early(4, top), lambda i: far_ref[i], b, across)

    upd_ref[...] = jnp.zeros_like(upd_ref)

    def update(i, _):
        at = pl.ds(pl.multiple_of(i * 256, 256), 256)
        upd_ref[...] += jnp.dot(turned_ref[i], grad_ref[at], preferred_element_type=F32)
        return 0

    lax.fori_loop(0, nodes // 256, update, 0)
    load_feats.wait()

    def turn_feats(k, _):
        at = pl.ds(pl.multiple_of(k * 256, 256), 256)
        turned_ref[k] = jnp.transpose(pre_ref[at])
        return 0

    lax.fori_loop(0, nodes // 256, turn_feats, 0)
    to_smem.wait()
    lax.fori_loop(0, slabs - 1, lambda n, x: (rec_copy(n).wait_send(), x)[1], 0)
    group = 8

    def products(ref, start, size):
        def step(m, total):
            for q in range(group):
                k = m * group + q
                f = lax.clamp(start, order_smem[0, k], start + size - 1)
                part = jnp.dot(tiles_ref[f], ref[f - start], preferred_element_type=F32)
                total = total * order_smem[1, k].astype(F32) + part
                run_ref[k] = total.astype(BF16)
            return total

        lax.fori_loop(start // group, (start + size) // group, step, jnp.zeros((128, width), F32))

    for m in (5, 8, 9, 10):
        copies[m].wait_recv()
    products(early_ref, 0, early)
    for m in (11, 12, 13, 14, 15, 16):
        copies[m].wait_recv()
    half = len(scratch) // 2
    upd_sum = sum_stages(parts, slabs, factor, upd_ref, out_upd_ref, scratch[:half])
    msg_sum = sum_stages(parts, slabs, factor, msg_ref, out_msg_ref, scratch[half:])
    upd_sum[0]()
    products(late_ref, early, tiles - early)
    for m in range(len(copies)):
        copies[m].wait_send()

    def settle(j, _):
        piece = lambda k: run_ref[lax.clamp(0, order_smem[2, k], tiles - 1)].astype(F32) * order_smem[3, k].astype(F32)
        gp_ref[j] = (piece(j) + piece(j + panels)).astype(BF16)
        return 0

    lax.fori_loop(0, panels, settle, 0)
    upd_sum[1]()
    msg = jnp.zeros((width, width), F32)
    for k in range(nodes // 256):
        msg += jnp.dot(turned_ref[k], gp_ref[2 * k : 2 * k + 2].reshape(256, width), preferred_element_type=F32)
    msg_ref[...] = msg
    msg_sum[0]()
    upd_sum[2]()

    def features(i, _):
        at = pl.ds(pl.multiple_of(i * 512, 512), 512)
        spread = gp_ref[pl.ds(i * 4, 4)].reshape(512, width)
        below = lax.dot_general(spread, wm_ref[...], NT, preferred_element_type=F32)
        pre_ref[at] = (grad_ref[at].astype(F32) + below).astype(BF16)
        return 0

    lax.fori_loop(0, nodes // 512, features, 0)
    store_out = pltpu.make_async_copy(pre_ref, out_hbm, store_sem.at[1])
    store_out.start()
    msg_sum[1]()
    upd_sum[3]()
    msg_sum[2]()
    msg_sum[3]()
    upd_sum[4]()
    msg_sum[4]()
    store_out.wait()


def main_step(
    picks, slab, local, remote, weight, cols, w_update, w_message, grad, pre, feats, tiles, slabs, parts, cap, factor
):
    nodes, width = grad.shape
    count = picks.shape[-1]
    panels, early = nodes // 128, 5 * count
    vmem = pl.BlockSpec(memory_space=pltpu.VMEM)
    hbm = pl.BlockSpec(memory_space=pl.ANY)
    dma = pltpu.SemaphoreType.DMA
    square = jax.ShapeDtypeStruct((width, width), F32)
    return pl.pallas_call(
        functools.partial(main_kernel, parts, slabs, factor),
        out_shape=[jax.ShapeDtypeStruct((nodes, width), BF16), square, square],
        in_specs=[pl.BlockSpec(memory_space=pltpu.SMEM)] + [vmem] * 7 + [hbm] * 4,
        out_specs=[hbm, vmem, vmem],
        scratch_shapes=[
            pltpu.VMEM((cap, 128), F32),
            pltpu.VMEM((slabs, EXT, width), BF16),
            pltpu.VMEM((slabs, cap + EXT, width), BF16),
            pltpu.VMEM((slabs, cap + EXT, width), BF16),
            pltpu.VMEM((nodes, width), BF16),
            pltpu.VMEM((nodes, width), BF16),
            pltpu.VMEM((nodes, width), F32),
            pltpu.VMEM((nodes, width), F32),
            pltpu.VMEM((panels, 128, width), BF16),
            pltpu.VMEM((2, panels, SPLIT, width), BF16),
            pltpu.VMEM((panels, SPLIT, width), BF16),
            pltpu.VMEM((panels, 128 - SPLIT, width), BF16),
            pltpu.VMEM((4, count, SPLIT, width), BF16),
            pltpu.VMEM((6, count, 128 - SPLIT, width), BF16),
            pltpu.VMEM((early, 128, width), BF16),
            pltpu.VMEM((parts * count - early, 128, width), BF16),
            pltpu.VMEM((parts * count, 128, 128), BF16),
            pltpu.VMEM((parts * count, 128, width), BF16),
            pltpu.VMEM((nodes // 256, width, 256), BF16),
            pltpu.VMEM((8, parts * count), jnp.int32),
            pltpu.SMEM((8, parts * count), jnp.int32),
            pltpu.VMEM((width, width), F32),
            pltpu.VMEM((width, width), F32),
            dma((3,)), dma((parts,)), dma((slabs - 1,)), dma((slabs,)), dma((17,)), dma((17,)), dma((2,)),
        ]
        + sum_scratch(parts, slabs, width) * 2,
        compiler_params=pltpu.CompilerParams(collective_id=0, has_side_effects=True, vmem_limit_bytes=VMEM_LIMIT),
        name="main_step",
    )(picks, slab, local, remote, weight, cols, w_update, w_message, grad, pre, feats, tiles)


def final_kernel(out_ref, msg_ref, upd_ref, to_out_ref, to_msg_ref, to_upd_ref, sem):
    rows = out_ref.shape[0] // 4
    pairs = [(out_ref.at[pl.ds(k * rows, rows)], to_out_ref.at[pl.ds(k * rows, rows)]) for k in range(4)]
    pairs += [(msg_ref, to_msg_ref), (upd_ref, to_upd_ref)]
    moves = [pltpu.make_async_copy(src, dst, sem.at[k]) for k, (src, dst) in enumerate(pairs)]
    for move in moves:
        move.start()
    for move in moves:
        move.wait()


def final_step(out, msg, upd):
    hbm = pl.BlockSpec(memory_space=pl.ANY)
    args = (out, msg, upd)
    return pl.pallas_call(
        final_kernel,
        out_shape=[jax.ShapeDtypeStruct(a.shape, a.dtype) for a in args],
        in_specs=[hbm] * 3,
        out_specs=[hbm] * 3,
        scratch_shapes=[pltpu.SemaphoreType.DMA((6,))],
        compiler_params=pltpu.CompilerParams(vmem_limit_bytes=VMEM_LIMIT),
        name="final_step",
    )(*args)


def local(
    grad_out, pre_act, node_feats, w_message, w_update, tile_vals, tile_rows, tile_cols,
    rec_slab, rec_local, rec_remote, rec_weight,
):
    grad = grad_out[0]
    rows, width = grad.shape
    slabs = lax.axis_size("grp")
    parts = lax.axis_size("blk")
    records = rec_local.shape[1]
    cap = 2 * records // slabs
    factor = float((slabs * parts * rows) ** -0.5)
    lanes = lambda a: a.reshape(records // 128, 128)
    tiles = tile_vals[0, 0]
    count = tiles.shape[0] * tiles.shape[1]
    out, msg, upd = main_step(
        tile_rows[0], lanes(rec_slab), lanes(rec_local), lanes(rec_remote), lanes(rec_weight),
        tile_cols[0, 0], w_update, w_message, grad, pre_act[0], node_feats[0],
        tiles.reshape(count, *tiles.shape[2:]), slabs, parts, cap, factor,
    )
    feats, msg, upd = final_step(out, msg, upd)
    return (feats[None], msg, upd)


def solution(mesh):
    placed = (
        P("grp", "blk", None),
        P("grp", "blk", None),
        P("grp", "blk", None),
        P(),
        P(),
        P("grp", "blk", None, None, None, None),
        P("grp", None, None, None),
        P("grp", "blk", None, None),
        P("grp", "blk", None),
        P("grp", "blk"),
        P("grp", "blk"),
        P("grp", "blk"),
    )
    return jax.shard_map(
        local,
        mesh=mesh,
        in_specs=placed,
        out_specs=(P("grp", "blk", None), P(), P()),
        check_vma=False,
    )
```

```python
import functools

import jax
import jax.numpy as jnp
from jax import lax
from jax.experimental import pallas as pl
from jax.experimental.pallas import tpu as pltpu
from jax.sharding import PartitionSpec as P

F32 = jnp.float32
BF16 = jnp.bfloat16
MESH = pl.DeviceIdType.MESH
NT = (((1,), (1,)), ((), ()))
TN = (((0,), (0,)), ((), ()))
EXT = 16
VMEM_LIMIT = 61 * 1024 * 1024


def iota(shape, dim):
    return lax.broadcasted_iota(jnp.int32, shape, dim)


def index_tables(slab_ref, local_ref, remote_ref, weight_ref, pair_ref, ext_ref):
    slabs, cap = ext_ref.shape[0], pair_ref.shape[0]
    chunks = slab_ref.shape[0]
    slab = slab_ref[...]
    ids = iota((chunks, slabs, 128), 1)
    choose = jnp.where(ids == slab[:, None, :], 1.0, 0.0)
    flat = choose.reshape(chunks * slabs, 128)
    flat16 = flat.astype(BF16)
    upper = jnp.where(iota((128, 128), 0) < iota((128, 128), 1), 1.0, 0.0).astype(BF16)
    prefix = jnp.dot(flat16, upper, preferred_element_type=F32)
    totals = jnp.dot(flat16, jnp.ones((128, 128), BF16), preferred_element_type=F32)
    size = chunks * slabs
    row, col = iota((size, size), 0), iota((size, size), 1)
    earlier = (col < row) & (lax.rem(col, slabs) == lax.rem(row, slabs))
    offset = jnp.dot(jnp.where(earlier, 1.0, 0.0).astype(BF16), totals.astype(BF16), preferred_element_type=F32)
    place = ((prefix + offset) * flat).reshape(chunks, slabs, 128).sum(axis=1).astype(jnp.int32)
    remote, local, weight = remote_ref[...], local_ref[...], weight_ref[...]
    first = weight.astype(BF16).astype(F32)
    second = (weight - first).astype(BF16).astype(F32)
    third = weight - first - second
    values = [
        (remote // 256).astype(F32),
        (remote % 256).astype(F32),
        (local // 64).astype(F32),
        (local % 64).astype(F32),
        first,
        second,
        third,
        jnp.ones_like(weight),
    ]
    table = jnp.zeros((len(values) * slabs, cap), F32)
    for c in range(chunks):
        left = jnp.concatenate([choose[c] * v[c : c + 1] for v in values], axis=0).astype(BF16)
        right = jnp.where(iota((cap, 128), 0) == place[c : c + 1], 1.0, 0.0).astype(BF16)
        table += lax.dot_general(left, right, NT, preferred_element_type=F32)
    valid = table[7 * slabs : 8 * slabs]
    upper_part = jnp.where(valid > 0.5, table[:slabs], 64.0)
    lower_part = table[slabs : 2 * slabs]
    half = cap // 2
    for s in range(slabs):
        rows = [part[s : s + 1, q * half : (q + 1) * half] for part in (upper_part, lower_part) for q in range(2)]
        block = jnp.concatenate(rows + [jnp.zeros((EXT - 4, half), F32)], axis=0)
        ext_ref[s] = block.astype(BF16)
    row = lambda v: table[v * slabs : (v + 1) * slabs]
    node, scale = row(2) * 64.0 + row(3), row(4) + row(5) + row(6)
    empty = jnp.zeros((128 - 2 * slabs, cap), F32)
    pair_ref[...] = jnp.transpose(jnp.concatenate([node, scale, empty], axis=0))


def sum_scratch(parts, slabs, width):
    rows = width // parts
    dma = pltpu.SemaphoreType.DMA
    return [
        pltpu.VMEM((parts, rows, width), F32),
        pltpu.VMEM((parts - 1, rows, width), F32),
        pltpu.VMEM((slabs, 8, 128), F32),
        pltpu.VMEM((slabs - 1, 8, 128), F32),
        pltpu.VMEM((8, 128), F32),
        pltpu.VMEM((slabs, 8, 128), F32),
        pltpu.VMEM((rows, width), F32),
        pltpu.VMEM((parts, rows, width), F32),
        dma((parts - 1,)), dma((parts - 1,)),
        dma((slabs - 1,)), dma((slabs - 1,)),
        dma((slabs - 1,)), dma((slabs - 1,)),
        dma((parts - 1,)), dma((parts - 1,)),
    ]


def sum_stages(parts, slabs, factor, term_ref, out_ref, scratch):
    mine, in1, mid, in2, part, all2, done, all1, s1, r1, s2, r2, s3, r3, s4, r4 = scratch
    b, g = lax.axis_index("blk"), lax.axis_index("grp")
    rows = mine.shape[1]
    high = rows * 2 // slabs
    spots = [(slice(n // 2 * high, (n // 2 + 1) * high), slice(n % 2 * 128, n % 2 * 128 + 128)) for n in range(slabs)]
    flights = []

    def exchange(n, axis, me, src, dst, send, recv):
        copies = []
        for k in range(1, n):
            peer = lax.rem(me + k, n)
            copy = pltpu.make_async_remote_copy(
                src(peer), dst(k), send.at[k - 1], recv.at[k - 1], device_id={axis: peer}, device_id_type=MESH
            )
            copy.start()
            copies.append(copy)
        flights.append(copies)

    def landed():
        for copy in flights[-1]:
            copy.wait_recv()

    def split_blk():
        mid[...] = jnp.zeros_like(mid)
        for k in range(parts):
            mine[k] = term_ref[k * rows : (k + 1) * rows]
        exchange(parts, "blk", b, lambda p: mine.at[p], lambda k: in1.at[k - 1], s1, r1)

    def split_grp():
        landed()
        total = mine[b]
        for k in range(parts - 1):
            total += in1[k]
        for n in range(slabs):
            mid[n, :high] = total[spots[n]]
        exchange(slabs, "grp", g, lambda p: mid.at[p], lambda k: in2.at[k - 1], s2, r2)

    def join_grp():
        landed()
        piece = mid[g]
        for k in range(slabs - 1):
            piece += in2[k]
        part[...] = piece * factor
        all2[g] = piece * factor
        exchange(slabs, "grp", g, lambda p: part, lambda k: all2.at[g], s3, r3)

    def join_blk():
        landed()
        for n in range(slabs):
            done[spots[n]] = all2[n, :high]
        all1[b] = done[...]
        exchange(parts, "blk", b, lambda p: done, lambda k: all1.at[b], s4, r4)

    def finish():
        landed()
        for k in range(parts):
            out_ref[k * rows : (k + 1) * rows] = all1[k]
        for copies in flights:
            for copy in copies:
                copy.wait_send()

    return split_blk, split_grp, join_grp, join_blk, finish


def column_order(cols, early, order_ref):
    parts, picks = cols.shape
    count = parts * picks
    repeat = jnp.where(iota((picks, count), 1) % picks == iota((picks, count), 0), 1.0, 0.0).astype(BF16)
    wide = jnp.dot(cols.astype(F32).astype(BF16), repeat, preferred_element_type=F32)
    own = jnp.where(iota((parts, count), 1) // picks == iota((parts, count), 0), wide, 0.0)
    line = jnp.sum(own, axis=0, keepdims=True) + jnp.where(iota((1, count), 1) >= early, 32.0, 0.0)
    cols = jnp.broadcast_to(line, (count, count))
    across, down = iota((count, count), 1).astype(F32), iota((count, count), 0).astype(F32)
    turned = jnp.transpose(cols)
    ones = lambda hit: jnp.where(hit, 1.0, 0.0)
    total = lambda x: jnp.sum(x, axis=0, keepdims=True)
    rank = total(ones(turned * count + down < cols * count + across))
    ranks = jnp.transpose(jnp.broadcast_to(rank, (count, count)))
    hit = ones(ranks == across)
    order = total(hit * down)
    here = total(hit * turned)
    before = total(ones(ranks == across - 1.0) * (turned + 1.0)) - 1.0
    last = jnp.maximum(total(ones(turned <= across)) - 1.0, 0.0)
    named = jnp.minimum(total(ones(turned == across)), 1.0)
    rows = [order, ones(here == before), last, named, jnp.zeros((4, count), F32)]
    order_ref[...] = jnp.concatenate(rows, axis=0).astype(jnp.int32)


SPLIT = 80


def main_kernel(
    parts, slabs, factor,
    picks_ref, slab_ref, local_ref, remote_ref, weight_ref, cols_ref, w_ref, wm_ref, grad_hbm, pre_hbm, feats_hbm, tiles_hbm,
    out_hbm, out_msg_ref, out_upd_ref,
    pair_ref, ext_ref, out_buf, in_buf, grad_ref, pre_ref, acc_ref, slope_ref, gp_ref,
    near_ref, far_ref, side_ref, stage_a, stage_b, early_ref, late_ref,
    tiles_ref, run_ref, turned_ref, order_ref, order_smem, msg_ref, upd_ref,
    load_sem, tile_sem, rec_send, rec_recv, blk_send, blk_recv, store_sem, *scratch,
):
    b, g = lax.axis_index("blk"), lax.axis_index("grp")
    y, xh = b // 2, b % 2
    xl, z, core = g // 8, (g // 2) % 4, g % 2
    cap = pair_ref.shape[0]
    nodes, width = acc_ref.shape
    picks = stage_a.shape[1]

    load_grad = pltpu.make_async_copy(grad_hbm, grad_ref, load_sem.at[0])
    load_pre = pltpu.make_async_copy(pre_hbm, pre_ref, load_sem.at[1])
    load_feats = pltpu.make_async_copy(feats_hbm, pre_ref, load_sem.at[2])
    load_grad.start()
    load_pre.start()

    def rec_peer(n):
        q = n // 4
        dz, dx, dc = (n % 4 + 1) % 4, 1 - n // 8, (q + q // 2) % 2
        return ((xl + dx) % 2 * 4 + (z + dz) % 4) * 2 + (core + dc) % 2

    ring = parts // 2
    spot = lambda dy, dx: (y + dy) % ring * 2 + (xh + dx) % 2
    up, down, across, side = spot(1, 0), spot(ring - 1, 0), spot(2, 0), spot(0, 1)
    owners = (b, down, up, side, across, spot(ring - 1, 1), spot(1, 1), spot(2, 1))
    load_tiles = [
        pltpu.make_async_copy(
            tiles_hbm.at[pl.ds(r * picks, picks)], tiles_ref.at[pl.ds(k * picks, picks)], tile_sem.at[k]
        )
        for k, r in enumerate(owners)
    ]
    for load in load_tiles:
        load.start()

    barrier = pltpu.get_barrier_semaphore()
    for n in range(slabs - 1):
        pl.semaphore_signal(barrier, inc=1, device_id={"grp": rec_peer(n)}, device_id_type=MESH)
    for n in range(parts - 1):
        pl.semaphore_signal(barrier, inc=1, device_id={"blk": lax.rem(b + n + 1, parts)}, device_id_type=MESH)

    index_tables(slab_ref, local_ref, remote_ref, weight_ref, pair_ref, ext_ref)
    load_grad.wait()
    pl.semaphore_wait(barrier, slabs + parts - 2)

    def rec_copy(n):
        return pltpu.make_async_remote_copy(
            out_buf.at[n], in_buf.at[n], rec_send.at[n], rec_recv.at[n],
            device_id={"grp": rec_peer(n)}, device_id_type=MESH,
        )

    own = slabs - 1
    own_copy = pltpu.make_async_copy(out_buf.at[own], in_buf.at[own], rec_recv.at[own])
    wide = 1024

    def gather(n, _):
        s = rec_peer(n)
        lane = iota((cap, 128), 1)
        column = lambda at: jnp.sum(jnp.where(lane == at, pair_ref[...], 0.0), axis=1, keepdims=True)
        node = jnp.broadcast_to(column(s).astype(jnp.int32), (cap, 128))
        total = jnp.zeros((cap, width), F32)
        for k in range(nodes // wide):
            pieces = [
                jnp.where(node == iota((1, 128), 1) + (k * wide + j * 128), 1.0, 0.0).astype(BF16)
                for j in range(wide // 128)
            ]
            total += jnp.dot(
                jnp.concatenate(pieces, axis=1), grad_ref[k * wide : (k + 1) * wide], preferred_element_type=F32
            )
        out_buf[n, :cap] = (total * column(s + slabs)).astype(BF16)
        out_buf[n, cap:] = ext_ref[s]

        @pl.when(n < own)
        def _():
            rec_copy(n).start()

        return 0

    lax.fori_loop(0, slabs, gather, 0)
    own_copy.start()
    acc_ref[...] = grad_ref[...].astype(F32)
    load_pre.wait()

    def slopes(i, _):
        at = pl.ds(pl.multiple_of(i * 256, 256), 256)
        pre = pre_ref[at].astype(F32)
        sig = 1.0 / (1.0 + jnp.exp(-pre))
        slope_ref[at] = sig * (1.0 + pre * (1.0 - sig))
        turned_ref[i] = jnp.transpose((pre * sig).astype(BF16))
        return 0

    lax.fori_loop(0, nodes // 256, slopes, 0)
    load_feats.start()
    own_copy.wait()

    tall = 1024

    def scatter(m, _):
        n = (m + own) % slabs

        @pl.when(m > 0)
        def _():
            rec_copy(n).wait_recv()

        ext = in_buf[n, cap:].astype(F32)
        lane = lambda q: jnp.concatenate([ext[q : q + 1], ext[q + 1 : q + 2]], axis=1).astype(jnp.int32)
        high, low = lane(0), lane(2)
        base = jnp.where(iota((256, cap), 0) == low, 1.0, 0.0).astype(BF16).reshape(16, 16, cap)
        block = in_buf[n, :cap]
        for i in range(nodes // tall):
            pieces = []
            for c in range(i * tall // 256, (i + 1) * tall // 256):
                mask = jnp.where(jnp.broadcast_to(high, (16, cap)) == c, 1.0, 0.0).astype(BF16)
                pieces.append((base * mask[None]).reshape(256, cap))
            at = slice(i * tall, (i + 1) * tall)
            acc_ref[at] += jnp.dot(jnp.concatenate(pieces, axis=0), block, preferred_element_type=F32)
        return 0

    lax.fori_loop(0, slabs, scatter, 0)

    def finish(i, _):
        at = pl.ds(pl.multiple_of(i * 512, 512), 512)
        gradh = acc_ref[at].astype(BF16)
        grad_ref[at] = gradh
        back = lax.dot_general(gradh, w_ref[...], NT, preferred_element_type=F32)
        gp_ref[pl.ds(i * 4, 4)] = (back * slope_ref[at]).astype(BF16).reshape(4, 128, width)
        return 0

    copies = {}

    def send(m, src, dst, peer):
        copies[m] = pltpu.make_async_remote_copy(
            src, dst, blk_send.at[m], blk_recv.at[m], device_id={"blk": peer}, device_id_type=MESH
        )
        copies[m].start()

    panels = nodes // 128
    low, high = pl.ds(0, panels // 2), pl.ds(panels // 2, panels // 2)
    rows_a, rows_b = pl.ds(0, SPLIT), pl.ds(SPLIT, 128 - SPLIT)
    lax.fori_loop(0, nodes // 1024, finish, 0)
    send(0, gp_ref.at[low, rows_a], near_ref.at[0, low], up)
    lax.fori_loop(nodes // 1024, nodes // 512, finish, 0)
    send(1, gp_ref.at[high, rows_a], near_ref.at[1, high], down)
    send(4, gp_ref.at[:, rows_b], side_ref, side)
    send(2, gp_ref.at[high, rows_a], near_ref.at[0, high], up)
    send(3, gp_ref.at[low, rows_a], near_ref.at[1, low], down)
    def pack(store, load, c, r):
        def one(t, _):
            store(t, load(picks_ref[c, r, t]))
            return 0

        lax.fori_loop(0, picks, one, 0)

    def to_stage(ref, n):
        def store(t, value):
            ref[n, t] = value

        return store

    def to_early(slot, rows):
        def store(t, value):
            early_ref[slot * picks + t, rows] = value

        return store

    top, rest, whole = slice(0, SPLIT), slice(SPLIT, 128), slice(0, 128)
    place = lambda ref, slot, rows: ref.at[pl.ds(slot * picks, picks), rows]
    near = [lambda i: near_ref[0, i], lambda i: near_ref[1, i]]
    pack(to_stage(stage_a, 0), lambda i: gp_ref[i, top], side, b)
    send(5, stage_a.at[0], place(early_ref, 3, rows_a), side)
    copies[0].wait_recv()
    copies[1].wait_recv()
    send(6, near_ref.at[0, low], far_ref.at[low], up)
    send(7, near_ref.at[1, high], far_ref.at[high], down)
    for n, peer in enumerate((up, down, across)):
        pack(to_stage(stage_b, n), lambda i: gp_ref[i, rest], peer, b)
        send(8 + n, stage_b.at[n], place(early_ref, (1, 2, 4)[n], rows_b), peer)
    copies[2].wait_recv()
    copies[3].wait_recv()
    for n, r in enumerate((down, up)):
        pack(to_stage(stage_a, 1 + n), near[n], side, r)
        send(11 + n, stage_a.at[1 + n], place(late_ref, n, rows_a), side)
    copies[4].wait_recv()
    for n, peer in enumerate((up, down, across)):
        pack(to_stage(stage_b, 3 + n), lambda i: side_ref[i], peer, side)
        send(13 + n, stage_b.at[3 + n], place(late_ref, n, rows_b), peer)
    pack(to_early(0, whole), lambda i: gp_ref[i], b, b)
    pack(to_early(1, top), near[0], b, down)
    pack(to_early(2, top), near[1], b, up)
    pack(to_early(3, rest), lambda i: side_ref[i], b, side)

    cols = jnp.concatenate([cols_ref[pl.ds(r, 1)] for r in owners], axis=0)
    early = 5 * picks
    column_order(cols, early, order_ref)
    to_smem = pltpu.make_async_copy(order_ref, order_smem, store_sem.at[0])
    to_smem.start()
    for load in load_tiles:
        load.wait()
    tiles = parts * picks

    def turn(k, _):
        tiles_ref[k] = jnp.transpose(tiles_ref[k])
        return 0

    lax.fori_loop(0, tiles, turn, 0)
    copies[6].wait_recv()
    copies[7].wait_recv()
    pack(to_stage(stage_a, 3), lambda i: far_ref[i], side, across)
    send(16, stage_a.at[3], place(late_ref, 2, rows_a), side)
    pack(to_early(4, top), lambda i: far_ref[i], b, across)

    upd_ref[...] = jnp.zeros_like(upd_ref)

    def update(i, _):
        at = pl.ds(pl.multiple_of(i * 256, 256), 256)
        upd_ref[...] += jnp.dot(turned_ref[i], grad_ref[at], preferred_element_type=F32)
        return 0

    lax.fori_loop(0, nodes // 256, update, 0)
    load_feats.wait()

    def turn_feats(k, _):
        at = pl.ds(pl.multiple_of(k * 256, 256), 256)
        turned_ref[k] = jnp.transpose(pre_ref[at])
        return 0

    lax.fori_loop(0, nodes // 256, turn_feats, 0)
    to_smem.wait()
    lax.fori_loop(0, slabs - 1, lambda n, x: (rec_copy(n).wait_send(), x)[1], 0)
    group = 8

    def products(ref, start, size):
        def step(m, total):
            for q in range(group):
                k = m * group + q
                f = lax.clamp(start, order_smem[0, k], start + size - 1)
                part = jnp.dot(tiles_ref[f], ref[f - start], preferred_element_type=F32)
                total = total * order_smem[1, k].astype(F32) + part
                run_ref[k] = total.astype(BF16)
            return total

        lax.fori_loop(start // group, (start + size) // group, step, jnp.zeros((128, width), F32))

    for m in (5, 8, 9, 10):
        copies[m].wait_recv()
    products(early_ref, 0, early)
    for m in (11, 12, 13, 14, 15, 16):
        copies[m].wait_recv()
    half = len(scratch) // 2
    upd_sum = sum_stages(parts, slabs, factor, upd_ref, out_upd_ref, scratch[:half])
    msg_sum = sum_stages(parts, slabs, factor, msg_ref, out_msg_ref, scratch[half:])
    upd_sum[0]()
    products(late_ref, early, tiles - early)
    for m in range(len(copies)):
        copies[m].wait_send()

    def settle(j, _):
        piece = lambda k: run_ref[lax.clamp(0, order_smem[2, k], tiles - 1)].astype(F32) * order_smem[3, k].astype(F32)
        gp_ref[j] = (piece(j) + piece(j + panels)).astype(BF16)
        return 0

    lax.fori_loop(0, panels, settle, 0)
    upd_sum[1]()
    msg = jnp.zeros((width, width), F32)
    for k in range(nodes // 256):
        msg += jnp.dot(turned_ref[k], gp_ref[2 * k : 2 * k + 2].reshape(256, width), preferred_element_type=F32)
    msg_ref[...] = msg
    msg_sum[0]()
    upd_sum[2]()

    def features(i, _):
        at = pl.ds(pl.multiple_of(i * 512, 512), 512)
        spread = gp_ref[pl.ds(i * 4, 4)].reshape(512, width)
        below = lax.dot_general(spread, wm_ref[...], NT, preferred_element_type=F32)
        pre_ref[at] = (grad_ref[at].astype(F32) + below).astype(BF16)
        return 0

    lax.fori_loop(0, nodes // 512, features, 0)
    store_out = pltpu.make_async_copy(pre_ref, out_hbm, store_sem.at[1])
    store_out.start()
    msg_sum[1]()
    upd_sum[3]()
    msg_sum[2]()
    msg_sum[3]()
    upd_sum[4]()
    msg_sum[4]()
    store_out.wait()


def main_step(
    picks, slab, local, remote, weight, cols, w_update, w_message, grad, pre, feats, tiles, slabs, parts, cap, factor
):
    nodes, width = grad.shape
    count = picks.shape[-1]
    panels, early = nodes // 128, 5 * count
    vmem = pl.BlockSpec(memory_space=pltpu.VMEM)
    hbm = pl.BlockSpec(memory_space=pl.ANY)
    dma = pltpu.SemaphoreType.DMA
    square = jax.ShapeDtypeStruct((width, width), F32)
    return pl.pallas_call(
        functools.partial(main_kernel, parts, slabs, factor),
        out_shape=[jax.ShapeDtypeStruct((nodes, width), BF16), square, square],
        in_specs=[pl.BlockSpec(memory_space=pltpu.SMEM)] + [vmem] * 7 + [hbm] * 4,
        out_specs=[hbm, vmem, vmem],
        scratch_shapes=[
            pltpu.VMEM((cap, 128), F32),
            pltpu.VMEM((slabs, EXT, width), BF16),
            pltpu.VMEM((slabs, cap + EXT, width), BF16),
            pltpu.VMEM((slabs, cap + EXT, width), BF16),
            pltpu.VMEM((nodes, width), BF16),
            pltpu.VMEM((nodes, width), BF16),
            pltpu.VMEM((nodes, width), F32),
            pltpu.VMEM((nodes, width), F32),
            pltpu.VMEM((panels, 128, width), BF16),
            pltpu.VMEM((2, panels, SPLIT, width), BF16),
            pltpu.VMEM((panels, SPLIT, width), BF16),
            pltpu.VMEM((panels, 128 - SPLIT, width), BF16),
            pltpu.VMEM((4, count, SPLIT, width), BF16),
            pltpu.VMEM((6, count, 128 - SPLIT, width), BF16),
            pltpu.VMEM((early, 128, width), BF16),
            pltpu.VMEM((parts * count - early, 128, width), BF16),
            pltpu.VMEM((parts * count, 128, 128), BF16),
            pltpu.VMEM((parts * count, 128, width), BF16),
            pltpu.VMEM((nodes // 256, width, 256), BF16),
            pltpu.VMEM((8, parts * count), jnp.int32),
            pltpu.SMEM((8, parts * count), jnp.int32),
            pltpu.VMEM((width, width), F32),
            pltpu.VMEM((width, width), F32),
            dma((3,)), dma((parts,)), dma((slabs - 1,)), dma((slabs,)), dma((17,)), dma((17,)), dma((2,)),
        ]
        + sum_scratch(parts, slabs, width) * 2,
        compiler_params=pltpu.CompilerParams(collective_id=0, has_side_effects=True, vmem_limit_bytes=VMEM_LIMIT),
        name="main_step",
    )(picks, slab, local, remote, weight, cols, w_update, w_message, grad, pre, feats, tiles)


def final_kernel(out_ref, msg_ref, upd_ref, to_out_ref, to_msg_ref, to_upd_ref):
    to_out_ref[...] = out_ref[...]
    to_msg_ref[...] = msg_ref[...]
    to_upd_ref[...] = upd_ref[...]


def final_step(out, msg, upd):
    steps = 4
    args = (out, msg, upd)
    specs = [pl.BlockSpec((a.shape[0] // steps, a.shape[1]), lambda i: (i, 0)) for a in args]
    return pl.pallas_call(
        final_kernel,
        grid=(steps,),
        out_shape=[jax.ShapeDtypeStruct(a.shape, a.dtype) for a in args],
        in_specs=specs,
        out_specs=specs,
        compiler_params=pltpu.CompilerParams(vmem_limit_bytes=VMEM_LIMIT),
        name="final_step",
    )(*args)


def local(
    grad_out, pre_act, node_feats, w_message, w_update, tile_vals, tile_rows, tile_cols,
    rec_slab, rec_local, rec_remote, rec_weight,
):
    grad = grad_out[0]
    rows, width = grad.shape
    slabs = lax.axis_size("grp")
    parts = lax.axis_size("blk")
    records = rec_local.shape[1]
    cap = 2 * records // slabs
    factor = float((slabs * parts * rows) ** -0.5)
    lanes = lambda a: a.reshape(records // 128, 128)
    tiles = tile_vals[0, 0]
    count = tiles.shape[0] * tiles.shape[1]
    out, msg, upd = main_step(
        tile_rows[0], lanes(rec_slab), lanes(rec_local), lanes(rec_remote), lanes(rec_weight),
        tile_cols[0, 0], w_update, w_message, grad, pre_act[0], node_feats[0],
        tiles.reshape(count, *tiles.shape[2:]), slabs, parts, cap, factor,
    )
    feats, msg, upd = final_step(out, msg, upd)
    return (feats[None], msg, upd)


def solution(mesh):
    placed = (
        P("grp", "blk", None),
        P("grp", "blk", None),
        P("grp", "blk", None),
        P(),
        P(),
        P("grp", "blk", None, None, None, None),
        P("grp", None, None, None),
        P("grp", "blk", None, None),
        P("grp", "blk", None),
        P("grp", "blk"),
        P("grp", "blk"),
        P("grp", "blk"),
    )
    return jax.shard_map(
        local,
        mesh=mesh,
        in_specs=placed,
        out_specs=(P("grp", "blk", None), P(), P()),
        check_vma=False,
    )
```

```python
import functools

import jax
import jax.numpy as jnp
from jax import lax
from jax.experimental import pallas as pl
from jax.experimental.pallas import tpu as pltpu
from jax.sharding import PartitionSpec as P

F32 = jnp.float32
BF16 = jnp.bfloat16
MESH = pl.DeviceIdType.MESH
NT = (((1,), (1,)), ((), ()))
TN = (((0,), (0,)), ((), ()))
EXT = 16
VMEM_LIMIT = 61 * 1024 * 1024


def iota(shape, dim):
    return lax.broadcasted_iota(jnp.int32, shape, dim)


def index_tables(slab_ref, local_ref, remote_ref, weight_ref, pair_ref, ext_ref):
    slabs, cap = ext_ref.shape[0], pair_ref.shape[0]
    chunks = slab_ref.shape[0]
    slab = slab_ref[...]
    ids = iota((chunks, slabs, 128), 1)
    choose = jnp.where(ids == slab[:, None, :], 1.0, 0.0)
    flat = choose.reshape(chunks * slabs, 128)
    flat16 = flat.astype(BF16)
    upper = jnp.where(iota((128, 128), 0) < iota((128, 128), 1), 1.0, 0.0).astype(BF16)
    prefix = jnp.dot(flat16, upper, preferred_element_type=F32)
    totals = jnp.dot(flat16, jnp.ones((128, 128), BF16), preferred_element_type=F32)
    size = chunks * slabs
    row, col = iota((size, size), 0), iota((size, size), 1)
    earlier = (col < row) & (lax.rem(col, slabs) == lax.rem(row, slabs))
    offset = jnp.dot(jnp.where(earlier, 1.0, 0.0).astype(BF16), totals.astype(BF16), preferred_element_type=F32)
    place = ((prefix + offset) * flat).reshape(chunks, slabs, 128).sum(axis=1).astype(jnp.int32)
    remote, local, weight = remote_ref[...], local_ref[...], weight_ref[...]
    first = weight.astype(BF16).astype(F32)
    second = (weight - first).astype(BF16).astype(F32)
    third = weight - first - second
    values = [
        (remote // 256).astype(F32),
        (remote % 256).astype(F32),
        (local // 64).astype(F32),
        (local % 64).astype(F32),
        first,
        second,
        third,
        jnp.ones_like(weight),
    ]
    table = jnp.zeros((len(values) * slabs, cap), F32)
    for c in range(chunks):
        left = jnp.concatenate([choose[c] * v[c : c + 1] for v in values], axis=0).astype(BF16)
        right = jnp.where(iota((cap, 128), 0) == place[c : c + 1], 1.0, 0.0).astype(BF16)
        table += lax.dot_general(left, right, NT, preferred_element_type=F32)
    valid = table[7 * slabs : 8 * slabs]
    upper_part = jnp.where(valid > 0.5, table[:slabs], 64.0)
    lower_part = table[slabs : 2 * slabs]
    half = cap // 2
    for s in range(slabs):
        rows = [part[s : s + 1, q * half : (q + 1) * half] for part in (upper_part, lower_part) for q in range(2)]
        block = jnp.concatenate(rows + [jnp.zeros((EXT - 4, half), F32)], axis=0)
        ext_ref[s] = block.astype(BF16)
    row = lambda v: table[v * slabs : (v + 1) * slabs]
    node, scale = row(2) * 64.0 + row(3), row(4) + row(5) + row(6)
    empty = jnp.zeros((128 - 2 * slabs, cap), F32)
    pair_ref[...] = jnp.transpose(jnp.concatenate([node, scale, empty], axis=0))


def sum_scratch(parts, slabs, width):
    rows = width // parts
    dma = pltpu.SemaphoreType.DMA
    return [
        pltpu.VMEM((parts, rows, width), F32),
        pltpu.VMEM((parts - 1, rows, width), F32),
        pltpu.VMEM((slabs, 8, 128), F32),
        pltpu.VMEM((slabs - 1, 8, 128), F32),
        pltpu.VMEM((8, 128), F32),
        pltpu.VMEM((slabs, 8, 128), F32),
        pltpu.VMEM((rows, width), F32),
        pltpu.VMEM((parts, rows, width), F32),
        dma((parts - 1,)), dma((parts - 1,)),
        dma((slabs - 1,)), dma((slabs - 1,)),
        dma((slabs - 1,)), dma((slabs - 1,)),
        dma((parts - 1,)), dma((parts - 1,)),
    ]


def sum_stages(parts, slabs, factor, term_ref, out_ref, scratch):
    mine, in1, mid, in2, part, all2, done, all1, s1, r1, s2, r2, s3, r3, s4, r4 = scratch
    b, g = lax.axis_index("blk"), lax.axis_index("grp")
    rows = mine.shape[1]
    high = rows * 2 // slabs
    spots = [(slice(n // 2 * high, (n // 2 + 1) * high), slice(n % 2 * 128, n % 2 * 128 + 128)) for n in range(slabs)]
    flights = []

    def exchange(n, axis, me, src, dst, send, recv):
        copies = []
        for k in range(1, n):
            peer = lax.rem(me + k, n)
            copy = pltpu.make_async_remote_copy(
                src(peer), dst(k), send.at[k - 1], recv.at[k - 1], device_id={axis: peer}, device_id_type=MESH
            )
            copy.start()
            copies.append(copy)
        flights.append(copies)

    def landed():
        for copy in flights[-1]:
            copy.wait_recv()

    def split_blk():
        mid[...] = jnp.zeros_like(mid)
        for k in range(parts):
            mine[k] = term_ref[k * rows : (k + 1) * rows]
        exchange(parts, "blk", b, lambda p: mine.at[p], lambda k: in1.at[k - 1], s1, r1)

    def split_grp():
        landed()
        total = mine[b]
        for k in range(parts - 1):
            total += in1[k]
        for n in range(slabs):
            mid[n, :high] = total[spots[n]]
        exchange(slabs, "grp", g, lambda p: mid.at[p], lambda k: in2.at[k - 1], s2, r2)

    def join_grp():
        landed()
        piece = mid[g]
        for k in range(slabs - 1):
            piece += in2[k]
        part[...] = piece * factor
        all2[g] = piece * factor
        exchange(slabs, "grp", g, lambda p: part, lambda k: all2.at[g], s3, r3)

    def join_blk():
        landed()
        for n in range(slabs):
            done[spots[n]] = all2[n, :high]
        all1[b] = done[...]
        exchange(parts, "blk", b, lambda p: done, lambda k: all1.at[b], s4, r4)

    def finish():
        landed()
        for k in range(parts):
            out_ref[k * rows : (k + 1) * rows] = all1[k]
        for copies in flights:
            for copy in copies:
                copy.wait_send()

    return split_blk, split_grp, join_grp, join_blk, finish


def chip_scratch(parts, slabs):
    chips = parts * slabs // 2
    dma = pltpu.SemaphoreType.DMA
    return [
        pltpu.VMEM((chips, 8, 128), F32),
        pltpu.VMEM((chips - 1, 8, 128), F32),
        pltpu.VMEM((8, 128), F32),
        pltpu.VMEM((8, 128), F32),
        pltpu.VMEM((8, 128), F32),
        pltpu.VMEM((chips, 8, 128), F32),
        dma, dma, dma, dma, dma, dma,
    ]


def chip_peer(parts, slabs, k):
    b, g = lax.axis_index("blk"), lax.axis_index("grp")
    half = slabs // 2
    return (b + k // half) % parts, (g // 2 + k % half) % half, g % 2


def chip_stages(parts, slabs, factor, term_ref, out_ref, scratch):
    mine, come, part, pair, piece, whole, s1, r1, s2, r2, s3, r3 = scratch
    b, g = lax.axis_index("blk"), lax.axis_index("grp")
    half = slabs // 2
    chips = parts * half
    me = b * half + g // 2
    spots = [(slice(c // 2 * 8, c // 2 * 8 + 8), slice(c % 2 * 128, c % 2 * 128 + 128)) for c in range(chips)]
    many = pl.ds(0, chips - 1)
    other = pltpu.make_async_remote_copy(
        part, pair, s2, r2, device_id={"grp": g // 2 * 2 + 1 - g % 2}, device_id_type=MESH
    )

    def spread(src, dst, send, recv):
        def one(k, _):
            pb, pq, core = chip_peer(parts, slabs, k)
            pltpu.make_async_remote_copy(
                src(pb * half + pq), dst(k), send, recv,
                device_id={"blk": pb, "grp": pq * 2 + core}, device_id_type=MESH,
            ).start()
            return 0

        lax.fori_loop(1, chips, one, 0)

    def split():
        for c in range(chips):
            mine[c] = term_ref[spots[c]]
        spread(lambda c: mine.at[c], lambda k: come.at[k - 1], s1, r1)

    def cores():
        pltpu.make_async_copy(come, come, r1).wait()
        terms = [mine[me]] + [come[k] for k in range(chips - 1)]
        while len(terms) > 1:
            terms = [sum(terms[k : k + 2][1:], terms[k]) for k in range(0, len(terms), 2)]
        part[...] = terms[0]
        other.start()

    def join():
        other.wait_recv()
        piece[...] = (part[...] + pair[...]) * factor
        whole[me] = piece[...]
        spread(lambda c: piece, lambda k: whole.at[me], s3, r3)

    def finish():
        pltpu.make_async_copy(whole.at[many], whole.at[many], r3).wait()
        for c in range(chips):
            out_ref[spots[c]] = whole[c]
        pltpu.make_async_copy(come, come, s1).wait()
        other.wait_send()
        pltpu.make_async_copy(whole.at[many], whole.at[many], s3).wait()

    return split, cores, join, finish


def column_order(cols, early, order_ref):
    parts, picks = cols.shape
    count = parts * picks
    repeat = jnp.where(iota((picks, count), 1) % picks == iota((picks, count), 0), 1.0, 0.0).astype(BF16)
    wide = jnp.dot(cols.astype(F32).astype(BF16), repeat, preferred_element_type=F32)
    own = jnp.where(iota((parts, count), 1) // picks == iota((parts, count), 0), wide, 0.0)
    line = jnp.sum(own, axis=0, keepdims=True) + jnp.where(iota((1, count), 1) >= early, 32.0, 0.0)
    cols = jnp.broadcast_to(line, (count, count))
    across, down = iota((count, count), 1).astype(F32), iota((count, count), 0).astype(F32)
    turned = jnp.transpose(cols)
    ones = lambda hit: jnp.where(hit, 1.0, 0.0)
    total = lambda x: jnp.sum(x, axis=0, keepdims=True)
    rank = total(ones(turned * count + down < cols * count + across))
    ranks = jnp.transpose(jnp.broadcast_to(rank, (count, count)))
    hit = ones(ranks == across)
    order = total(hit * down)
    here = total(hit * turned)
    before = total(ones(ranks == across - 1.0) * (turned + 1.0)) - 1.0
    last = jnp.maximum(total(ones(turned <= across)) - 1.0, 0.0)
    named = jnp.minimum(total(ones(turned == across)), 1.0)
    rows = [order, ones(here == before), last, named, jnp.zeros((4, count), F32)]
    order_ref[...] = jnp.concatenate(rows, axis=0).astype(jnp.int32)


SPLIT = 80


def main_kernel(
    parts, slabs, factor,
    picks_ref, slab_ref, local_ref, remote_ref, weight_ref, cols_ref, w_ref, wm_ref, grad_hbm, pre_hbm, feats_hbm, tiles_hbm,
    out_hbm, out_msg_ref, out_upd_ref,
    pair_ref, ext_ref, out_buf, in_buf, grad_ref, pre_ref, acc_ref, slope_ref, gp_ref,
    near_ref, far_ref, side_ref, stage_a, stage_b, early_ref, late_ref,
    tiles_ref, run_ref, turned_ref, order_ref, order_smem, msg_ref, upd_ref,
    load_sem, tile_sem, rec_send, rec_recv, blk_send, blk_recv, store_sem, *scratch,
):
    b, g = lax.axis_index("blk"), lax.axis_index("grp")
    y, xh = b // 2, b % 2
    xl, z, core = g // 8, (g // 2) % 4, g % 2
    cap = pair_ref.shape[0]
    nodes, width = acc_ref.shape
    picks = stage_a.shape[1]

    load_grad = pltpu.make_async_copy(grad_hbm, grad_ref, load_sem.at[0])
    load_pre = pltpu.make_async_copy(pre_hbm, pre_ref, load_sem.at[1])
    load_feats = pltpu.make_async_copy(feats_hbm, pre_ref, load_sem.at[2])
    load_grad.start()
    load_pre.start()

    def rec_peer(n):
        q = n // 4
        dz, dx, dc = (n % 4 + 1) % 4, 1 - n // 8, (q + q // 2) % 2
        return ((xl + dx) % 2 * 4 + (z + dz) % 4) * 2 + (core + dc) % 2

    ring = parts // 2
    spot = lambda dy, dx: (y + dy) % ring * 2 + (xh + dx) % 2
    up, down, across, side = spot(1, 0), spot(ring - 1, 0), spot(2, 0), spot(0, 1)
    owners = (b, down, up, side, across, spot(ring - 1, 1), spot(1, 1), spot(2, 1))
    load_tiles = [
        pltpu.make_async_copy(
            tiles_hbm.at[pl.ds(r * picks, picks)], tiles_ref.at[pl.ds(k * picks, picks)], tile_sem.at[k]
        )
        for k, r in enumerate(owners)
    ]
    for load in load_tiles:
        load.start()

    barrier = pltpu.get_barrier_semaphore()
    chips = parts * slabs // 2

    def greet(k, _):
        pb, pq, same = chip_peer(parts, slabs, k)
        pl.semaphore_signal(barrier, inc=1, device_id={"blk": pb, "grp": pq * 2 + same}, device_id_type=MESH)
        return 0

    lax.fori_loop(1, chips, greet, 0)
    for n in range(slabs // 2):
        peer = (g // 2 + n) % (slabs // 2) * 2 + 1 - core
        pl.semaphore_signal(barrier, inc=1, device_id={"grp": peer}, device_id_type=MESH)

    index_tables(slab_ref, local_ref, remote_ref, weight_ref, pair_ref, ext_ref)
    load_grad.wait()
    pl.semaphore_wait(barrier, chips - 1 + slabs // 2)

    def rec_copy(n):
        return pltpu.make_async_remote_copy(
            out_buf.at[n], in_buf.at[n], rec_send.at[n], rec_recv.at[n],
            device_id={"grp": rec_peer(n)}, device_id_type=MESH,
        )

    own = slabs - 1
    own_copy = pltpu.make_async_copy(out_buf.at[own], in_buf.at[own], rec_recv.at[own])
    wide = 1024

    def gather(n, _):
        s = rec_peer(n)
        lane = iota((cap, 128), 1)
        column = lambda at: jnp.sum(jnp.where(lane == at, pair_ref[...], 0.0), axis=1, keepdims=True)
        node = jnp.broadcast_to(column(s).astype(jnp.int32), (cap, 128))
        total = jnp.zeros((cap, width), F32)
        for k in range(nodes // wide):
            pieces = [
                jnp.where(node == iota((1, 128), 1) + (k * wide + j * 128), 1.0, 0.0).astype(BF16)
                for j in range(wide // 128)
            ]
            total += jnp.dot(
                jnp.concatenate(pieces, axis=1), grad_ref[k * wide : (k + 1) * wide], preferred_element_type=F32
            )
        out_buf[n, :cap] = (total * column(s + slabs)).astype(BF16)
        out_buf[n, cap:] = ext_ref[s]

        @pl.when(n < own)
        def _():
            rec_copy(n).start()

        return 0

    lax.fori_loop(0, slabs, gather, 0)
    own_copy.start()
    acc_ref[...] = grad_ref[...].astype(F32)
    load_pre.wait()

    def slopes(i, _):
        at = pl.ds(pl.multiple_of(i * 256, 256), 256)
        pre = pre_ref[at].astype(F32)
        sig = 1.0 / (1.0 + jnp.exp(-pre))
        slope_ref[at] = sig * (1.0 + pre * (1.0 - sig))
        turned_ref[i] = jnp.transpose((pre * sig).astype(BF16))
        return 0

    lax.fori_loop(0, nodes // 256, slopes, 0)
    load_feats.start()
    own_copy.wait()

    tall = 1024

    def scatter(m, _):
        n = (m + own) % slabs

        @pl.when(m > 0)
        def _():
            rec_copy(n).wait_recv()

        ext = in_buf[n, cap:].astype(F32)
        lane = lambda q: jnp.concatenate([ext[q : q + 1], ext[q + 1 : q + 2]], axis=1).astype(jnp.int32)
        high, low = lane(0), lane(2)
        base = jnp.where(iota((256, cap), 0) == low, 1.0, 0.0).astype(BF16).reshape(16, 16, cap)
        block = in_buf[n, :cap]
        for i in range(nodes // tall):
            pieces = []
            for c in range(i * tall // 256, (i + 1) * tall // 256):
                mask = jnp.where(jnp.broadcast_to(high, (16, cap)) == c, 1.0, 0.0).astype(BF16)
                pieces.append((base * mask[None]).reshape(256, cap))
            at = slice(i * tall, (i + 1) * tall)
            acc_ref[at] += jnp.dot(jnp.concatenate(pieces, axis=0), block, preferred_element_type=F32)
        return 0

    lax.fori_loop(0, slabs, scatter, 0)

    def finish(i, _):
        at = pl.ds(pl.multiple_of(i * 512, 512), 512)
        gradh = acc_ref[at].astype(BF16)
        grad_ref[at] = gradh
        back = lax.dot_general(gradh, w_ref[...], NT, preferred_element_type=F32)
        gp_ref[pl.ds(i * 4, 4)] = (back * slope_ref[at]).astype(BF16).reshape(4, 128, width)
        return 0

    copies = {}

    def send(m, src, dst, peer):
        copies[m] = pltpu.make_async_remote_copy(
            src, dst, blk_send.at[m], blk_recv.at[m], device_id={"blk": peer}, device_id_type=MESH
        )
        copies[m].start()

    panels = nodes // 128
    low, high = pl.ds(0, panels // 2), pl.ds(panels // 2, panels // 2)
    rows_a, rows_b = pl.ds(0, SPLIT), pl.ds(SPLIT, 128 - SPLIT)
    lax.fori_loop(0, nodes // 1024, finish, 0)
    send(0, gp_ref.at[low, rows_a], near_ref.at[0, low], up)
    lax.fori_loop(nodes // 1024, nodes // 512, finish, 0)
    send(1, gp_ref.at[high, rows_a], near_ref.at[1, high], down)
    send(4, gp_ref.at[:, rows_b], side_ref, side)
    send(2, gp_ref.at[high, rows_a], near_ref.at[0, high], up)
    send(3, gp_ref.at[low, rows_a], near_ref.at[1, low], down)
    def pack(store, load, c, r):
        def one(t, _):
            store(t, load(picks_ref[c, r, t]))
            return 0

        lax.fori_loop(0, picks, one, 0)

    def to_stage(ref, n):
        def store(t, value):
            ref[n, t] = value

        return store

    def to_early(slot, rows):
        def store(t, value):
            early_ref[slot * picks + t, rows] = value

        return store

    top, rest, whole = slice(0, SPLIT), slice(SPLIT, 128), slice(0, 128)
    place = lambda ref, slot, rows: ref.at[pl.ds(slot * picks, picks), rows]
    near = [lambda i: near_ref[0, i], lambda i: near_ref[1, i]]
    pack(to_stage(stage_a, 0), lambda i: gp_ref[i, top], side, b)
    send(5, stage_a.at[0], place(early_ref, 3, rows_a), side)
    copies[0].wait_recv()
    copies[1].wait_recv()
    send(6, near_ref.at[0, low], far_ref.at[low], up)
    send(7, near_ref.at[1, high], far_ref.at[high], down)
    for n, peer in enumerate((up, down, across)):
        pack(to_stage(stage_b, n), lambda i: gp_ref[i, rest], peer, b)
        send(8 + n, stage_b.at[n], place(early_ref, (1, 2, 4)[n], rows_b), peer)
    copies[2].wait_recv()
    copies[3].wait_recv()
    for n, r in enumerate((down, up)):
        pack(to_stage(stage_a, 1 + n), near[n], side, r)
        send(11 + n, stage_a.at[1 + n], place(late_ref, n, rows_a), side)
    copies[4].wait_recv()
    for n, peer in enumerate((up, down, across)):
        pack(to_stage(stage_b, 3 + n), lambda i: side_ref[i], peer, side)
        send(13 + n, stage_b.at[3 + n], place(late_ref, n, rows_b), peer)
    pack(to_early(0, whole), lambda i: gp_ref[i], b, b)
    pack(to_early(1, top), near[0], b, down)
    pack(to_early(2, top), near[1], b, up)
    pack(to_early(3, rest), lambda i: side_ref[i], b, side)

    cols = jnp.concatenate([cols_ref[pl.ds(r, 1)] for r in owners], axis=0)
    early = 5 * picks
    column_order(cols, early, order_ref)
    to_smem = pltpu.make_async_copy(order_ref, order_smem, store_sem.at[0])
    to_smem.start()
    for load in load_tiles:
        load.wait()
    tiles = parts * picks

    def turn(k, _):
        tiles_ref[k] = jnp.transpose(tiles_ref[k])
        return 0

    lax.fori_loop(0, tiles, turn, 0)
    copies[6].wait_recv()
    copies[7].wait_recv()
    pack(to_stage(stage_a, 3), lambda i: far_ref[i], side, across)
    send(16, stage_a.at[3], place(late_ref, 2, rows_a), side)
    pack(to_early(4, top), lambda i: far_ref[i], b, across)

    upd_ref[...] = jnp.zeros_like(upd_ref)

    def update(i, _):
        at = pl.ds(pl.multiple_of(i * 256, 256), 256)
        upd_ref[...] += jnp.dot(turned_ref[i], grad_ref[at], preferred_element_type=F32)
        return 0

    lax.fori_loop(0, nodes // 256, update, 0)
    load_feats.wait()

    def turn_feats(k, _):
        at = pl.ds(pl.multiple_of(k * 256, 256), 256)
        turned_ref[k] = jnp.transpose(pre_ref[at])
        return 0

    lax.fori_loop(0, nodes // 256, turn_feats, 0)
    to_smem.wait()
    lax.fori_loop(0, slabs - 1, lambda n, x: (rec_copy(n).wait_send(), x)[1], 0)
    group = 8

    def products(ref, start, size):
        def step(m, total):
            for q in range(group):
                k = m * group + q
                f = lax.clamp(start, order_smem[0, k], start + size - 1)
                part = jnp.dot(tiles_ref[f], ref[f - start], preferred_element_type=F32)
                total = total * order_smem[1, k].astype(F32) + part
                run_ref[k] = total.astype(BF16)
            return total

        lax.fori_loop(start // group, (start + size) // group, step, jnp.zeros((128, width), F32))

    for m in (5, 8, 9, 10):
        copies[m].wait_recv()
    products(early_ref, 0, early)
    count = len(sum_scratch(parts, slabs, width))
    upd_sum = sum_stages(parts, slabs, factor, upd_ref, out_upd_ref, scratch[:count])
    msg_sum = chip_stages(parts, slabs, factor, msg_ref, out_msg_ref, scratch[count:])
    upd_sum[0]()
    for m in (11, 12, 13, 14, 15, 16):
        copies[m].wait_recv()
    upd_sum[1]()
    products(late_ref, early, tiles - early)
    for m in range(len(copies)):
        copies[m].wait_send()

    def settle(j, _):
        piece = lambda k: run_ref[lax.clamp(0, order_smem[2, k], tiles - 1)].astype(F32) * order_smem[3, k].astype(F32)
        gp_ref[j] = (piece(j) + piece(j + panels)).astype(BF16)
        return 0

    lax.fori_loop(0, panels, settle, 0)
    upd_sum[2]()
    msg = jnp.zeros((width, width), F32)
    for k in range(nodes // 256):
        msg += jnp.dot(turned_ref[k], gp_ref[2 * k : 2 * k + 2].reshape(256, width), preferred_element_type=F32)
    msg_ref[...] = msg
    msg_sum[0]()

    def features(i, _):
        at = pl.ds(pl.multiple_of(i * 512, 512), 512)
        spread = gp_ref[pl.ds(i * 4, 4)].reshape(512, width)
        below = lax.dot_general(spread, wm_ref[...], NT, preferred_element_type=F32)
        pre_ref[at] = (grad_ref[at].astype(F32) + below).astype(BF16)
        return 0

    lax.fori_loop(0, nodes // 512, features, 0)
    store_out = pltpu.make_async_copy(pre_ref, out_hbm, store_sem.at[1])
    store_out.start()
    msg_sum[1]()
    upd_sum[3]()
    msg_sum[2]()
    msg_sum[3]()
    upd_sum[4]()
    store_out.wait()


def main_step(
    picks, slab, local, remote, weight, cols, w_update, w_message, grad, pre, feats, tiles, slabs, parts, cap, factor
):
    nodes, width = grad.shape
    count = picks.shape[-1]
    panels, early = nodes // 128, 5 * count
    vmem = pl.BlockSpec(memory_space=pltpu.VMEM)
    hbm = pl.BlockSpec(memory_space=pl.ANY)
    dma = pltpu.SemaphoreType.DMA
    square = jax.ShapeDtypeStruct((width, width), F32)
    return pl.pallas_call(
        functools.partial(main_kernel, parts, slabs, factor),
        out_shape=[jax.ShapeDtypeStruct((nodes, width), BF16), square, square],
        in_specs=[pl.BlockSpec(memory_space=pltpu.SMEM)] + [vmem] * 7 + [hbm] * 4,
        out_specs=[hbm, vmem, vmem],
        scratch_shapes=[
            pltpu.VMEM((cap, 128), F32),
            pltpu.VMEM((slabs, EXT, width), BF16),
            pltpu.VMEM((slabs, cap + EXT, width), BF16),
            pltpu.VMEM((slabs, cap + EXT, width), BF16),
            pltpu.VMEM((nodes, width), BF16),
            pltpu.VMEM((nodes, width), BF16),
            pltpu.VMEM((nodes, width), F32),
            pltpu.VMEM((nodes, width), F32),
            pltpu.VMEM((panels, 128, width), BF16),
            pltpu.VMEM((2, panels, SPLIT, width), BF16),
            pltpu.VMEM((panels, SPLIT, width), BF16),
            pltpu.VMEM((panels, 128 - SPLIT, width), BF16),
            pltpu.VMEM((4, count, SPLIT, width), BF16),
            pltpu.VMEM((6, count, 128 - SPLIT, width), BF16),
            pltpu.VMEM((early, 128, width), BF16),
            pltpu.VMEM((parts * count - early, 128, width), BF16),
            pltpu.VMEM((parts * count, 128, 128), BF16),
            pltpu.VMEM((parts * count, 128, width), BF16),
            pltpu.VMEM((nodes // 256, width, 256), BF16),
            pltpu.VMEM((8, parts * count), jnp.int32),
            pltpu.SMEM((8, parts * count), jnp.int32),
            pltpu.VMEM((width, width), F32),
            pltpu.VMEM((width, width), F32),
            dma((3,)), dma((parts,)), dma((slabs - 1,)), dma((slabs,)), dma((17,)), dma((17,)), dma((2,)),
        ]
        + sum_scratch(parts, slabs, width)
        + chip_scratch(parts, slabs),
        compiler_params=pltpu.CompilerParams(collective_id=0, has_side_effects=True, vmem_limit_bytes=VMEM_LIMIT),
        name="main_step",
    )(picks, slab, local, remote, weight, cols, w_update, w_message, grad, pre, feats, tiles)


def final_kernel(out_ref, msg_ref, upd_ref, to_out_ref, to_msg_ref, to_upd_ref):
    to_out_ref[...] = out_ref[...]
    to_msg_ref[...] = msg_ref[...]
    to_upd_ref[...] = upd_ref[...]


def final_step(out, msg, upd):
    steps = 4
    args = (out, msg, upd)
    specs = [pl.BlockSpec((a.shape[0] // steps, a.shape[1]), lambda i: (i, 0)) for a in args]
    return pl.pallas_call(
        final_kernel,
        grid=(steps,),
        out_shape=[jax.ShapeDtypeStruct(a.shape, a.dtype) for a in args],
        in_specs=specs,
        out_specs=specs,
        compiler_params=pltpu.CompilerParams(vmem_limit_bytes=VMEM_LIMIT),
        name="final_step",
    )(*args)


def local(
    grad_out, pre_act, node_feats, w_message, w_update, tile_vals, tile_rows, tile_cols,
    rec_slab, rec_local, rec_remote, rec_weight,
):
    grad = grad_out[0]
    rows, width = grad.shape
    slabs = lax.axis_size("grp")
    parts = lax.axis_size("blk")
    records = rec_local.shape[1]
    cap = 2 * records // slabs
    factor = float((slabs * parts * rows) ** -0.5)
    lanes = lambda a: a.reshape(records // 128, 128)
    tiles = tile_vals[0, 0]
    count = tiles.shape[0] * tiles.shape[1]
    out, msg, upd = main_step(
        tile_rows[0], lanes(rec_slab), lanes(rec_local), lanes(rec_remote), lanes(rec_weight),
        tile_cols[0, 0], w_update, w_message, grad, pre_act[0], node_feats[0],
        tiles.reshape(count, *tiles.shape[2:]), slabs, parts, cap, factor,
    )
    feats, msg, upd = final_step(out, msg, upd)
    return (feats[None], msg, upd)


def solution(mesh):
    placed = (
        P("grp", "blk", None),
        P("grp", "blk", None),
        P("grp", "blk", None),
        P(),
        P(),
        P("grp", "blk", None, None, None, None),
        P("grp", None, None, None),
        P("grp", "blk", None, None),
        P("grp", "blk", None),
        P("grp", "blk"),
        P("grp", "blk"),
        P("grp", "blk"),
    )
    return jax.shard_map(
        local,
        mesh=mesh,
        in_specs=placed,
        out_specs=(P("grp", "blk", None), P(), P()),
        check_vma=False,
    )
```

```python
import functools

import jax
import jax.numpy as jnp
from jax import lax
from jax.experimental import pallas as pl
from jax.experimental.pallas import tpu as pltpu
from jax.sharding import PartitionSpec as P

F32 = jnp.float32
BF16 = jnp.bfloat16
MESH = pl.DeviceIdType.MESH
NT = (((1,), (1,)), ((), ()))
TN = (((0,), (0,)), ((), ()))
EXT = 16
VMEM_LIMIT = 61 * 1024 * 1024


def iota(shape, dim):
    return lax.broadcasted_iota(jnp.int32, shape, dim)


def index_tables(slab_ref, local_ref, remote_ref, weight_ref, pair_ref, ext_ref):
    slabs, cap = ext_ref.shape[0], pair_ref.shape[0]
    chunks = slab_ref.shape[0]
    slab = slab_ref[...]
    ids = iota((chunks, slabs, 128), 1)
    choose = jnp.where(ids == slab[:, None, :], 1.0, 0.0)
    flat = choose.reshape(chunks * slabs, 128)
    flat16 = flat.astype(BF16)
    upper = jnp.where(iota((128, 128), 0) < iota((128, 128), 1), 1.0, 0.0).astype(BF16)
    prefix = jnp.dot(flat16, upper, preferred_element_type=F32)
    totals = jnp.dot(flat16, jnp.ones((128, 128), BF16), preferred_element_type=F32)
    size = chunks * slabs
    row, col = iota((size, size), 0), iota((size, size), 1)
    earlier = (col < row) & (lax.rem(col, slabs) == lax.rem(row, slabs))
    offset = jnp.dot(jnp.where(earlier, 1.0, 0.0).astype(BF16), totals.astype(BF16), preferred_element_type=F32)
    place = ((prefix + offset) * flat).reshape(chunks, slabs, 128).sum(axis=1).astype(jnp.int32)
    remote, local, weight = remote_ref[...], local_ref[...], weight_ref[...]
    first = weight.astype(BF16).astype(F32)
    second = (weight - first).astype(BF16).astype(F32)
    third = weight - first - second
    values = [
        (remote // 256).astype(F32),
        (remote % 256).astype(F32),
        (local // 64).astype(F32),
        (local % 64).astype(F32),
        first,
        second,
        third,
        jnp.ones_like(weight),
    ]
    table = jnp.zeros((len(values) * slabs, cap), F32)
    for c in range(chunks):
        left = jnp.concatenate([choose[c] * v[c : c + 1] for v in values], axis=0).astype(BF16)
        right = jnp.where(iota((cap, 128), 0) == place[c : c + 1], 1.0, 0.0).astype(BF16)
        table += lax.dot_general(left, right, NT, preferred_element_type=F32)
    valid = table[7 * slabs : 8 * slabs]
    upper_part = jnp.where(valid > 0.5, table[:slabs], 64.0)
    lower_part = table[slabs : 2 * slabs]
    half = cap // 2
    for s in range(slabs):
        rows = [part[s : s + 1, q * half : (q + 1) * half] for part in (upper_part, lower_part) for q in range(2)]
        block = jnp.concatenate(rows + [jnp.zeros((EXT - 4, half), F32)], axis=0)
        ext_ref[s] = block.astype(BF16)
    row = lambda v: table[v * slabs : (v + 1) * slabs]
    node, scale = row(2) * 64.0 + row(3), row(4) + row(5) + row(6)
    empty = jnp.zeros((128 - 2 * slabs, cap), F32)
    pair_ref[...] = jnp.transpose(jnp.concatenate([node, scale, empty], axis=0))


def sum_scratch(parts, slabs, width):
    rows = width // parts
    dma = pltpu.SemaphoreType.DMA
    return [
        pltpu.VMEM((parts, rows, width), F32),
        pltpu.VMEM((parts - 1, rows, width), F32),
        pltpu.VMEM((slabs, 8, 128), F32),
        pltpu.VMEM((slabs - 1, 8, 128), F32),
        pltpu.VMEM((8, 128), F32),
        pltpu.VMEM((slabs, 8, 128), F32),
        pltpu.VMEM((rows, width), F32),
        pltpu.VMEM((parts, rows, width), F32),
        dma((parts - 1,)), dma((parts - 1,)),
        dma((slabs - 1,)), dma((slabs - 1,)),
        dma((slabs - 1,)), dma((slabs - 1,)),
        dma((parts - 1,)), dma((parts - 1,)),
    ]


def sum_stages(parts, slabs, factor, term_ref, out_ref, scratch):
    mine, in1, mid, in2, part, all2, done, all1, s1, r1, s2, r2, s3, r3, s4, r4 = scratch
    b, g = lax.axis_index("blk"), lax.axis_index("grp")
    rows = mine.shape[1]
    high = rows * 2 // slabs
    spots = [(slice(n // 2 * high, (n // 2 + 1) * high), slice(n % 2 * 128, n % 2 * 128 + 128)) for n in range(slabs)]
    flights = []

    def exchange(n, axis, me, src, dst, send, recv):
        copies = []
        for k in range(1, n):
            peer = lax.rem(me + k, n)
            copy = pltpu.make_async_remote_copy(
                src(peer), dst(k), send.at[k - 1], recv.at[k - 1], device_id={axis: peer}, device_id_type=MESH
            )
            copy.start()
            copies.append(copy)
        flights.append(copies)

    def landed():
        for copy in flights[-1]:
            copy.wait_recv()

    def split_blk():
        mid[...] = jnp.zeros_like(mid)
        for k in range(parts):
            mine[k] = term_ref[k * rows : (k + 1) * rows]
        exchange(parts, "blk", b, lambda p: mine.at[p], lambda k: in1.at[k - 1], s1, r1)

    def split_grp():
        landed()
        total = mine[b]
        for k in range(parts - 1):
            total += in1[k]
        for n in range(slabs):
            mid[n, :high] = total[spots[n]]
        exchange(slabs, "grp", g, lambda p: mid.at[p], lambda k: in2.at[k - 1], s2, r2)

    def join_grp():
        landed()
        piece = mid[g]
        for k in range(slabs - 1):
            piece += in2[k]
        part[...] = piece * factor
        all2[g] = piece * factor
        exchange(slabs, "grp", g, lambda p: part, lambda k: all2.at[g], s3, r3)

    def join_blk():
        landed()
        for n in range(slabs):
            done[spots[n]] = all2[n, :high]
        all1[b] = done[...]
        exchange(parts, "blk", b, lambda p: done, lambda k: all1.at[b], s4, r4)

    def finish():
        landed()
        for k in range(parts):
            out_ref[k * rows : (k + 1) * rows] = all1[k]
        for copies in flights:
            for copy in copies:
                copy.wait_send()

    return split_blk, split_grp, join_grp, join_blk, finish


def chip_scratch(parts, slabs):
    chips = parts * slabs // 2
    dma = pltpu.SemaphoreType.DMA
    return [
        pltpu.VMEM((chips, 8, 128), F32),
        pltpu.VMEM((chips - 1, 8, 128), F32),
        pltpu.VMEM((8, 128), F32),
        pltpu.VMEM((8, 128), F32),
        pltpu.VMEM((8, 128), F32),
        pltpu.VMEM((chips, 8, 128), F32),
        dma, dma, dma, dma, dma, dma,
    ]


def chip_peer(parts, slabs, k):
    b, g = lax.axis_index("blk"), lax.axis_index("grp")
    half = slabs // 2
    return (b + k // half) % parts, (g // 2 + k % half) % half, g % 2


def chip_stages(parts, slabs, factor, term_ref, out_ref, scratch):
    mine, come, part, pair, piece, whole, s1, r1, s2, r2, s3, r3 = scratch
    b, g = lax.axis_index("blk"), lax.axis_index("grp")
    half = slabs // 2
    chips = parts * half
    me = b * half + g // 2
    spots = [(slice(c // 2 * 8, c // 2 * 8 + 8), slice(c % 2 * 128, c % 2 * 128 + 128)) for c in range(chips)]
    many = pl.ds(0, chips - 1)
    other = pltpu.make_async_remote_copy(
        part, pair, s2, r2, device_id={"grp": g // 2 * 2 + 1 - g % 2}, device_id_type=MESH
    )

    def spread(src, dst, send, recv):
        def one(k, _):
            pb, pq, core = chip_peer(parts, slabs, k)
            pltpu.make_async_remote_copy(
                src(pb * half + pq), dst(k), send, recv,
                device_id={"blk": pb, "grp": pq * 2 + core}, device_id_type=MESH,
            ).start()
            return 0

        lax.fori_loop(1, chips, one, 0)

    def split():
        for c in range(chips):
            mine[c] = term_ref[spots[c]]
        spread(lambda c: mine.at[c], lambda k: come.at[k - 1], s1, r1)

    def cores():
        pltpu.make_async_copy(come, come, r1).wait()
        terms = [mine[me]] + [come[k] for k in range(chips - 1)]
        while len(terms) > 1:
            terms = [sum(terms[k : k + 2][1:], terms[k]) for k in range(0, len(terms), 2)]
        part[...] = terms[0]
        other.start()

    def join():
        other.wait_recv()
        piece[...] = (part[...] + pair[...]) * factor
        whole[me] = piece[...]
        spread(lambda c: piece, lambda k: whole.at[me], s3, r3)

    def finish():
        pltpu.make_async_copy(whole.at[many], whole.at[many], r3).wait()
        for c in range(chips):
            out_ref[spots[c]] = whole[c]
        pltpu.make_async_copy(come, come, s1).wait()
        other.wait_send()
        pltpu.make_async_copy(whole.at[many], whole.at[many], s3).wait()

    return split, cores, join, finish


def column_order(cols, early, order_ref):
    parts, picks = cols.shape
    count = parts * picks
    repeat = jnp.where(iota((picks, count), 1) % picks == iota((picks, count), 0), 1.0, 0.0).astype(BF16)
    wide = jnp.dot(cols.astype(F32).astype(BF16), repeat, preferred_element_type=F32)
    own = jnp.where(iota((parts, count), 1) // picks == iota((parts, count), 0), wide, 0.0)
    line = jnp.sum(own, axis=0, keepdims=True) + jnp.where(iota((1, count), 1) >= early, 32.0, 0.0)
    cols = jnp.broadcast_to(line, (count, count))
    across, down = iota((count, count), 1).astype(F32), iota((count, count), 0).astype(F32)
    turned = jnp.transpose(cols)
    ones = lambda hit: jnp.where(hit, 1.0, 0.0)
    total = lambda x: jnp.sum(x, axis=0, keepdims=True)
    rank = total(ones(turned * count + down < cols * count + across))
    ranks = jnp.transpose(jnp.broadcast_to(rank, (count, count)))
    hit = ones(ranks == across)
    order = total(hit * down)
    here = total(hit * turned)
    before = total(ones(ranks == across - 1.0) * (turned + 1.0)) - 1.0
    last = jnp.maximum(total(ones(turned <= across)) - 1.0, 0.0)
    named = jnp.minimum(total(ones(turned == across)), 1.0)
    rows = [order, ones(here == before), last, named, jnp.zeros((4, count), F32)]
    order_ref[...] = jnp.concatenate(rows, axis=0).astype(jnp.int32)


SPLIT = 80


def main_kernel(
    parts, slabs, factor,
    picks_ref, slab_ref, local_ref, remote_ref, weight_ref, cols_ref, w_ref, wm_ref, grad_hbm, pre_hbm, feats_hbm, tiles_hbm,
    out_hbm, out_msg_ref, out_upd_ref,
    pair_ref, ext_ref, out_buf, in_buf, grad_ref, pre_ref, acc_ref, slope_ref, gp_ref,
    near_ref, far_ref, side_ref, stage_a, stage_b, early_ref, late_ref,
    tiles_ref, run_ref, turned_ref, order_ref, order_smem, msg_ref, upd_ref,
    load_sem, tile_sem, rec_send, rec_recv, blk_send, blk_recv, store_sem, *scratch,
):
    b, g = lax.axis_index("blk"), lax.axis_index("grp")
    y, xh = b // 2, b % 2
    xl, z, core = g // 8, (g // 2) % 4, g % 2
    cap = pair_ref.shape[0]
    nodes, width = acc_ref.shape
    picks = stage_a.shape[1]

    load_grad = pltpu.make_async_copy(grad_hbm, grad_ref, load_sem.at[0])
    load_pre = pltpu.make_async_copy(pre_hbm, pre_ref, load_sem.at[1])
    load_feats = pltpu.make_async_copy(feats_hbm, pre_ref, load_sem.at[2])
    load_grad.start()
    load_pre.start()

    def rec_peer(n):
        q = n // 4
        dz, dx, dc = (n % 4 + 1) % 4, 1 - n // 8, (q + q // 2) % 2
        return ((xl + dx) % 2 * 4 + (z + dz) % 4) * 2 + (core + dc) % 2

    ring = parts // 2
    spot = lambda dy, dx: (y + dy) % ring * 2 + (xh + dx) % 2
    up, down, across, side = spot(1, 0), spot(ring - 1, 0), spot(2, 0), spot(0, 1)
    owners = (b, down, up, side, across, spot(ring - 1, 1), spot(1, 1), spot(2, 1))
    load_tiles = [
        pltpu.make_async_copy(
            tiles_hbm.at[pl.ds(r * picks, picks)], tiles_ref.at[pl.ds(k * picks, picks)], tile_sem.at[k]
        )
        for k, r in enumerate(owners)
    ]
    for load in load_tiles:
        load.start()

    barrier = pltpu.get_barrier_semaphore()
    for n in range(slabs - 1):
        pl.semaphore_signal(barrier, inc=1, device_id={"grp": rec_peer(n)}, device_id_type=MESH)
    for n in range(parts - 1):
        pl.semaphore_signal(barrier, inc=1, device_id={"blk": lax.rem(b + n + 1, parts)}, device_id_type=MESH)

    index_tables(slab_ref, local_ref, remote_ref, weight_ref, pair_ref, ext_ref)
    load_grad.wait()
    pl.semaphore_wait(barrier, slabs + parts - 2)

    def rec_copy(n):
        return pltpu.make_async_remote_copy(
            out_buf.at[n], in_buf.at[n], rec_send.at[n], rec_recv.at[n],
            device_id={"grp": rec_peer(n)}, device_id_type=MESH,
        )

    own = slabs - 1
    own_copy = pltpu.make_async_copy(out_buf.at[own], in_buf.at[own], rec_recv.at[own])
    wide = 1024

    def gather(n, _):
        s = rec_peer(n)
        lane = iota((cap, 128), 1)
        column = lambda at: jnp.sum(jnp.where(lane == at, pair_ref[...], 0.0), axis=1, keepdims=True)
        node = jnp.broadcast_to(column(s).astype(jnp.int32), (cap, 128))
        total = jnp.zeros((cap, width), F32)
        for k in range(nodes // wide):
            pieces = [
                jnp.where(node == iota((1, 128), 1) + (k * wide + j * 128), 1.0, 0.0).astype(BF16)
                for j in range(wide // 128)
            ]
            total += jnp.dot(
                jnp.concatenate(pieces, axis=1), grad_ref[k * wide : (k + 1) * wide], preferred_element_type=F32
            )
        out_buf[n, :cap] = (total * column(s + slabs)).astype(BF16)
        out_buf[n, cap:] = ext_ref[s]

        @pl.when(n < own)
        def _():
            rec_copy(n).start()

        return 0

    lax.fori_loop(0, slabs, gather, 0)
    own_copy.start()
    acc_ref[...] = grad_ref[...].astype(F32)
    load_pre.wait()

    def slopes(i, _):
        at = pl.ds(pl.multiple_of(i * 256, 256), 256)
        pre = pre_ref[at].astype(F32)
        sig = 1.0 / (1.0 + jnp.exp(-pre))
        slope_ref[at] = sig * (1.0 + pre * (1.0 - sig))
        turned_ref[i] = jnp.transpose((pre * sig).astype(BF16))
        return 0

    lax.fori_loop(0, nodes // 256, slopes, 0)
    load_feats.start()
    own_copy.wait()

    tall = 1024

    def scatter(m, _):
        n = (m + own) % slabs

        @pl.when(m > 0)
        def _():
            rec_copy(n).wait_recv()

        ext = in_buf[n, cap:].astype(F32)
        lane = lambda q: jnp.concatenate([ext[q : q + 1], ext[q + 1 : q + 2]], axis=1).astype(jnp.int32)
        high, low = lane(0), lane(2)
        base = jnp.where(iota((256, cap), 0) == low, 1.0, 0.0).astype(BF16).reshape(16, 16, cap)
        block = in_buf[n, :cap]
        for i in range(nodes // tall):
            pieces = []
            for c in range(i * tall // 256, (i + 1) * tall // 256):
                mask = jnp.where(jnp.broadcast_to(high, (16, cap)) == c, 1.0, 0.0).astype(BF16)
                pieces.append((base * mask[None]).reshape(256, cap))
            at = slice(i * tall, (i + 1) * tall)
            acc_ref[at] += jnp.dot(jnp.concatenate(pieces, axis=0), block, preferred_element_type=F32)
        return 0

    lax.fori_loop(0, slabs, scatter, 0)

    def finish(i, _):
        at = pl.ds(pl.multiple_of(i * 512, 512), 512)
        gradh = acc_ref[at].astype(BF16)
        grad_ref[at] = gradh
        back = lax.dot_general(gradh, w_ref[...], NT, preferred_element_type=F32)
        gp_ref[pl.ds(i * 4, 4)] = (back * slope_ref[at]).astype(BF16).reshape(4, 128, width)
        return 0

    copies = {}

    def send(m, src, dst, peer):
        copies[m] = pltpu.make_async_remote_copy(
            src, dst, blk_send.at[m], blk_recv.at[m], device_id={"blk": peer}, device_id_type=MESH
        )
        copies[m].start()

    panels = nodes // 128
    low, high = pl.ds(0, panels // 2), pl.ds(panels // 2, panels // 2)
    rows_a, rows_b = pl.ds(0, SPLIT), pl.ds(SPLIT, 128 - SPLIT)
    lax.fori_loop(0, nodes // 1024, finish, 0)
    send(0, gp_ref.at[low, rows_a], near_ref.at[0, low], up)
    lax.fori_loop(nodes // 1024, nodes // 512, finish, 0)
    send(1, gp_ref.at[high, rows_a], near_ref.at[1, high], down)
    send(4, gp_ref.at[:, rows_b], side_ref, side)
    send(2, gp_ref.at[high, rows_a], near_ref.at[0, high], up)
    send(3, gp_ref.at[low, rows_a], near_ref.at[1, low], down)
    def pack(store, load, c, r):
        def one(t, _):
            store(t, load(picks_ref[c, r, t]))
            return 0

        lax.fori_loop(0, picks, one, 0)

    def to_stage(ref, n):
        def store(t, value):
            ref[n, t] = value

        return store

    def to_early(slot, rows):
        def store(t, value):
            early_ref[slot * picks + t, rows] = value

        return store

    top, rest, whole = slice(0, SPLIT), slice(SPLIT, 128), slice(0, 128)
    place = lambda ref, slot, rows: ref.at[pl.ds(slot * picks, picks), rows]
    near = [lambda i: near_ref[0, i], lambda i: near_ref[1, i]]
    pack(to_stage(stage_a, 0), lambda i: gp_ref[i, top], side, b)
    send(5, stage_a.at[0], place(early_ref, 3, rows_a), side)
    copies[0].wait_recv()
    copies[1].wait_recv()
    send(6, near_ref.at[0, low], far_ref.at[low], up)
    send(7, near_ref.at[1, high], far_ref.at[high], down)
    for n, peer in enumerate((up, down, across)):
        pack(to_stage(stage_b, n), lambda i: gp_ref[i, rest], peer, b)
        send(8 + n, stage_b.at[n], place(early_ref, (1, 2, 4)[n], rows_b), peer)
    copies[2].wait_recv()
    copies[3].wait_recv()
    for n, r in enumerate((down, up)):
        pack(to_stage(stage_a, 1 + n), near[n], side, r)
        send(11 + n, stage_a.at[1 + n], place(late_ref, n, rows_a), side)
    copies[4].wait_recv()
    for n, peer in enumerate((up, down, across)):
        pack(to_stage(stage_b, 3 + n), lambda i: side_ref[i], peer, side)
        send(13 + n, stage_b.at[3 + n], place(late_ref, n, rows_b), peer)
    pack(to_early(0, whole), lambda i: gp_ref[i], b, b)
    pack(to_early(1, top), near[0], b, down)
    pack(to_early(2, top), near[1], b, up)
    pack(to_early(3, rest), lambda i: side_ref[i], b, side)

    cols = jnp.concatenate([cols_ref[pl.ds(r, 1)] for r in owners], axis=0)
    early = 5 * picks
    column_order(cols, early, order_ref)
    to_smem = pltpu.make_async_copy(order_ref, order_smem, store_sem.at[0])
    to_smem.start()
    for load in load_tiles:
        load.wait()
    tiles = parts * picks

    def turn(k, _):
        tiles_ref[k] = jnp.transpose(tiles_ref[k])
        return 0

    lax.fori_loop(0, tiles, turn, 0)
    copies[6].wait_recv()
    copies[7].wait_recv()
    pack(to_stage(stage_a, 3), lambda i: far_ref[i], side, across)
    send(16, stage_a.at[3], place(late_ref, 2, rows_a), side)
    pack(to_early(4, top), lambda i: far_ref[i], b, across)

    upd_ref[...] = jnp.zeros_like(upd_ref)

    def update(i, _):
        at = pl.ds(pl.multiple_of(i * 256, 256), 256)
        upd_ref[...] += jnp.dot(turned_ref[i], grad_ref[at], preferred_element_type=F32)
        return 0

    lax.fori_loop(0, nodes // 256, update, 0)
    load_feats.wait()

    def turn_feats(k, _):
        at = pl.ds(pl.multiple_of(k * 256, 256), 256)
        turned_ref[k] = jnp.transpose(pre_ref[at])
        return 0

    lax.fori_loop(0, nodes // 256, turn_feats, 0)
    to_smem.wait()
    lax.fori_loop(0, slabs - 1, lambda n, x: (rec_copy(n).wait_send(), x)[1], 0)
    group = 8

    def products(ref, start, size):
        def step(m, total):
            for q in range(group):
                k = m * group + q
                f = lax.clamp(start, order_smem[0, k], start + size - 1)
                part = jnp.dot(tiles_ref[f], ref[f - start], preferred_element_type=F32)
                total = total * order_smem[1, k].astype(F32) + part
                run_ref[k] = total.astype(BF16)
            return total

        lax.fori_loop(start // group, (start + size) // group, step, jnp.zeros((128, width), F32))

    for m in (5, 8, 9, 10):
        copies[m].wait_recv()
    products(early_ref, 0, early)
    count = len(sum_scratch(parts, slabs, width))
    upd_sum = sum_stages(parts, slabs, factor, upd_ref, out_upd_ref, scratch[:count])
    msg_sum = chip_stages(parts, slabs, factor, msg_ref, out_msg_ref, scratch[count:])
    upd_sum[0]()
    for m in (11, 12, 13, 14, 15, 16):
        copies[m].wait_recv()
    upd_sum[1]()
    products(late_ref, early, tiles - early)
    for m in range(len(copies)):
        copies[m].wait_send()

    def settle(j, _):
        piece = lambda k: run_ref[lax.clamp(0, order_smem[2, k], tiles - 1)].astype(F32) * order_smem[3, k].astype(F32)
        gp_ref[j] = (piece(j) + piece(j + panels)).astype(BF16)
        return 0

    lax.fori_loop(0, panels, settle, 0)
    upd_sum[2]()
    msg = jnp.zeros((width, width), F32)
    for k in range(nodes // 256):
        msg += jnp.dot(turned_ref[k], gp_ref[2 * k : 2 * k + 2].reshape(256, width), preferred_element_type=F32)
    msg_ref[...] = msg
    msg_sum[0]()

    def features(i, _):
        at = pl.ds(pl.multiple_of(i * 512, 512), 512)
        spread = gp_ref[pl.ds(i * 4, 4)].reshape(512, width)
        below = lax.dot_general(spread, wm_ref[...], NT, preferred_element_type=F32)
        pre_ref[at] = (grad_ref[at].astype(F32) + below).astype(BF16)
        return 0

    lax.fori_loop(0, nodes // 512, features, 0)
    store_out = pltpu.make_async_copy(pre_ref, out_hbm, store_sem.at[1])
    store_out.start()
    msg_sum[1]()
    upd_sum[3]()
    msg_sum[2]()
    msg_sum[3]()
    upd_sum[4]()
    store_out.wait()


def main_step(
    picks, slab, local, remote, weight, cols, w_update, w_message, grad, pre, feats, tiles, slabs, parts, cap, factor
):
    nodes, width = grad.shape
    count = picks.shape[-1]
    panels, early = nodes // 128, 5 * count
    vmem = pl.BlockSpec(memory_space=pltpu.VMEM)
    hbm = pl.BlockSpec(memory_space=pl.ANY)
    dma = pltpu.SemaphoreType.DMA
    square = jax.ShapeDtypeStruct((width, width), F32)
    return pl.pallas_call(
        functools.partial(main_kernel, parts, slabs, factor),
        out_shape=[jax.ShapeDtypeStruct((nodes, width), BF16), square, square],
        in_specs=[pl.BlockSpec(memory_space=pltpu.SMEM)] + [vmem] * 7 + [hbm] * 4,
        out_specs=[hbm, vmem, vmem],
        scratch_shapes=[
            pltpu.VMEM((cap, 128), F32),
            pltpu.VMEM((slabs, EXT, width), BF16),
            pltpu.VMEM((slabs, cap + EXT, width), BF16),
            pltpu.VMEM((slabs, cap + EXT, width), BF16),
            pltpu.VMEM((nodes, width), BF16),
            pltpu.VMEM((nodes, width), BF16),
            pltpu.VMEM((nodes, width), F32),
            pltpu.VMEM((nodes, width), F32),
            pltpu.VMEM((panels, 128, width), BF16),
            pltpu.VMEM((2, panels, SPLIT, width), BF16),
            pltpu.VMEM((panels, SPLIT, width), BF16),
            pltpu.VMEM((panels, 128 - SPLIT, width), BF16),
            pltpu.VMEM((4, count, SPLIT, width), BF16),
            pltpu.VMEM((6, count, 128 - SPLIT, width), BF16),
            pltpu.VMEM((early, 128, width), BF16),
            pltpu.VMEM((parts * count - early, 128, width), BF16),
            pltpu.VMEM((parts * count, 128, 128), BF16),
            pltpu.VMEM((parts * count, 128, width), BF16),
            pltpu.VMEM((nodes // 256, width, 256), BF16),
            pltpu.VMEM((8, parts * count), jnp.int32),
            pltpu.SMEM((8, parts * count), jnp.int32),
            pltpu.VMEM((width, width), F32),
            pltpu.VMEM((width, width), F32),
            dma((3,)), dma((parts,)), dma((slabs - 1,)), dma((slabs,)), dma((17,)), dma((17,)), dma((2,)),
        ]
        + sum_scratch(parts, slabs, width)
        + chip_scratch(parts, slabs),
        compiler_params=pltpu.CompilerParams(collective_id=0, has_side_effects=True, vmem_limit_bytes=VMEM_LIMIT),
        name="main_step",
    )(picks, slab, local, remote, weight, cols, w_update, w_message, grad, pre, feats, tiles)


def final_kernel(out_ref, msg_ref, upd_ref, to_out_ref, to_msg_ref, to_upd_ref, out_buf, msg_buf, upd_buf, come, go):
    steps = 4
    rows = out_ref.shape[0] // steps
    ways = [(msg_ref, msg_buf, to_msg_ref), (upd_ref, upd_buf, to_upd_ref)]
    for k in range(steps):
        at = pl.ds(k * rows, rows)
        ways.append((out_ref.at[at], out_buf.at[at], to_out_ref.at[at]))
    loads = [pltpu.make_async_copy(src, buf, come.at[k]) for k, (src, buf, _) in enumerate(ways)]
    stores = [pltpu.make_async_copy(buf, dst, go.at[k]) for k, (_, buf, dst) in enumerate(ways)]
    for load in loads:
        load.start()
    for load, store in zip(loads, stores):
        load.wait()
        store.start()
    for store in stores:
        store.wait()


def final_step(out, msg, upd):
    hbm = pl.BlockSpec(memory_space=pl.ANY)
    args = (out, msg, upd)
    return pl.pallas_call(
        final_kernel,
        out_shape=[jax.ShapeDtypeStruct(a.shape, a.dtype) for a in args],
        in_specs=[hbm] * 3,
        out_specs=[hbm] * 3,
        scratch_shapes=[pltpu.VMEM(a.shape, a.dtype) for a in args] + [pltpu.SemaphoreType.DMA((6,))] * 2,
        compiler_params=pltpu.CompilerParams(vmem_limit_bytes=VMEM_LIMIT),
        name="final_step",
    )(*args)


def local(
    grad_out, pre_act, node_feats, w_message, w_update, tile_vals, tile_rows, tile_cols,
    rec_slab, rec_local, rec_remote, rec_weight,
):
    grad = grad_out[0]
    rows, width = grad.shape
    slabs = lax.axis_size("grp")
    parts = lax.axis_size("blk")
    records = rec_local.shape[1]
    cap = 2 * records // slabs
    factor = float((slabs * parts * rows) ** -0.5)
    lanes = lambda a: a.reshape(records // 128, 128)
    tiles = tile_vals[0, 0]
    count = tiles.shape[0] * tiles.shape[1]
    out, msg, upd = main_step(
        tile_rows[0], lanes(rec_slab), lanes(rec_local), lanes(rec_remote), lanes(rec_weight),
        tile_cols[0, 0], w_update, w_message, grad, pre_act[0], node_feats[0],
        tiles.reshape(count, *tiles.shape[2:]), slabs, parts, cap, factor,
    )
    feats, msg, upd = final_step(out, msg, upd)
    return (feats[None], msg, upd)


def solution(mesh):
    placed = (
        P("grp", "blk", None),
        P("grp", "blk", None),
        P("grp", "blk", None),
        P(),
        P(),
        P("grp", "blk", None, None, None, None),
        P("grp", None, None, None),
        P("grp", "blk", None, None),
        P("grp", "blk", None),
        P("grp", "blk"),
        P("grp", "blk"),
        P("grp", "blk"),
    )
    return jax.shard_map(
        local,
        mesh=mesh,
        in_specs=placed,
        out_specs=(P("grp", "blk", None), P(), P()),
        check_vma=False,
    )
```

```python
import functools

import jax
import jax.numpy as jnp
from jax import lax
from jax.experimental import pallas as pl
from jax.experimental.pallas import tpu as pltpu
from jax.sharding import PartitionSpec as P

F32 = jnp.float32
BF16 = jnp.bfloat16
MESH = pl.DeviceIdType.MESH
NT = (((1,), (1,)), ((), ()))
TN = (((0,), (0,)), ((), ()))
EXT = 16
VMEM_LIMIT = 61 * 1024 * 1024


def iota(shape, dim):
    return lax.broadcasted_iota(jnp.int32, shape, dim)


def index_tables(slab_ref, local_ref, remote_ref, weight_ref, pair_ref, ext_ref):
    slabs, cap = ext_ref.shape[0], pair_ref.shape[0]
    chunks = slab_ref.shape[0]
    slab = slab_ref[...]
    ids = iota((chunks, slabs, 128), 1)
    choose = jnp.where(ids == slab[:, None, :], 1.0, 0.0)
    flat = choose.reshape(chunks * slabs, 128)
    flat16 = flat.astype(BF16)
    upper = jnp.where(iota((128, 128), 0) < iota((128, 128), 1), 1.0, 0.0).astype(BF16)
    prefix = jnp.dot(flat16, upper, preferred_element_type=F32)
    totals = jnp.dot(flat16, jnp.ones((128, 128), BF16), preferred_element_type=F32)
    size = chunks * slabs
    row, col = iota((size, size), 0), iota((size, size), 1)
    earlier = (col < row) & (((col ^ row) & (slabs - 1)) == 0)
    offset = jnp.dot(jnp.where(earlier, 1.0, 0.0).astype(BF16), totals.astype(BF16), preferred_element_type=F32)
    place = ((prefix + offset) * flat).reshape(chunks, slabs, 128).sum(axis=1).astype(jnp.int32)
    remote, local, weight = remote_ref[...], local_ref[...], weight_ref[...]
    first = weight.astype(BF16).astype(F32)
    second = (weight - first).astype(BF16).astype(F32)
    third = weight - first - second
    values = [
        (remote // 256).astype(F32),
        (remote % 256).astype(F32),
        (local // 64).astype(F32),
        (local % 64).astype(F32),
        first,
        second,
        third,
        jnp.ones_like(weight),
    ]
    table = jnp.zeros((len(values) * slabs, cap), F32)
    for c in range(0, chunks, 2):
        pair = (c, c + 1)
        left = [jnp.concatenate([choose[k] * v[k : k + 1] for v in values], axis=0).astype(BF16) for k in pair]
        right = [jnp.where(iota((cap, 128), 0) == place[k : k + 1], 1.0, 0.0).astype(BF16) for k in pair]
        left, right = jnp.concatenate(left, axis=1), jnp.concatenate(right, axis=1)
        table += lax.dot_general(left, right, NT, preferred_element_type=F32)
    valid = table[7 * slabs : 8 * slabs]
    upper_part = jnp.where(valid > 0.5, table[:slabs], 64.0)
    lower_part = table[slabs : 2 * slabs]
    half = cap // 2
    for s in range(slabs):
        rows = [part[s : s + 1, q * half : (q + 1) * half] for part in (upper_part, lower_part) for q in range(2)]
        block = jnp.concatenate(rows + [jnp.zeros((EXT - 4, half), F32)], axis=0)
        ext_ref[s] = block.astype(BF16)
    row = lambda v: table[v * slabs : (v + 1) * slabs]
    node, scale = row(2) * 64.0 + row(3), row(4) + row(5) + row(6)
    empty = jnp.zeros((128 - 2 * slabs, cap), F32)
    pair_ref[...] = jnp.transpose(jnp.concatenate([node, scale, empty], axis=0))


def sum_scratch(parts, slabs, width):
    rows = width // parts
    dma = pltpu.SemaphoreType.DMA
    return [
        pltpu.VMEM((parts, rows, width), F32),
        pltpu.VMEM((parts - 1, rows, width), F32),
        pltpu.VMEM((slabs, 8, 128), F32),
        pltpu.VMEM((slabs - 1, 8, 128), F32),
        pltpu.VMEM((8, 128), F32),
        pltpu.VMEM((slabs, 8, 128), F32),
        pltpu.VMEM((rows, width), F32),
        pltpu.VMEM((parts, rows, width), F32),
        dma((parts - 1,)), dma((parts - 1,)),
        dma((slabs - 1,)), dma((slabs - 1,)),
        dma((slabs - 1,)), dma((slabs - 1,)),
        dma((parts - 1,)), dma((parts - 1,)),
    ]


def sum_stages(parts, slabs, factor, term_ref, out_ref, scratch):
    mine, in1, mid, in2, part, all2, done, all1, s1, r1, s2, r2, s3, r3, s4, r4 = scratch
    b, g = lax.axis_index("blk"), lax.axis_index("grp")
    rows = mine.shape[1]
    high = rows * 2 // slabs
    spots = [(slice(n // 2 * high, (n // 2 + 1) * high), slice(n % 2 * 128, n % 2 * 128 + 128)) for n in range(slabs)]
    flights = []

    def exchange(n, axis, me, src, dst, send, recv):
        copies = []
        for k in range(1, n):
            peer = lax.rem(me + k, n)
            copy = pltpu.make_async_remote_copy(
                src(peer), dst(k), send.at[k - 1], recv.at[k - 1], device_id={axis: peer}, device_id_type=MESH
            )
            copy.start()
            copies.append(copy)
        flights.append(copies)

    def landed():
        for copy in flights[-1]:
            copy.wait_recv()

    def split_blk():
        mid[...] = jnp.zeros_like(mid)
        for k in range(parts):
            mine[k] = term_ref[k * rows : (k + 1) * rows]
        exchange(parts, "blk", b, lambda p: mine.at[p], lambda k: in1.at[k - 1], s1, r1)

    def split_grp():
        landed()
        total = mine[b]
        for k in range(parts - 1):
            total += in1[k]
        for n in range(slabs):
            mid[n, :high] = total[spots[n]]
        exchange(slabs, "grp", g, lambda p: mid.at[p], lambda k: in2.at[k - 1], s2, r2)

    def join_grp():
        landed()
        piece = mid[g]
        for k in range(slabs - 1):
            piece += in2[k]
        part[...] = piece * factor
        all2[g] = piece * factor
        exchange(slabs, "grp", g, lambda p: part, lambda k: all2.at[g], s3, r3)

    def join_blk():
        landed()
        for n in range(slabs):
            done[spots[n]] = all2[n, :high]
        all1[b] = done[...]
        exchange(parts, "blk", b, lambda p: done, lambda k: all1.at[b], s4, r4)

    def finish():
        landed()
        for k in range(parts):
            out_ref[k * rows : (k + 1) * rows] = all1[k]
        for copies in flights:
            for copy in copies:
                copy.wait_send()

    return split_blk, split_grp, join_grp, join_blk, finish


def chip_scratch(parts, slabs):
    chips = parts * slabs // 2
    dma = pltpu.SemaphoreType.DMA
    return [
        pltpu.VMEM((chips, 8, 128), F32),
        pltpu.VMEM((chips - 1, 8, 128), F32),
        pltpu.VMEM((8, 128), F32),
        pltpu.VMEM((8, 128), F32),
        pltpu.VMEM((8, 128), F32),
        pltpu.VMEM((chips, 8, 128), F32),
        dma, dma, dma, dma, dma, dma,
    ]


def chip_peer(parts, slabs, k):
    b, g = lax.axis_index("blk"), lax.axis_index("grp")
    half = slabs // 2
    return (b + k // half) % parts, (g // 2 + k % half) % half, g % 2


def chip_stages(parts, slabs, factor, term_ref, out_ref, scratch):
    mine, come, part, pair, piece, whole, s1, r1, s2, r2, s3, r3 = scratch
    b, g = lax.axis_index("blk"), lax.axis_index("grp")
    half = slabs // 2
    chips = parts * half
    me = b * half + g // 2
    spots = [(slice(c // 2 * 8, c // 2 * 8 + 8), slice(c % 2 * 128, c % 2 * 128 + 128)) for c in range(chips)]
    many = pl.ds(0, chips - 1)
    other = pltpu.make_async_remote_copy(
        part, pair, s2, r2, device_id={"grp": g // 2 * 2 + 1 - g % 2}, device_id_type=MESH
    )

    def spread(src, dst, send, recv):
        def one(k, _):
            pb, pq, core = chip_peer(parts, slabs, k)
            pltpu.make_async_remote_copy(
                src(pb * half + pq), dst(k), send, recv,
                device_id={"blk": pb, "grp": pq * 2 + core}, device_id_type=MESH,
            ).start()
            return 0

        lax.fori_loop(1, chips, one, 0)

    def split():
        for c in range(chips):
            mine[c] = term_ref[spots[c]]
        spread(lambda c: mine.at[c], lambda k: come.at[k - 1], s1, r1)

    def cores():
        pltpu.make_async_copy(come, come, r1).wait()
        terms = [mine[me]] + [come[k] for k in range(chips - 1)]
        while len(terms) > 1:
            terms = [sum(terms[k : k + 2][1:], terms[k]) for k in range(0, len(terms), 2)]
        part[...] = terms[0]
        other.start()

    def join():
        other.wait_recv()
        piece[...] = (part[...] + pair[...]) * factor
        whole[me] = piece[...]
        spread(lambda c: piece, lambda k: whole.at[me], s3, r3)

    def finish():
        pltpu.make_async_copy(whole.at[many], whole.at[many], r3).wait()
        for c in range(chips):
            out_ref[spots[c]] = whole[c]
        pltpu.make_async_copy(come, come, s1).wait()
        other.wait_send()
        pltpu.make_async_copy(whole.at[many], whole.at[many], s3).wait()

    return split, cores, join, finish


def column_order(cols, early, order_ref):
    parts, picks = cols.shape
    count = parts * picks
    repeat = jnp.where(iota((picks, count), 1) % picks == iota((picks, count), 0), 1.0, 0.0).astype(BF16)
    wide = jnp.dot(cols.astype(F32).astype(BF16), repeat, preferred_element_type=F32)
    own = jnp.where(iota((parts, count), 1) // picks == iota((parts, count), 0), wide, 0.0)
    line = jnp.sum(own, axis=0, keepdims=True) + jnp.where(iota((1, count), 1) >= early, 32.0, 0.0)
    cols = jnp.broadcast_to(line, (count, count))
    across, down = iota((count, count), 1).astype(F32), iota((count, count), 0).astype(F32)
    turned = jnp.transpose(cols)
    ones = lambda hit: jnp.where(hit, 1.0, 0.0)
    total = lambda x: jnp.sum(x, axis=0, keepdims=True)
    rank = total(ones(turned * count + down < cols * count + across))
    ranks = jnp.transpose(jnp.broadcast_to(rank, (count, count)))
    hit = ones(ranks == across)
    order = total(hit * down)
    here = total(hit * turned)
    before = total(ones(ranks == across - 1.0) * (turned + 1.0)) - 1.0
    last = jnp.maximum(total(ones(turned <= across)) - 1.0, 0.0)
    named = jnp.minimum(total(ones(turned == across)), 1.0)
    rows = [order, ones(here == before), last, named, jnp.zeros((4, count), F32)]
    order_ref[...] = jnp.concatenate(rows, axis=0).astype(jnp.int32)


SPLIT = 80


def main_kernel(
    parts, slabs, factor,
    picks_ref, slab_ref, local_ref, remote_ref, weight_ref, cols_ref, w_ref, wm_ref, grad_hbm, pre_hbm, feats_hbm, tiles_hbm,
    out_hbm, out_msg_ref, out_upd_ref,
    pair_ref, ext_ref, out_buf, in_buf, grad_ref, pre_ref, acc_ref, slope_ref, gp_ref,
    near_ref, far_ref, side_ref, stage_a, stage_b, early_ref, late_ref,
    tiles_ref, run_ref, turned_ref, order_ref, order_smem, msg_ref, upd_ref,
    load_sem, tile_sem, rec_send, rec_recv, blk_send, blk_recv, store_sem, *scratch,
):
    b, g = lax.axis_index("blk"), lax.axis_index("grp")
    y, xh = b // 2, b % 2
    xl, z, core = g // 8, (g // 2) % 4, g % 2
    cap = pair_ref.shape[0]
    nodes, width = acc_ref.shape
    picks = stage_a.shape[1]

    load_grad = pltpu.make_async_copy(grad_hbm, grad_ref, load_sem.at[0])
    load_pre = pltpu.make_async_copy(pre_hbm, pre_ref, load_sem.at[1])
    load_feats = pltpu.make_async_copy(feats_hbm, pre_ref, load_sem.at[2])
    load_grad.start()
    load_pre.start()

    def rec_peer(n):
        q = n // 4
        dz, dx, dc = (n % 4 + 1) % 4, 1 - n // 8, (q + q // 2) % 2
        return ((xl + dx) % 2 * 4 + (z + dz) % 4) * 2 + (core + dc) % 2

    ring = parts // 2
    spot = lambda dy, dx: (y + dy) % ring * 2 + (xh + dx) % 2
    up, down, across, side = spot(1, 0), spot(ring - 1, 0), spot(2, 0), spot(0, 1)
    owners = (b, down, up, side, across, spot(ring - 1, 1), spot(1, 1), spot(2, 1))
    load_tiles = [
        pltpu.make_async_copy(
            tiles_hbm.at[pl.ds(r * picks, picks)], tiles_ref.at[pl.ds(k * picks, picks)], tile_sem.at[k]
        )
        for k, r in enumerate(owners)
    ]
    for load in load_tiles:
        load.start()

    barrier = pltpu.get_barrier_semaphore()
    for n in range(slabs - 1):
        pl.semaphore_signal(barrier, inc=1, device_id={"grp": rec_peer(n)}, device_id_type=MESH)
    for n in range(parts - 1):
        pl.semaphore_signal(barrier, inc=1, device_id={"blk": lax.rem(b + n + 1, parts)}, device_id_type=MESH)

    index_tables(slab_ref, local_ref, remote_ref, weight_ref, pair_ref, ext_ref)
    load_grad.wait()
    pl.semaphore_wait(barrier, slabs + parts - 2)

    def rec_copy(n):
        return pltpu.make_async_remote_copy(
            out_buf.at[n], in_buf.at[n], rec_send.at[n], rec_recv.at[n],
            device_id={"grp": rec_peer(n)}, device_id_type=MESH,
        )

    own = slabs - 1
    own_copy = pltpu.make_async_copy(out_buf.at[own], in_buf.at[own], rec_recv.at[own])
    wide = 1024

    def gather(n, _):
        s = rec_peer(n)
        lane = iota((cap, 128), 1)
        column = lambda at: jnp.sum(jnp.where(lane == at, pair_ref[...], 0.0), axis=1, keepdims=True)
        node = jnp.broadcast_to(column(s).astype(jnp.int32), (cap, 128))
        total = jnp.zeros((cap, width), F32)
        for k in range(nodes // wide):
            pieces = [
                jnp.where(node == iota((1, 128), 1) + (k * wide + j * 128), 1.0, 0.0).astype(BF16)
                for j in range(wide // 128)
            ]
            total += jnp.dot(
                jnp.concatenate(pieces, axis=1), grad_ref[k * wide : (k + 1) * wide], preferred_element_type=F32
            )
        out_buf[n, :cap] = (total * column(s + slabs)).astype(BF16)
        out_buf[n, cap:] = ext_ref[s]

        @pl.when(n < own)
        def _():
            rec_copy(n).start()

        return 0

    lax.fori_loop(0, slabs, gather, 0)
    own_copy.start()
    acc_ref[...] = grad_ref[...].astype(F32)
    load_pre.wait()

    def slopes(i, _):
        at = pl.ds(pl.multiple_of(i * 256, 256), 256)
        pre = pre_ref[at].astype(F32)
        sig = 1.0 / (1.0 + jnp.exp(-pre))
        slope_ref[at] = sig * (1.0 + pre * (1.0 - sig))
        turned_ref[i] = jnp.transpose((pre * sig).astype(BF16))
        return 0

    lax.fori_loop(0, nodes // 256, slopes, 0)
    load_feats.start()
    own_copy.wait()

    tall = 1024

    def scatter(m, _):
        n = (m + own) % slabs

        @pl.when(m > 0)
        def _():
            rec_copy(n).wait_recv()

        ext = in_buf[n, cap:].astype(F32)
        lane = lambda q: jnp.concatenate([ext[q : q + 1], ext[q + 1 : q + 2]], axis=1).astype(jnp.int32)
        high, low = lane(0), lane(2)
        base = jnp.where(iota((256, cap), 0) == low, 1.0, 0.0).astype(BF16).reshape(16, 16, cap)
        block = in_buf[n, :cap]
        for i in range(nodes // tall):
            pieces = []
            for c in range(i * tall // 256, (i + 1) * tall // 256):
                mask = jnp.where(jnp.broadcast_to(high, (16, cap)) == c, 1.0, 0.0).astype(BF16)
                pieces.append((base * mask[None]).reshape(256, cap))
            at = slice(i * tall, (i + 1) * tall)
            acc_ref[at] += jnp.dot(jnp.concatenate(pieces, axis=0), block, preferred_element_type=F32)
        return 0

    lax.fori_loop(0, slabs, scatter, 0)

    def finish(i, _):
        at = pl.ds(pl.multiple_of(i * 512, 512), 512)
        gradh = acc_ref[at].astype(BF16)
        grad_ref[at] = gradh
        back = lax.dot_general(gradh, w_ref[...], NT, preferred_element_type=F32)
        gp_ref[pl.ds(i * 4, 4)] = (back * slope_ref[at]).astype(BF16).reshape(4, 128, width)
        return 0

    copies = {}

    def send(m, src, dst, peer):
        copies[m] = pltpu.make_async_remote_copy(
            src, dst, blk_send.at[m], blk_recv.at[m], device_id={"blk": peer}, device_id_type=MESH
        )
        copies[m].start()

    panels = nodes // 128
    low, high = pl.ds(0, panels // 2), pl.ds(panels // 2, panels // 2)
    rows_a, rows_b = pl.ds(0, SPLIT), pl.ds(SPLIT, 128 - SPLIT)
    lax.fori_loop(0, nodes // 1024, finish, 0)
    send(0, gp_ref.at[low, rows_a], near_ref.at[0, low], up)
    lax.fori_loop(nodes // 1024, nodes // 512, finish, 0)
    send(1, gp_ref.at[high, rows_a], near_ref.at[1, high], down)
    send(4, gp_ref.at[:, rows_b], side_ref, side)
    send(2, gp_ref.at[high, rows_a], near_ref.at[0, high], up)
    send(3, gp_ref.at[low, rows_a], near_ref.at[1, low], down)
    def pack(store, load, c, r):
        def one(t, _):
            store(t, load(picks_ref[c, r, t]))
            return 0

        lax.fori_loop(0, picks, one, 0, unroll=4)

    def to_stage(ref, n):
        def store(t, value):
            ref[n, t] = value

        return store

    def to_early(slot, rows):
        def store(t, value):
            early_ref[slot * picks + t, rows] = value

        return store

    top, rest, whole = slice(0, SPLIT), slice(SPLIT, 128), slice(0, 128)
    place = lambda ref, slot, rows: ref.at[pl.ds(slot * picks, picks), rows]
    near = [lambda i: near_ref[0, i], lambda i: near_ref[1, i]]
    pack(to_stage(stage_a, 0), lambda i: gp_ref[i, top], side, b)
    send(5, stage_a.at[0], place(early_ref, 3, rows_a), side)
    copies[0].wait_recv()
    copies[1].wait_recv()
    send(6, near_ref.at[0, low], far_ref.at[low], up)
    send(7, near_ref.at[1, high], far_ref.at[high], down)
    for n, peer in enumerate((up, down, across)):
        pack(to_stage(stage_b, n), lambda i: gp_ref[i, rest], peer, b)
        send(8 + n, stage_b.at[n], place(early_ref, (1, 2, 4)[n], rows_b), peer)
    copies[2].wait_recv()
    copies[3].wait_recv()
    for n, r in enumerate((down, up)):
        pack(to_stage(stage_a, 1 + n), near[n], side, r)
        send(11 + n, stage_a.at[1 + n], place(late_ref, n, rows_a), side)
    copies[4].wait_recv()
    for n, peer in enumerate((up, down, across)):
        pack(to_stage(stage_b, 3 + n), lambda i: side_ref[i], peer, side)
        send(13 + n, stage_b.at[3 + n], place(late_ref, n, rows_b), peer)
    pack(to_early(0, whole), lambda i: gp_ref[i], b, b)
    pack(to_early(1, top), near[0], b, down)
    pack(to_early(2, top), near[1], b, up)
    pack(to_early(3, rest), lambda i: side_ref[i], b, side)

    cols = jnp.concatenate([cols_ref[pl.ds(r, 1)] for r in owners], axis=0)
    early = 5 * picks
    column_order(cols, early, order_ref)
    to_smem = pltpu.make_async_copy(order_ref, order_smem, store_sem.at[0])
    to_smem.start()
    for load in load_tiles:
        load.wait()
    tiles = parts * picks

    def turn(k, _):
        tiles_ref[k] = jnp.transpose(tiles_ref[k])
        return 0

    lax.fori_loop(0, tiles, turn, 0, unroll=4)
    copies[6].wait_recv()
    copies[7].wait_recv()
    pack(to_stage(stage_a, 3), lambda i: far_ref[i], side, across)
    send(16, stage_a.at[3], place(late_ref, 2, rows_a), side)
    pack(to_early(4, top), lambda i: far_ref[i], b, across)

    upd_ref[...] = jnp.zeros_like(upd_ref)

    def update(i, _):
        at = pl.ds(pl.multiple_of(i * 256, 256), 256)
        upd_ref[...] += jnp.dot(turned_ref[i], grad_ref[at], preferred_element_type=F32)
        return 0

    lax.fori_loop(0, nodes // 256, update, 0)
    load_feats.wait()

    def turn_feats(k, _):
        at = pl.ds(pl.multiple_of(k * 256, 256), 256)
        turned_ref[k] = jnp.transpose(pre_ref[at])
        return 0

    lax.fori_loop(0, nodes // 256, turn_feats, 0)
    to_smem.wait()
    lax.fori_loop(0, slabs - 1, lambda n, x: (rec_copy(n).wait_send(), x)[1], 0)
    group = 8

    def products(ref, start, size):
        def step(m, total):
            for q in range(group):
                k = m * group + q
                f = lax.clamp(start, order_smem[0, k], start + size - 1)
                part = jnp.dot(tiles_ref[f], ref[f - start], preferred_element_type=F32)
                total = total * order_smem[1, k].astype(F32) + part
                run_ref[k] = total.astype(BF16)
            return total

        lax.fori_loop(start // group, (start + size) // group, step, jnp.zeros((128, width), F32))

    for m in (5, 8, 9, 10):
        copies[m].wait_recv()
    products(early_ref, 0, early)
    count = len(sum_scratch(parts, slabs, width))
    upd_sum = sum_stages(parts, slabs, factor, upd_ref, out_upd_ref, scratch[:count])
    msg_sum = chip_stages(parts, slabs, factor, msg_ref, out_msg_ref, scratch[count:])
    upd_sum[0]()
    for m in (11, 12, 13, 14, 15, 16):
        copies[m].wait_recv()
    upd_sum[1]()
    products(late_ref, early, tiles - early)
    for m in range(len(copies)):
        copies[m].wait_send()

    def settle(j, _):
        piece = lambda k: run_ref[lax.clamp(0, order_smem[2, k], tiles - 1)].astype(F32) * order_smem[3, k].astype(F32)
        gp_ref[j] = (piece(j) + piece(j + panels)).astype(BF16)
        return 0

    lax.fori_loop(0, panels, settle, 0, unroll=4)
    upd_sum[2]()
    msg = jnp.zeros((width, width), F32)
    for k in range(nodes // 256):
        msg += jnp.dot(turned_ref[k], gp_ref[2 * k : 2 * k + 2].reshape(256, width), preferred_element_type=F32)
    msg_ref[...] = msg
    msg_sum[0]()

    def features(i, _):
        at = pl.ds(pl.multiple_of(i * 512, 512), 512)
        spread = gp_ref[pl.ds(i * 4, 4)].reshape(512, width)
        below = lax.dot_general(spread, wm_ref[...], NT, preferred_element_type=F32)
        pre_ref[at] = (grad_ref[at].astype(F32) + below).astype(BF16)
        return 0

    lax.fori_loop(0, nodes // 512, features, 0)
    store_out = pltpu.make_async_copy(pre_ref, out_hbm, store_sem.at[1])
    store_out.start()
    msg_sum[1]()
    upd_sum[3]()
    msg_sum[2]()
    msg_sum[3]()
    upd_sum[4]()
    store_out.wait()


def main_step(
    picks, slab, local, remote, weight, cols, w_update, w_message, grad, pre, feats, tiles, slabs, parts, cap, factor
):
    nodes, width = grad.shape
    count = picks.shape[-1]
    panels, early = nodes // 128, 5 * count
    vmem = pl.BlockSpec(memory_space=pltpu.VMEM)
    hbm = pl.BlockSpec(memory_space=pl.ANY)
    dma = pltpu.SemaphoreType.DMA
    square = jax.ShapeDtypeStruct((width, width), F32)
    return pl.pallas_call(
        functools.partial(main_kernel, parts, slabs, factor),
        out_shape=[jax.ShapeDtypeStruct((nodes, width), BF16), square, square],
        in_specs=[pl.BlockSpec(memory_space=pltpu.SMEM)] + [vmem] * 7 + [hbm] * 4,
        out_specs=[hbm, vmem, vmem],
        scratch_shapes=[
            pltpu.VMEM((cap, 128), F32),
            pltpu.VMEM((slabs, EXT, width), BF16),
            pltpu.VMEM((slabs, cap + EXT, width), BF16),
            pltpu.VMEM((slabs, cap + EXT, width), BF16),
            pltpu.VMEM((nodes, width), BF16),
            pltpu.VMEM((nodes, width), BF16),
            pltpu.VMEM((nodes, width), F32),
            pltpu.VMEM((nodes, width), F32),
            pltpu.VMEM((panels, 128, width), BF16),
            pltpu.VMEM((2, panels, SPLIT, width), BF16),
            pltpu.VMEM((panels, SPLIT, width), BF16),
            pltpu.VMEM((panels, 128 - SPLIT, width), BF16),
            pltpu.VMEM((4, count, SPLIT, width), BF16),
            pltpu.VMEM((6, count, 128 - SPLIT, width), BF16),
            pltpu.VMEM((early, 128, width), BF16),
            pltpu.VMEM((parts * count - early, 128, width), BF16),
            pltpu.VMEM((parts * count, 128, 128), BF16),
            pltpu.VMEM((parts * count, 128, width), BF16),
            pltpu.VMEM((nodes // 256, width, 256), BF16),
            pltpu.VMEM((8, parts * count), jnp.int32),
            pltpu.SMEM((8, parts * count), jnp.int32),
            pltpu.VMEM((width, width), F32),
            pltpu.VMEM((width, width), F32),
            dma((3,)), dma((parts,)), dma((slabs - 1,)), dma((slabs,)), dma((17,)), dma((17,)), dma((2,)),
        ]
        + sum_scratch(parts, slabs, width)
        + chip_scratch(parts, slabs),
        compiler_params=pltpu.CompilerParams(collective_id=0, has_side_effects=True, vmem_limit_bytes=VMEM_LIMIT),
        name="main_step",
    )(picks, slab, local, remote, weight, cols, w_update, w_message, grad, pre, feats, tiles)


def final_kernel(out_ref, msg_ref, upd_ref, to_out_ref, to_msg_ref, to_upd_ref, out_buf, msg_buf, upd_buf, come, go):
    steps = 4
    rows = out_ref.shape[0] // steps
    ways = [(msg_ref, msg_buf, to_msg_ref), (upd_ref, upd_buf, to_upd_ref)]
    for k in range(steps):
        at = pl.ds(k * rows, rows)
        ways.append((out_ref.at[at], out_buf.at[at], to_out_ref.at[at]))
    loads = [pltpu.make_async_copy(src, buf, come.at[k]) for k, (src, buf, _) in enumerate(ways)]
    stores = [pltpu.make_async_copy(buf, dst, go.at[k]) for k, (_, buf, dst) in enumerate(ways)]
    for load in loads:
        load.start()
    for load, store in zip(loads, stores):
        load.wait()
        store.start()
    for store in stores:
        store.wait()


def final_step(out, msg, upd):
    hbm = pl.BlockSpec(memory_space=pl.ANY)
    args = (out, msg, upd)
    return pl.pallas_call(
        final_kernel,
        out_shape=[jax.ShapeDtypeStruct(a.shape, a.dtype) for a in args],
        in_specs=[hbm] * 3,
        out_specs=[hbm] * 3,
        scratch_shapes=[pltpu.VMEM(a.shape, a.dtype) for a in args] + [pltpu.SemaphoreType.DMA((6,))] * 2,
        compiler_params=pltpu.CompilerParams(vmem_limit_bytes=VMEM_LIMIT),
        name="final_step",
    )(*args)


def local(
    grad_out, pre_act, node_feats, w_message, w_update, tile_vals, tile_rows, tile_cols,
    rec_slab, rec_local, rec_remote, rec_weight,
):
    grad = grad_out[0]
    rows, width = grad.shape
    slabs = lax.axis_size("grp")
    parts = lax.axis_size("blk")
    records = rec_local.shape[1]
    cap = 2 * records // slabs
    factor = float((slabs * parts * rows) ** -0.5)
    lanes = lambda a: a.reshape(records // 128, 128)
    tiles = tile_vals[0, 0]
    count = tiles.shape[0] * tiles.shape[1]
    out, msg, upd = main_step(
        tile_rows[0], lanes(rec_slab), lanes(rec_local), lanes(rec_remote), lanes(rec_weight),
        tile_cols[0, 0], w_update, w_message, grad, pre_act[0], node_feats[0],
        tiles.reshape(count, *tiles.shape[2:]), slabs, parts, cap, factor,
    )
    feats, msg, upd = final_step(out, msg, upd)
    return (feats[None], msg, upd)


def solution(mesh):
    placed = (
        P("grp", "blk", None),
        P("grp", "blk", None),
        P("grp", "blk", None),
        P(),
        P(),
        P("grp", "blk", None, None, None, None),
        P("grp", None, None, None),
        P("grp", "blk", None, None),
        P("grp", "blk", None),
        P("grp", "blk"),
        P("grp", "blk"),
        P("grp", "blk"),
    )
    return jax.shard_map(
        local,
        mesh=mesh,
        in_specs=placed,
        out_specs=(P("grp", "blk", None), P(), P()),
        check_vma=False,
    )
```

```python
import functools

import jax
import jax.numpy as jnp
from jax import lax
from jax.experimental import pallas as pl
from jax.experimental.pallas import tpu as pltpu
from jax.sharding import PartitionSpec as P

F32 = jnp.float32
BF16 = jnp.bfloat16
MESH = pl.DeviceIdType.MESH
NT = (((1,), (1,)), ((), ()))
TN = (((0,), (0,)), ((), ()))
EXT = 16
VMEM_LIMIT = 61 * 1024 * 1024


def iota(shape, dim):
    return lax.broadcasted_iota(jnp.int32, shape, dim)


def index_tables(slab_ref, local_ref, remote_ref, weight_ref, pair_ref, ext_ref):
    slabs, cap = ext_ref.shape[0], pair_ref.shape[0]
    chunks = slab_ref.shape[0]
    slab = slab_ref[...]
    ids = iota((chunks, slabs, 128), 1)
    choose = jnp.where(ids == slab[:, None, :], 1.0, 0.0)
    flat = choose.reshape(chunks * slabs, 128)
    flat16 = flat.astype(BF16)
    upper = jnp.where(iota((128, 128), 0) < iota((128, 128), 1), 1.0, 0.0).astype(BF16)
    prefix = jnp.dot(flat16, upper, preferred_element_type=F32)
    totals = jnp.dot(flat16, jnp.ones((128, 128), BF16), preferred_element_type=F32)
    size = chunks * slabs
    row, col = iota((size, size), 0), iota((size, size), 1)
    earlier = (col < row) & (lax.rem(col, slabs) == lax.rem(row, slabs))
    offset = jnp.dot(jnp.where(earlier, 1.0, 0.0).astype(BF16), totals.astype(BF16), preferred_element_type=F32)
    place = ((prefix + offset) * flat).reshape(chunks, slabs, 128).sum(axis=1).astype(jnp.int32)
    remote, local, weight = remote_ref[...], local_ref[...], weight_ref[...]
    first = weight.astype(BF16).astype(F32)
    second = (weight - first).astype(BF16).astype(F32)
    third = weight - first - second
    values = [
        (remote // 256).astype(F32),
        (remote % 256).astype(F32),
        (local // 64).astype(F32),
        (local % 64).astype(F32),
        first,
        second,
        third,
        jnp.ones_like(weight),
    ]
    table = jnp.zeros((len(values) * slabs, cap), F32)
    for c in range(chunks):
        left = jnp.concatenate([choose[c] * v[c : c + 1] for v in values], axis=0).astype(BF16)
        right = jnp.where(iota((cap, 128), 0) == place[c : c + 1], 1.0, 0.0).astype(BF16)
        table += lax.dot_general(left, right, NT, preferred_element_type=F32)
    valid = table[7 * slabs : 8 * slabs]
    upper_part = jnp.where(valid > 0.5, table[:slabs], 64.0)
    lower_part = table[slabs : 2 * slabs]
    half = cap // 2
    for s in range(slabs):
        rows = [part[s : s + 1, q * half : (q + 1) * half] for part in (upper_part, lower_part) for q in range(2)]
        block = jnp.concatenate(rows + [jnp.zeros((EXT - 4, half), F32)], axis=0)
        ext_ref[s] = block.astype(BF16)
    row = lambda v: table[v * slabs : (v + 1) * slabs]
    node, scale = row(2) * 64.0 + row(3), row(4) + row(5) + row(6)
    empty = jnp.zeros((128 - 2 * slabs, cap), F32)
    pair_ref[...] = jnp.transpose(jnp.concatenate([node, scale, empty], axis=0))


def sum_scratch(parts, slabs, width):
    rows = width // parts
    dma = pltpu.SemaphoreType.DMA
    return [
        pltpu.VMEM((parts, rows, width), F32),
        pltpu.VMEM((parts - 1, rows, width), F32),
        pltpu.VMEM((slabs, 8, 128), F32),
        pltpu.VMEM((slabs - 1, 8, 128), F32),
        pltpu.VMEM((8, 128), F32),
        pltpu.VMEM((slabs, 8, 128), F32),
        pltpu.VMEM((rows, width), F32),
        pltpu.VMEM((parts, rows, width), F32),
        dma((parts - 1,)), dma((parts - 1,)),
        dma((slabs - 1,)), dma((slabs - 1,)),
        dma((slabs - 1,)), dma((slabs - 1,)),
        dma((parts - 1,)), dma((parts - 1,)),
    ]


def sum_stages(parts, slabs, factor, term_ref, out_ref, scratch):
    mine, in1, mid, in2, part, all2, done, all1, s1, r1, s2, r2, s3, r3, s4, r4 = scratch
    b, g = lax.axis_index("blk"), lax.axis_index("grp")
    rows = mine.shape[1]
    high = rows * 2 // slabs
    spots = [(slice(n // 2 * high, (n // 2 + 1) * high), slice(n % 2 * 128, n % 2 * 128 + 128)) for n in range(slabs)]
    flights = []

    def exchange(n, axis, me, src, dst, send, recv):
        copies = []
        for k in range(1, n):
            peer = lax.rem(me + k, n)
            copy = pltpu.make_async_remote_copy(
                src(peer), dst(k), send.at[k - 1], recv.at[k - 1], device_id={axis: peer}, device_id_type=MESH
            )
            copy.start()
            copies.append(copy)
        flights.append(copies)

    def landed():
        for copy in flights[-1]:
            copy.wait_recv()

    def split_blk():
        mid[...] = jnp.zeros_like(mid)
        for k in range(parts):
            mine[k] = term_ref[k * rows : (k + 1) * rows]
        exchange(parts, "blk", b, lambda p: mine.at[p], lambda k: in1.at[k - 1], s1, r1)

    def split_grp():
        landed()
        total = mine[b]
        for k in range(parts - 1):
            total += in1[k]
        for n in range(slabs):
            mid[n, :high] = total[spots[n]]
        exchange(slabs, "grp", g, lambda p: mid.at[p], lambda k: in2.at[k - 1], s2, r2)

    def join_grp():
        landed()
        piece = mid[g]
        for k in range(slabs - 1):
            piece += in2[k]
        part[...] = piece * factor
        all2[g] = piece * factor
        exchange(slabs, "grp", g, lambda p: part, lambda k: all2.at[g], s3, r3)

    def join_blk():
        landed()
        for n in range(slabs):
            done[spots[n]] = all2[n, :high]
        all1[b] = done[...]
        exchange(parts, "blk", b, lambda p: done, lambda k: all1.at[b], s4, r4)

    def finish():
        landed()
        for k in range(parts):
            out_ref[k * rows : (k + 1) * rows] = all1[k]
        for copies in flights:
            for copy in copies:
                copy.wait_send()

    return split_blk, split_grp, join_grp, join_blk, finish


def chip_scratch(parts, slabs):
    chips = parts * slabs // 2
    dma = pltpu.SemaphoreType.DMA
    return [
        pltpu.VMEM((chips, 8, 128), F32),
        pltpu.VMEM((chips - 1, 8, 128), F32),
        pltpu.VMEM((8, 128), F32),
        pltpu.VMEM((8, 128), F32),
        pltpu.VMEM((8, 128), F32),
        pltpu.VMEM((chips, 8, 128), F32),
        dma, dma, dma, dma, dma, dma,
    ]


def chip_peer(parts, slabs, k):
    b, g = lax.axis_index("blk"), lax.axis_index("grp")
    half = slabs // 2
    return (b + k // half) % parts, (g // 2 + k % half) % half, g % 2


def chip_stages(parts, slabs, factor, term_ref, out_ref, scratch):
    mine, come, part, pair, piece, whole, s1, r1, s2, r2, s3, r3 = scratch
    b, g = lax.axis_index("blk"), lax.axis_index("grp")
    half = slabs // 2
    chips = parts * half
    me = b * half + g // 2
    spots = [(slice(c // 2 * 8, c // 2 * 8 + 8), slice(c % 2 * 128, c % 2 * 128 + 128)) for c in range(chips)]
    many = pl.ds(0, chips - 1)
    other = pltpu.make_async_remote_copy(
        part, pair, s2, r2, device_id={"grp": g // 2 * 2 + 1 - g % 2}, device_id_type=MESH
    )

    def spread(src, dst, send, recv):
        def one(k, _):
            pb, pq, core = chip_peer(parts, slabs, k)
            pltpu.make_async_remote_copy(
                src(pb * half + pq), dst(k), send, recv,
                device_id={"blk": pb, "grp": pq * 2 + core}, device_id_type=MESH,
            ).start()
            return 0

        lax.fori_loop(1, chips, one, 0)

    def split():
        for c in range(chips):
            mine[c] = term_ref[spots[c]]
        spread(lambda c: mine.at[c], lambda k: come.at[k - 1], s1, r1)

    def cores():
        pltpu.make_async_copy(come, come, r1).wait()
        terms = [mine[me]] + [come[k] for k in range(chips - 1)]
        while len(terms) > 1:
            terms = [sum(terms[k : k + 2][1:], terms[k]) for k in range(0, len(terms), 2)]
        part[...] = terms[0]
        other.start()

    def join():
        other.wait_recv()
        piece[...] = (part[...] + pair[...]) * factor
        whole[me] = piece[...]
        spread(lambda c: piece, lambda k: whole.at[me], s3, r3)

    def finish():
        pltpu.make_async_copy(whole.at[many], whole.at[many], r3).wait()
        for c in range(chips):
            out_ref[spots[c]] = whole[c]
        pltpu.make_async_copy(come, come, s1).wait()
        other.wait_send()
        pltpu.make_async_copy(whole.at[many], whole.at[many], s3).wait()

    return split, cores, join, finish


def column_order(cols, early, order_ref):
    parts, picks = cols.shape
    count = parts * picks
    repeat = jnp.where(iota((picks, count), 1) % picks == iota((picks, count), 0), 1.0, 0.0).astype(BF16)
    wide = jnp.dot(cols.astype(F32).astype(BF16), repeat, preferred_element_type=F32)
    own = jnp.where(iota((parts, count), 1) // picks == iota((parts, count), 0), wide, 0.0)
    line = jnp.sum(own, axis=0, keepdims=True) + jnp.where(iota((1, count), 1) >= early, 32.0, 0.0)
    cols = jnp.broadcast_to(line, (count, count))
    across, down = iota((count, count), 1).astype(F32), iota((count, count), 0).astype(F32)
    turned = jnp.transpose(cols)
    ones = lambda hit: jnp.where(hit, 1.0, 0.0)
    total = lambda x: jnp.sum(x, axis=0, keepdims=True)
    rank = total(ones(turned * count + down < cols * count + across))
    ranks = jnp.transpose(jnp.broadcast_to(rank, (count, count)))
    hit = ones(ranks == across)
    order = total(hit * down)
    here = total(hit * turned)
    before = total(ones(ranks == across - 1.0) * (turned + 1.0)) - 1.0
    last = jnp.maximum(total(ones(turned <= across)) - 1.0, 0.0)
    named = jnp.minimum(total(ones(turned == across)), 1.0)
    rows = [order, ones(here == before), last, named, jnp.zeros((4, count), F32)]
    order_ref[...] = jnp.concatenate(rows, axis=0).astype(jnp.int32)


SPLIT = 80


def main_kernel(
    parts, slabs, factor,
    picks_ref, slab_ref, local_ref, remote_ref, weight_ref, cols_ref, w_ref, wm_ref, grad_hbm, pre_hbm, feats_hbm, tiles_hbm,
    out_hbm, out_msg_ref, out_upd_ref,
    pair_ref, ext_ref, out_buf, in_buf, grad_ref, pre_ref, acc_ref, slope_ref, gp_ref,
    near_ref, far_ref, side_ref, stage_a, stage_b, early_ref, late_ref,
    tiles_ref, run_ref, turned_ref, order_ref, order_smem, msg_ref, upd_ref,
    load_sem, tile_sem, rec_send, rec_recv, blk_send, blk_recv, store_sem, *scratch,
):
    b, g = lax.axis_index("blk"), lax.axis_index("grp")
    y, xh = b // 2, b % 2
    xl, z, core = g // 8, (g // 2) % 4, g % 2
    cap = pair_ref.shape[0]
    nodes, width = acc_ref.shape
    picks = stage_a.shape[1]

    load_grad = pltpu.make_async_copy(grad_hbm, grad_ref, load_sem.at[0])
    load_pre = pltpu.make_async_copy(pre_hbm, pre_ref, load_sem.at[1])
    load_feats = pltpu.make_async_copy(feats_hbm, pre_ref, load_sem.at[2])
    load_grad.start()
    load_pre.start()

    def rec_peer(n):
        q = n // 4
        dz, dx, dc = (2 + 3 * q + 3 * (q // 2) + 2 * (q // 3)) % 4, 1 - n % 4 // 2, 1 - n % 2
        return ((xl + dx) % 2 * 4 + (z + dz) % 4) * 2 + (core + dc) % 2

    ring = parts // 2
    spot = lambda dy, dx: (y + dy) % ring * 2 + (xh + dx) % 2
    up, down, across, side = spot(1, 0), spot(ring - 1, 0), spot(2, 0), spot(0, 1)
    owners = (b, down, up, side, across, spot(ring - 1, 1), spot(1, 1), spot(2, 1))
    load_tiles = [
        pltpu.make_async_copy(
            tiles_hbm.at[pl.ds(r * picks, picks)], tiles_ref.at[pl.ds(k * picks, picks)], tile_sem.at[k]
        )
        for k, r in enumerate(owners)
    ]
    for load in load_tiles:
        load.start()

    barrier = pltpu.get_barrier_semaphore()
    for n in range(slabs - 1):
        pl.semaphore_signal(barrier, inc=1, device_id={"grp": rec_peer(n)}, device_id_type=MESH)
    for n in range(parts - 1):
        pl.semaphore_signal(barrier, inc=1, device_id={"blk": lax.rem(b + n + 1, parts)}, device_id_type=MESH)

    index_tables(slab_ref, local_ref, remote_ref, weight_ref, pair_ref, ext_ref)
    load_grad.wait()
    pl.semaphore_wait(barrier, slabs + parts - 2)

    def rec_copy(n):
        return pltpu.make_async_remote_copy(
            out_buf.at[n], in_buf.at[n], rec_send.at[n], rec_recv.at[n],
            device_id={"grp": rec_peer(n)}, device_id_type=MESH,
        )

    own = slabs - 1
    own_copy = pltpu.make_async_copy(out_buf.at[own], in_buf.at[own], rec_recv.at[own])
    wide = 1024

    def gather(n, _):
        s = rec_peer(n)
        lane = iota((cap, 128), 1)
        column = lambda at: jnp.sum(jnp.where(lane == at, pair_ref[...], 0.0), axis=1, keepdims=True)
        node = jnp.broadcast_to(column(s).astype(jnp.int32), (cap, 128))
        total = jnp.zeros((cap, width), F32)
        for k in range(nodes // wide):
            pieces = [
                jnp.where(node == iota((1, 128), 1) + (k * wide + j * 128), 1.0, 0.0).astype(BF16)
                for j in range(wide // 128)
            ]
            total += jnp.dot(
                jnp.concatenate(pieces, axis=1), grad_ref[k * wide : (k + 1) * wide], preferred_element_type=F32
            )
        out_buf[n, :cap] = (total * column(s + slabs)).astype(BF16)
        out_buf[n, cap:] = ext_ref[s]

        @pl.when(n < own)
        def _():
            rec_copy(n).start()

        return 0

    lax.fori_loop(0, slabs, gather, 0)
    own_copy.start()
    acc_ref[...] = grad_ref[...].astype(F32)
    load_pre.wait()

    def slopes(i, _):
        at = pl.ds(pl.multiple_of(i * 256, 256), 256)
        pre = pre_ref[at].astype(F32)
        sig = 1.0 / (1.0 + jnp.exp(-pre))
        slope_ref[at] = sig * (1.0 + pre * (1.0 - sig))
        turned_ref[i] = jnp.transpose((pre * sig).astype(BF16))
        return 0

    lax.fori_loop(0, nodes // 256, slopes, 0)
    load_feats.start()
    own_copy.wait()

    tall = 1024

    def scatter(m, _):
        n = (m + own) % slabs

        @pl.when(m > 0)
        def _():
            rec_copy(n).wait_recv()

        ext = in_buf[n, cap:].astype(F32)
        lane = lambda q: jnp.concatenate([ext[q : q + 1], ext[q + 1 : q + 2]], axis=1).astype(jnp.int32)
        high, low = lane(0), lane(2)
        base = jnp.where(iota((256, cap), 0) == low, 1.0, 0.0).astype(BF16).reshape(16, 16, cap)
        block = in_buf[n, :cap]
        for i in range(nodes // tall):
            pieces = []
            for c in range(i * tall // 256, (i + 1) * tall // 256):
                mask = jnp.where(jnp.broadcast_to(high, (16, cap)) == c, 1.0, 0.0).astype(BF16)
                pieces.append((base * mask[None]).reshape(256, cap))
            at = slice(i * tall, (i + 1) * tall)
            acc_ref[at] += jnp.dot(jnp.concatenate(pieces, axis=0), block, preferred_element_type=F32)
        return 0

    lax.fori_loop(0, slabs, scatter, 0)

    def finish(i, _):
        at = pl.ds(pl.multiple_of(i * 512, 512), 512)
        gradh = acc_ref[at].astype(BF16)
        grad_ref[at] = gradh
        back = lax.dot_general(gradh, w_ref[...], NT, preferred_element_type=F32)
        gp_ref[pl.ds(i * 4, 4)] = (back * slope_ref[at]).astype(BF16).reshape(4, 128, width)
        return 0

    copies = {}

    def send(m, src, dst, peer):
        copies[m] = pltpu.make_async_remote_copy(
            src, dst, blk_send.at[m], blk_recv.at[m], device_id={"blk": peer}, device_id_type=MESH
        )
        copies[m].start()

    panels = nodes // 128
    low, high = pl.ds(0, panels // 2), pl.ds(panels // 2, panels // 2)
    rows_a, rows_b = pl.ds(0, SPLIT), pl.ds(SPLIT, 128 - SPLIT)
    lax.fori_loop(0, nodes // 1024, finish, 0)
    send(0, gp_ref.at[low, rows_a], near_ref.at[0, low], up)
    lax.fori_loop(nodes // 1024, nodes // 512, finish, 0)
    send(1, gp_ref.at[high, rows_a], near_ref.at[1, high], down)
    send(4, gp_ref.at[:, rows_b], side_ref, side)
    send(2, gp_ref.at[high, rows_a], near_ref.at[0, high], up)
    send(3, gp_ref.at[low, rows_a], near_ref.at[1, low], down)
    def pack(store, load, c, r):
        def one(t, _):
            store(t, load(picks_ref[c, r, t]))
            return 0

        lax.fori_loop(0, picks, one, 0)

    def to_stage(ref, n):
        def store(t, value):
            ref[n, t] = value

        return store

    def to_early(slot, rows):
        def store(t, value):
            early_ref[slot * picks + t, rows] = value

        return store

    top, rest, whole = slice(0, SPLIT), slice(SPLIT, 128), slice(0, 128)
    place = lambda ref, slot, rows: ref.at[pl.ds(slot * picks, picks), rows]
    near = [lambda i: near_ref[0, i], lambda i: near_ref[1, i]]
    pack(to_stage(stage_a, 0), lambda i: gp_ref[i, top], side, b)
    send(5, stage_a.at[0], place(early_ref, 3, rows_a), side)
    copies[0].wait_recv()
    copies[1].wait_recv()
    send(6, near_ref.at[0, low], far_ref.at[low], up)
    send(7, near_ref.at[1, high], far_ref.at[high], down)
    for n, peer in enumerate((up, down, across)):
        pack(to_stage(stage_b, n), lambda i: gp_ref[i, rest], peer, b)
        send(8 + n, stage_b.at[n], place(early_ref, (1, 2, 4)[n], rows_b), peer)
    copies[2].wait_recv()
    copies[3].wait_recv()
    for n, r in enumerate((down, up)):
        pack(to_stage(stage_a, 1 + n), near[n], side, r)
        send(11 + n, stage_a.at[1 + n], place(late_ref, n, rows_a), side)
    copies[4].wait_recv()
    for n, peer in enumerate((up, down, across)):
        pack(to_stage(stage_b, 3 + n), lambda i: side_ref[i], peer, side)
        send(13 + n, stage_b.at[3 + n], place(late_ref, n, rows_b), peer)
    pack(to_early(0, whole), lambda i: gp_ref[i], b, b)
    pack(to_early(1, top), near[0], b, down)
    pack(to_early(2, top), near[1], b, up)
    pack(to_early(3, rest), lambda i: side_ref[i], b, side)

    cols = jnp.concatenate([cols_ref[pl.ds(r, 1)] for r in owners], axis=0)
    early = 5 * picks
    column_order(cols, early, order_ref)
    to_smem = pltpu.make_async_copy(order_ref, order_smem, store_sem.at[0])
    to_smem.start()
    for load in load_tiles:
        load.wait()
    tiles = parts * picks

    def turn(k, _):
        tiles_ref[k] = jnp.transpose(tiles_ref[k])
        return 0

    lax.fori_loop(0, tiles, turn, 0)
    copies[6].wait_recv()
    copies[7].wait_recv()
    pack(to_stage(stage_a, 3), lambda i: far_ref[i], side, across)
    send(16, stage_a.at[3], place(late_ref, 2, rows_a), side)
    pack(to_early(4, top), lambda i: far_ref[i], b, across)

    upd_ref[...] = jnp.zeros_like(upd_ref)

    def update(i, _):
        at = pl.ds(pl.multiple_of(i * 256, 256), 256)
        upd_ref[...] += jnp.dot(turned_ref[i], grad_ref[at], preferred_element_type=F32)
        return 0

    lax.fori_loop(0, nodes // 256, update, 0)
    load_feats.wait()

    def turn_feats(k, _):
        at = pl.ds(pl.multiple_of(k * 256, 256), 256)
        turned_ref[k] = jnp.transpose(pre_ref[at])
        return 0

    lax.fori_loop(0, nodes // 256, turn_feats, 0)
    to_smem.wait()
    lax.fori_loop(0, slabs - 1, lambda n, x: (rec_copy(n).wait_send(), x)[1], 0)
    group = 8

    def products(ref, start, size):
        def step(m, total):
            for q in range(group):
                k = m * group + q
                f = lax.clamp(start, order_smem[0, k], start + size - 1)
                part = jnp.dot(tiles_ref[f], ref[f - start], preferred_element_type=F32)
                total = total * order_smem[1, k].astype(F32) + part
                run_ref[k] = total.astype(BF16)
            return total

        lax.fori_loop(start // group, (start + size) // group, step, jnp.zeros((128, width), F32))

    for m in (5, 8, 9, 10):
        copies[m].wait_recv()
    products(early_ref, 0, early)
    count = len(sum_scratch(parts, slabs, width))
    upd_sum = sum_stages(parts, slabs, factor, upd_ref, out_upd_ref, scratch[:count])
    msg_sum = chip_stages(parts, slabs, factor, msg_ref, out_msg_ref, scratch[count:])
    for m in (11, 12, 13, 14, 15, 16):
        copies[m].wait_recv()
    upd_sum[0]()
    products(late_ref, early, tiles - early)
    for m in range(len(copies)):
        copies[m].wait_send()

    def settle(j, _):
        piece = lambda k: run_ref[lax.clamp(0, order_smem[2, k], tiles - 1)].astype(F32) * order_smem[3, k].astype(F32)
        gp_ref[j] = (piece(j) + piece(j + panels)).astype(BF16)
        return 0

    lax.fori_loop(0, panels, settle, 0)
    msg = jnp.zeros((width, width), F32)
    for k in range(nodes // 256):
        msg += jnp.dot(turned_ref[k], gp_ref[2 * k : 2 * k + 2].reshape(256, width), preferred_element_type=F32)
    msg_ref[...] = msg
    msg_sum[0]()
    upd_sum[1]()

    def features(i, _):
        at = pl.ds(pl.multiple_of(i * 512, 512), 512)
        spread = gp_ref[pl.ds(i * 4, 4)].reshape(512, width)
        below = lax.dot_general(spread, wm_ref[...], NT, preferred_element_type=F32)
        pre_ref[at] = (grad_ref[at].astype(F32) + below).astype(BF16)
        return 0

    lax.fori_loop(0, nodes // 512, features, 0)
    store_out = pltpu.make_async_copy(pre_ref, out_hbm, store_sem.at[1])
    store_out.start()
    msg_sum[1]()
    upd_sum[2]()
    msg_sum[2]()
    upd_sum[3]()
    msg_sum[3]()
    upd_sum[4]()
    store_out.wait()


def main_step(
    picks, slab, local, remote, weight, cols, w_update, w_message, grad, pre, feats, tiles, slabs, parts, cap, factor
):
    nodes, width = grad.shape
    count = picks.shape[-1]
    panels, early = nodes // 128, 5 * count
    vmem = pl.BlockSpec(memory_space=pltpu.VMEM)
    hbm = pl.BlockSpec(memory_space=pl.ANY)
    dma = pltpu.SemaphoreType.DMA
    square = jax.ShapeDtypeStruct((width, width), F32)
    return pl.pallas_call(
        functools.partial(main_kernel, parts, slabs, factor),
        out_shape=[jax.ShapeDtypeStruct((nodes, width), BF16), square, square],
        in_specs=[pl.BlockSpec(memory_space=pltpu.SMEM)] + [vmem] * 7 + [hbm] * 4,
        out_specs=[hbm, vmem, vmem],
        scratch_shapes=[
            pltpu.VMEM((cap, 128), F32),
            pltpu.VMEM((slabs, EXT, width), BF16),
            pltpu.VMEM((slabs, cap + EXT, width), BF16),
            pltpu.VMEM((slabs, cap + EXT, width), BF16),
            pltpu.VMEM((nodes, width), BF16),
            pltpu.VMEM((nodes, width), BF16),
            pltpu.VMEM((nodes, width), F32),
            pltpu.VMEM((nodes, width), F32),
            pltpu.VMEM((panels, 128, width), BF16),
            pltpu.VMEM((2, panels, SPLIT, width), BF16),
            pltpu.VMEM((panels, SPLIT, width), BF16),
            pltpu.VMEM((panels, 128 - SPLIT, width), BF16),
            pltpu.VMEM((4, count, SPLIT, width), BF16),
            pltpu.VMEM((6, count, 128 - SPLIT, width), BF16),
            pltpu.VMEM((early, 128, width), BF16),
            pltpu.VMEM((parts * count - early, 128, width), BF16),
            pltpu.VMEM((parts * count, 128, 128), BF16),
            pltpu.VMEM((parts * count, 128, width), BF16),
            pltpu.VMEM((nodes // 256, width, 256), BF16),
            pltpu.VMEM((8, parts * count), jnp.int32),
            pltpu.SMEM((8, parts * count), jnp.int32),
            pltpu.VMEM((width, width), F32),
            pltpu.VMEM((width, width), F32),
            dma((3,)), dma((parts,)), dma((slabs - 1,)), dma((slabs,)), dma((17,)), dma((17,)), dma((2,)),
        ]
        + sum_scratch(parts, slabs, width)
        + chip_scratch(parts, slabs),
        compiler_params=pltpu.CompilerParams(collective_id=0, has_side_effects=True, vmem_limit_bytes=VMEM_LIMIT),
        name="main_step",
    )(picks, slab, local, remote, weight, cols, w_update, w_message, grad, pre, feats, tiles)


def final_kernel(out_ref, msg_ref, upd_ref, to_out_ref, to_msg_ref, to_upd_ref, out_buf, msg_buf, upd_buf, come, go):
    steps = 4
    rows = out_ref.shape[0] // steps
    ways = [(msg_ref, msg_buf, to_msg_ref), (upd_ref, upd_buf, to_upd_ref)]
    for k in range(steps):
        at = pl.ds(k * rows, rows)
        ways.append((out_ref.at[at], out_buf.at[at], to_out_ref.at[at]))
    loads = [pltpu.make_async_copy(src, buf, come.at[k]) for k, (src, buf, _) in enumerate(ways)]
    stores = [pltpu.make_async_copy(buf, dst, go.at[k]) for k, (_, buf, dst) in enumerate(ways)]
    for load in loads:
        load.start()
    for load, store in zip(loads, stores):
        load.wait()
        store.start()
    for store in stores:
        store.wait()


def final_step(out, msg, upd):
    hbm = pl.BlockSpec(memory_space=pl.ANY)
    args = (out, msg, upd)
    return pl.pallas_call(
        final_kernel,
        out_shape=[jax.ShapeDtypeStruct(a.shape, a.dtype) for a in args],
        in_specs=[hbm] * 3,
        out_specs=[hbm] * 3,
        scratch_shapes=[pltpu.VMEM(a.shape, a.dtype) for a in args] + [pltpu.SemaphoreType.DMA((6,))] * 2,
        compiler_params=pltpu.CompilerParams(vmem_limit_bytes=VMEM_LIMIT),
        name="final_step",
    )(*args)


def local(
    grad_out, pre_act, node_feats, w_message, w_update, tile_vals, tile_rows, tile_cols,
    rec_slab, rec_local, rec_remote, rec_weight,
):
    grad = grad_out[0]
    rows, width = grad.shape
    slabs = lax.axis_size("grp")
    parts = lax.axis_size("blk")
    records = rec_local.shape[1]
    cap = 2 * records // slabs
    factor = float((slabs * parts * rows) ** -0.5)
    lanes = lambda a: a.reshape(records // 128, 128)
    tiles = tile_vals[0, 0]
    count = tiles.shape[0] * tiles.shape[1]
    out, msg, upd = main_step(
        tile_rows[0], lanes(rec_slab), lanes(rec_local), lanes(rec_remote), lanes(rec_weight),
        tile_cols[0, 0], w_update, w_message, grad, pre_act[0], node_feats[0],
        tiles.reshape(count, *tiles.shape[2:]), slabs, parts, cap, factor,
    )
    feats, msg, upd = final_step(out, msg, upd)
    return (feats[None], msg, upd)


def solution(mesh):
    placed = (
        P("grp", "blk", None),
        P("grp", "blk", None),
        P("grp", "blk", None),
        P(),
        P(),
        P("grp", "blk", None, None, None, None),
        P("grp", None, None, None),
        P("grp", "blk", None, None),
        P("grp", "blk", None),
        P("grp", "blk"),
        P("grp", "blk"),
        P("grp", "blk"),
    )
    return jax.shard_map(
        local,
        mesh=mesh,
        in_specs=placed,
        out_specs=(P("grp", "blk", None), P(), P()),
        check_vma=False,
    )
```
